32 devices in a mesh: groups: 2 (over y), dp: 4 (over x, core), prefix: 4 (over z).
Axes of the slice: x: 2, y: 2, z: 4, core: 2. Of those that a mesh axis runs over, the one named last changes fastest.
Arguments:
- queries: bfloat16 [16, 512, 4096], P(('groups', 'dp'), None, 'prefix'), parts along dimension 0, may hold values from -4.5 to 4.5
- resp_kv: bfloat16 [16, 512, 2048], P(('groups', 'dp'), None, 'prefix'), parts along dimension 0, may hold values from -4.5 to 4.5
- prompt_kv: bfloat16 [4, 1024, 2048], P('groups', 'dp', 'prefix'), parts along dimension 0, may hold values from -4.5 to 4.5
- prompt_of: int32 [16], P(('groups', 'dp')), parts along dimension 0, may hold values from 0 to 1, as said below
- d_out: bfloat16 [16, 512, 4096], P(('groups', 'dp'), None, 'prefix'), parts along dimension 0, may hold values from -6 to 6
Outputs:
- attended: bfloat16 [16, 512, 4096], P(('groups', 'dp'), None, 'prefix'), parts along dimension 0
- d_queries: bfloat16 [16, 512, 4096], P(('groups', 'dp'), None, 'prefix'), parts along dimension 0
- d_resp_kv: bfloat16 [16, 512, 2048], P(('groups', 'dp'), None, 'prefix'), parts along dimension 0
- d_prompt_kv: float32 [4, 1024, 2048], P('groups', 'dp', 'prefix'), parts along dimension 0
The draws below stay inside these ranges and needn't reach their ends.
There are 2 independent parts, one for each index of `groups`. The reference program is written for one: setup_inputs(seed, part) draws one part's arguments, and reference() takes and returns one part's arrays. A program takes and returns all parts, laid end to end along the dimension named above; each array names one. Nothing has to cross between parts.
Inputs may be any that keep to these rules, and one draw needn't show every extreme that they name: `prompt_of`: each prompt has at least 2 responses; responses of the two prompts may stand in any order.
All inputs are finite; a program needn't handle non-finite values.
Results may differ from the reference program's by a relative error of at most 0.011.
Values may be sent and summed in bfloat16 or wider, within the bound.
No kernel may reach another device: no remote copies, remote signals or barrier semaphores. Data moves between devices by JAX's collectives and lax.ppermute only.
A program may use at most 192 MiB of HBM per device.

```python
import jax
import jax.numpy as jnp
from jax import lax

H = 32
KVH = 8
HD = 128
P_SIZE = 2
LP = 1024
LR = 512
R = 8
N_PREFIX = 4


def draw_queries(key, part):
    key = jax.random.fold_in(key, 1)
    shape = (R, LR, H * HD)
    values = jnp.clip(jax.random.normal(key, shape, jnp.float32), -4.5, 4.5)
    return values.astype(jnp.bfloat16)


def draw_prompt_kv(key, part):
    key = jax.random.fold_in(key, 3)
    shape = (P_SIZE, LP, 2 * KVH * HD)
    values = jnp.clip(jax.random.normal(key, shape, jnp.float32), -4.5, 4.5)
    return values.astype(jnp.bfloat16)


def draw_prompt_of(key, part):
    key = jax.random.fold_in(key, 5)
    key = jax.random.fold_in(key, part)
    least = R // 4
    count_key, order_key = jax.random.split(key)
    boundary = jax.random.randint(count_key, (), least, R - least + 1)
    ranks = jax.random.permutation(order_key, R).astype(jnp.int32)
    labels = (ranks >= boundary).astype(jnp.int32)
    wanted = jnp.asarray(part, jnp.int32) % 2
    flipped = jnp.where(labels[0] == wanted, labels, 1 - labels)
    return flipped.astype(jnp.int32)


def steps_of(rng, dims, shards, low, high):
    level = 1.0
    for dim, blocks in shards:
        draws = jax.random.uniform(jax.random.fold_in(jax.random.fold_in(rng, 6), dim), (blocks,), jnp.float32, low / len(shards), high / len(shards))
        level = level * jnp.repeat(jnp.exp(draws), dims[dim] // blocks).reshape((-1,) + (1,) * (len(dims) - 1 - dim))
    return level


def normal_values(key, extent, spread, reach, cuts=(), kind=jnp.bfloat16):
    drawn = jax.random.normal(key, extent, jnp.float32) * spread
    if len(cuts) > 0:
        drawn = steps_of(key, extent, cuts, -0.22, 0.18) * drawn
    return jnp.clip(drawn, min=-reach, max=reach).astype(kind)


def setup_inputs(seed: int = 0, part: int = 0) -> dict:
    splits = jax.random.split(jax.random.key(seed), 6)
    own_keys = jax.random.split(jax.random.fold_in(splits[5], part), 6)
    queries = draw_queries(jax.random.fold_in(jax.random.fold_in(splits[5], part), 71), part)
    resp_kv = normal_values(own_keys[1], (R, LR, 2 * KVH * HD), 1.0, 4.5, ((0, 4), (2, 4)))
    prompt_kv = draw_prompt_kv(jax.random.fold_in(jax.random.fold_in(splits[5], part), 71), part)
    prompt_of = draw_prompt_of(jax.random.fold_in(jax.random.fold_in(splits[5], part), 71), part)
    d_out = normal_values(own_keys[4], (R, LR, H * HD), 1.0, 6.0, ((0, 4), (2, 4)))
    return {"queries": queries, "resp_kv": resp_kv, "prompt_kv": prompt_kv, "prompt_of": prompt_of, "d_out": d_out}


masked_value = -1.0e30


def attend_head(query_rows, key_rows, value_rows, grad_rows, scaling):
    row_count = query_rows.shape[0]
    key_count = key_rows.shape[0]
    offset = key_count - row_count
    scores = jnp.dot(query_rows, key_rows.T, preferred_element_type=jnp.float32) * scaling
    query_pos = lax.broadcasted_iota(jnp.int32, (row_count, key_count), 0) + offset
    key_pos = lax.broadcasted_iota(jnp.int32, (row_count, key_count), 1)
    scores = jnp.where(key_pos <= query_pos, scores, masked_value)
    row_max = jnp.max(scores, axis=1, keepdims=True)
    weights = jnp.exp(scores - row_max)
    attention = weights / jnp.sum(weights, axis=1, keepdims=True)
    attn_bf16 = attention.astype(jnp.bfloat16)
    result = jnp.dot(attn_bf16, value_rows, preferred_element_type=jnp.float32)
    delta_row = jnp.sum(result * grad_rows.astype(jnp.float32), axis=1, keepdims=True)
    grad_attn = jnp.dot(grad_rows, value_rows.T, preferred_element_type=jnp.float32)
    grad_score = (attention * (grad_attn - delta_row) * scaling).astype(jnp.bfloat16)
    grad_query = jnp.dot(grad_score, key_rows, preferred_element_type=jnp.float32)
    grad_key = jnp.dot(grad_score.T, query_rows, preferred_element_type=jnp.float32)
    grad_value = jnp.dot(attn_bf16.T, grad_rows, preferred_element_type=jnp.float32)
    return result, grad_query, grad_key, grad_value


def split_heads(matrix, half_index):
    length = matrix.shape[0]
    blocks = matrix.reshape(length, N_PREFIX // 2, 2, 2 * KVH // N_PREFIX, HD)
    return blocks[:, :, half_index].reshape(length, KVH, HD)


def reference(queries, resp_kv, prompt_kv, prompt_of, d_out):
    scaling = HD ** -0.5
    group_size = H // KVH
    key_count = LP + LR

    def one_response(summed, pieces):
        query_rows, own_kv, grad_rows, prompt_id = pieces
        prompt_rows = lax.dynamic_index_in_dim(prompt_kv, prompt_id.astype(jnp.int32), 0, keepdims=False)
        joined = jnp.concatenate([prompt_rows, own_kv], axis=0)
        key_heads = jnp.repeat(split_heads(joined, 0), group_size, axis=1).transpose(1, 0, 2)
        value_heads = jnp.repeat(split_heads(joined, 1), group_size, axis=1).transpose(1, 0, 2)
        query_heads = query_rows.reshape(LR, H, HD).transpose(1, 0, 2)
        grad_heads = grad_rows.reshape(LR, H, HD).transpose(1, 0, 2)

        def per_head(members):
            return attend_head(members[0], members[1], members[2], members[3], scaling)

        outputs, grad_q, grad_k, grad_v = lax.map(per_head, (query_heads, key_heads, value_heads, grad_heads))
        key_grads = grad_k.reshape(KVH, group_size, key_count, HD).sum(axis=1)
        value_grads = grad_v.reshape(KVH, group_size, key_count, HD).sum(axis=1)
        kv_grads = jnp.stack([key_grads, value_grads], axis=0)
        kv_grads = kv_grads.reshape(2, N_PREFIX // 2, 2 * KVH // N_PREFIX, key_count, HD)
        kv_grads = kv_grads.transpose(3, 1, 0, 2, 4).reshape(key_count, 2 * KVH * HD)
        one_hot = (jnp.arange(P_SIZE, dtype=jnp.int32) == prompt_id.astype(jnp.int32)).astype(jnp.float32)
        summed = summed + one_hot[:, None, None] * kv_grads[None, :LP]
        attended = outputs.transpose(1, 0, 2).reshape(LR, H * HD).astype(jnp.bfloat16)
        query_grad = grad_q.transpose(1, 0, 2).reshape(LR, H * HD).astype(jnp.bfloat16)
        return summed, (attended, query_grad, kv_grads[LP:].astype(jnp.bfloat16))

    zero_sum = jnp.zeros((P_SIZE, LP, 2 * KVH * HD), jnp.float32)
    d_prompt, (attended, d_queries, d_resp) = lax.scan(one_response, zero_sum, (queries, resp_kv, d_out, prompt_of))
    return attended, d_queries, d_resp, d_prompt
```

```python
import functools

import jax
import jax.numpy as jnp
from jax import lax
from jax.experimental import pallas as pl
from jax.experimental.pallas import tpu as pltpu
from jax.sharding import PartitionSpec as P

H = 32
KVH = 8
HD = 128
P_SIZE = 2
GROUP = H // KVH
BLOCK = 256
MASKED = -1e30
SCALE = HD ** (-0.5)
LOG2E = 1.4426950408889634

NT = (((1,), (1,)), ((), ()))
NN = (((1,), (0,)), ((), ()))
TN = (((0,), (0,)), ((), ()))


def dot(a, b, dims):
    return lax.dot_general(a, b, dims, preferred_element_type=jnp.float32)


def swap(block, axis, bit):
    count = lax.axis_size(axis)
    route = [(i, i ^ (1 << bit)) for i in range(count)]
    return lax.ppermute(block, axis, route)


def attend_kernel(sizes, scalars, *refs):
    pieces, rows, n_keep, heads = sizes
    refs = list(refs)
    q_ref, do_ref, ra_ref, rb_ref = refs[:4]
    pa_refs = refs[4 : 4 + pieces]
    pb_refs = refs[4 + pieces : 4 + 2 * pieces]
    rest = refs[4 + 2 * pieces :]
    n_out = 5 + (1 if pieces > n_keep else 0)
    out_ref, dq_ref, dra_ref, drb_ref, dkeep_ref = rest[:5]
    dsend_ref = rest[5] if n_out == 6 else None
    k_all, v_all, probs, dscores, acc_k, acc_v, res_k, res_v = rest[n_out:]

    r = pl.program_id(0)
    head = pl.program_id(1)
    prompt = scalars[r]
    even = scalars[pl.num_programs(0)] == 0
    n_prompt = pieces * rows
    n_query = q_ref.shape[1]

    @pl.when((r == 0) & (head == 0))
    def _():
        acc_k[...] = jnp.zeros_like(acc_k)
        acc_v[...] = jnp.zeros_like(acc_v)

    def gather(dst, piece_refs, resp_ref):
        for i, ref in enumerate(piece_refs):
            dst[i * rows : (i + 1) * rows, :] = ref[0]
        dst[n_prompt:, :] = resp_ref[0]

    @pl.when((head == 0) & even)
    def _():
        gather(k_all, pa_refs, ra_ref)
        gather(v_all, pb_refs, rb_ref)

    @pl.when((head == 0) & jnp.logical_not(even))
    def _():
        gather(k_all, pb_refs, rb_ref)
        gather(v_all, pa_refs, ra_ref)

    @pl.when(head == 0)
    def _():
        res_k[...] = jnp.zeros_like(res_k)
        res_v[...] = jnp.zeros_like(res_v)

    n_blocks = n_query // BLOCK
    for i in range(n_blocks):
        t0 = i * BLOCK
        seen = n_prompt + t0 + BLOCK
        q = q_ref[0, t0 : t0 + BLOCK, :]
        do = do_ref[0, t0 : t0 + BLOCK, :]
        keys = k_all[:seen, :]
        values = v_all[:seen, :]
        s = dot(q, keys, NT)
        diag = s[:, seen - BLOCK :]
        row = lax.broadcasted_iota(jnp.int32, (BLOCK, BLOCK), 0)
        col = lax.broadcasted_iota(jnp.int32, (BLOCK, BLOCK), 1)
        diag = jnp.where(col <= row, diag, MASKED)
        s = jnp.concatenate([s[:, : seen - BLOCK], diag], axis=1)
        top = jnp.max(s, axis=1, keepdims=True)
        w = jnp.exp2(s * (SCALE * LOG2E) - top * (SCALE * LOG2E))
        p = w * (1.0 / jnp.sum(w, axis=1, keepdims=True))
        p16 = p.astype(jnp.bfloat16)
        probs[t0 : t0 + BLOCK, :seen] = p16
        o = dot(p16, values, NN)
        out_ref[0, t0 : t0 + BLOCK, :] = o.astype(jnp.bfloat16)
        delta = jnp.sum(o * do.astype(jnp.float32), axis=1, keepdims=True)
        dp = dot(do, values, NT)
        ds = (p * (dp - delta)).astype(jnp.bfloat16)
        dscores[t0 : t0 + BLOCK, :seen] = ds
        dq_ref[0, t0 : t0 + BLOCK, :] = (dot(ds, keys, NN) * SCALE).astype(jnp.bfloat16)

    q_all = q_ref[0]
    do_all = do_ref[0]
    acc_k[prompt] += dot(dscores[:, :n_prompt], q_all, TN)
    acc_v[prompt] += dot(probs[:, :n_prompt], do_all, TN)
    for i in range(n_blocks):
        t0 = i * BLOCK
        u0 = n_prompt + t0
        res_k[t0 : t0 + BLOCK, :] += dot(dscores[t0:, u0 : u0 + BLOCK], q_all[t0:], TN)
        res_v[t0 : t0 + BLOCK, :] += dot(probs[t0:, u0 : u0 + BLOCK], do_all[t0:], TN)

    last = head == heads - 1

    @pl.when(last & even)
    def _():
        dra_ref[0] = (res_k[...] * SCALE).astype(jnp.bfloat16)
        drb_ref[0] = res_v[...].astype(jnp.bfloat16)

    @pl.when(last & jnp.logical_not(even))
    def _():
        dra_ref[0] = res_v[...].astype(jnp.bfloat16)
        drb_ref[0] = (res_k[...] * SCALE).astype(jnp.bfloat16)

    done = last & (r == pl.num_programs(0) - 1)

    def scatter(slot, acc, factor):
        for i in range(pieces):
            for p_id in range(P_SIZE):
                val = acc[p_id, i * rows : (i + 1) * rows, :]
                if factor != 1.0:
                    val = val * factor
                if i < n_keep:
                    dkeep_ref[i, p_id, :, slot * HD : (slot + 1) * HD] = val
                else:
                    dsend_ref[i - n_keep, p_id, :, slot * HD : (slot + 1) * HD] = val.astype(jnp.bfloat16)

    @pl.when(done & even)
    def _():
        scatter(0, acc_k, SCALE)
        scatter(1, acc_v, 1.0)

    @pl.when(done & jnp.logical_not(even))
    def _():
        scatter(0, acc_v, 1.0)
        scatter(1, acc_k, SCALE)


def attend(scalars, queries, d_out, resp_a, resp_b, prompt_a, prompt_b, n_keep, chunk, heads):
    n_resp, n_query, _ = queries.shape
    pieces = len(prompt_a)
    rows = prompt_a[0][0].shape[1]
    n_prompt = pieces * rows
    n_keys = n_prompt + n_query
    n_send = pieces - n_keep

    def query_map(r, j, sc):
        return (r, 0, chunk * heads + j)

    def resp_map(column):
        return lambda r, j, sc: (r, 0, column(sc[n_resp]))

    def prompt_map(column):
        return lambda r, j, sc: (sc[r], 0, column(sc[n_resp]))

    q_spec = pl.BlockSpec((1, n_query, HD), query_map)
    in_specs = [q_spec, q_spec]
    in_specs += [pl.BlockSpec((1, n_query, HD), resp_map(c)) for _, c in (resp_a, resp_b)]
    in_specs += [pl.BlockSpec((1, rows, HD), prompt_map(c)) for _, c in (*prompt_a, *prompt_b)]
    own_map = lambda r, j, sc: (r, 0, j)
    out_specs = [
        pl.BlockSpec((1, n_query, HD), own_map),
        pl.BlockSpec((1, n_query, HD), own_map),
        pl.BlockSpec((1, n_query, HD), lambda r, j, sc: (r, 0, 0)),
        pl.BlockSpec((1, n_query, HD), lambda r, j, sc: (r, 0, 0)),
        pl.BlockSpec((n_keep, P_SIZE, rows, 2 * HD), lambda r, j, sc: (0, 0, 0, 0)),
    ]
    shape = jax.ShapeDtypeStruct
    out_shape = [
        shape((n_resp, n_query, heads * HD), jnp.bfloat16),
        shape((n_resp, n_query, heads * HD), jnp.bfloat16),
        shape((n_resp, n_query, HD), jnp.bfloat16),
        shape((n_resp, n_query, HD), jnp.bfloat16),
        shape((n_keep, P_SIZE, rows, 2 * HD), jnp.float32),
    ]
    if n_send:
        out_specs.append(pl.BlockSpec((n_send, P_SIZE, rows, 2 * HD), lambda r, j, sc: (0, 0, 0, 0)))
        out_shape.append(shape((n_send, P_SIZE, rows, 2 * HD), jnp.bfloat16))
    scratch = [
        pltpu.VMEM((n_keys, HD), jnp.bfloat16),
        pltpu.VMEM((n_keys, HD), jnp.bfloat16),
        pltpu.VMEM((n_query, n_keys), jnp.bfloat16),
        pltpu.VMEM((n_query, n_keys), jnp.bfloat16),
        pltpu.VMEM((P_SIZE, n_prompt, HD), jnp.float32),
        pltpu.VMEM((P_SIZE, n_prompt, HD), jnp.float32),
        pltpu.VMEM((n_query, HD), jnp.float32),
        pltpu.VMEM((n_query, HD), jnp.float32),
    ]
    flops = 12 * n_resp * heads * n_query * n_keys * HD
    return pl.pallas_call(
        functools.partial(attend_kernel, (pieces, rows, n_keep, heads)),
        grid_spec=pltpu.PrefetchScalarGridSpec(
            num_scalar_prefetch=1,
            grid=(n_resp, heads),
            in_specs=in_specs,
            out_specs=out_specs,
            scratch_shapes=scratch,
        ),
        out_shape=out_shape,
        compiler_params=pltpu.CompilerParams(vmem_limit_bytes=48 * 2**20),
        cost_estimate=pl.CostEstimate(flops=2 * flops, bytes_accessed=8 * 2**20, transcendentals=0),
    )(scalars, queries, d_out, resp_a[0], resp_b[0], *[a for a, _ in (*prompt_a, *prompt_b)])


def per_device(queries, resp_kv, prompt_kv, prompt_of, d_out):
    n_resp, n_query, width = queries.shape
    pair_heads = prompt_kv.shape[2] // HD
    parity = lax.axis_index("prefix") % 2
    scalars = jnp.concatenate([prompt_of, parity[None].astype(jnp.int32)])
    if lax.axis_size("dp") == 4 and pair_heads % 2 == 0:
        return whole_heads(queries, resp_kv, prompt_kv, scalars, parity, d_out)
    return shared_head(queries, resp_kv, prompt_kv, scalars, parity, d_out)


def whole_heads(queries, resp_kv, prompt_kv, scalars, parity, d_out):
    n_own = prompt_kv.shape[2] // HD // 2

    def column(array, which):
        return lax.dynamic_slice_in_dim(array, which * HD, HD, axis=array.ndim - 1)

    attended, d_queries, d_resp, d_prompt = [], [], [], []
    for h in range(n_own):
        own = lambda par, h=h: par * n_own + h
        theirs = (1 - parity) * n_own + h
        first = lambda par: 0
        pa0 = column(prompt_kv, own(parity))
        pb0 = swap(column(prompt_kv, theirs), "prefix", 0)
        rb = swap(column(resp_kv, theirs), "prefix", 0)
        pa2 = swap(pa0, "dp", 1)
        pb2 = swap(pb0, "dp", 1)
        pa1 = swap(pa0, "dp", 0)
        pb1 = swap(pb0, "dp", 0)
        pa3 = swap(pa2, "dp", 0)
        pb3 = swap(pb2, "dp", 0)
        att, dq, dra, drb, dkeep, dsend = attend(
            scalars,
            queries,
            d_out,
            (resp_kv, own),
            (rb, first),
            [(prompt_kv, own), (pa2, first), (pa1, first), (pa3, first)],
            [(pb0, first), (pb2, first), (pb1, first), (pb3, first)],
            2,
            h,
            GROUP,
        )
        attended.append(att)
        d_queries.append(dq)
        d_resp.append((dra, swap(drb, "prefix", 0)))
        part = swap(dsend, "dp", 0)
        sums = dkeep + part.astype(jnp.float32)
        across = swap(sums[1].astype(jnp.bfloat16), "dp", 1)
        total = sums[0] + across.astype(jnp.float32)
        mine = total[:, :, :HD]
        other = swap(total[:, :, HD:].astype(jnp.bfloat16), "prefix", 0)
        d_prompt.append((mine, other.astype(jnp.float32)))

    def place(parts):
        mine = jnp.concatenate([a for a, _ in parts], axis=-1)
        other = jnp.concatenate([b for _, b in parts], axis=-1)
        even = parity == 0
        return jnp.concatenate([jnp.where(even, mine, other), jnp.where(even, other, mine)], axis=-1)

    return (
        jnp.concatenate(attended, axis=-1),
        jnp.concatenate(d_queries, axis=-1),
        place(d_resp),
        place(d_prompt),
    )


def shared_head(queries, resp_kv, prompt_kv, scalars, parity, d_out):
    pair_heads = prompt_kv.shape[2] // HD
    local_heads = queries.shape[2] // HD
    prompt_a = lax.all_gather(prompt_kv, "dp", axis=1, tiled=True)
    prompt_b = swap(prompt_a, "prefix", 0)
    resp_b = swap(resp_kv, "prefix", 0)
    first = lambda par: 0
    att, dq, dra, drb, dkeep = attend(
        scalars,
        queries,
        d_out,
        (resp_kv, first),
        (resp_b, first),
        [(prompt_a, first)],
        [(prompt_b, first)],
        1,
        0,
        local_heads,
    )
    d_resp = (dra.astype(jnp.float32) + swap(drb, "prefix", 0).astype(jnp.float32)).astype(jnp.bfloat16)
    other = swap(dkeep[0, :, :, HD:].astype(jnp.bfloat16), "prefix", 0)
    paired = dkeep[0, :, :, :HD] + other.astype(jnp.float32)
    d_prompt = lax.psum_scatter(paired, "dp", scatter_dimension=1, tiled=True)
    return att, dq, d_resp, d_prompt


def solution(mesh):
    in_specs = (
        P(("groups", "dp"), None, "prefix"),
        P(("groups", "dp"), None, "prefix"),
        P("groups", "dp", "prefix"),
        P(("groups", "dp")),
        P(("groups", "dp"), None, "prefix"),
    )
    out_specs = (
        P(("groups", "dp"), None, "prefix"),
        P(("groups", "dp"), None, "prefix"),
        P(("groups", "dp"), None, "prefix"),
        P("groups", "dp", "prefix"),
    )
    return jax.shard_map(
        per_device, mesh=mesh, in_specs=in_specs, out_specs=out_specs, check_vma=False
    )
```

```python
import functools

import jax
import jax.numpy as jnp
from jax import lax
from jax.experimental import pallas as pl
from jax.experimental.pallas import tpu as pltpu
from jax.sharding import PartitionSpec as P

H = 32
KVH = 8
HD = 128
P_SIZE = 2
GROUP = H // KVH
BLOCK = 256
MASKED = -1e30
SCALE = HD ** (-0.5)
LOG2E = 1.4426950408889634

NT = (((1,), (1,)), ((), ()))
NN = (((1,), (0,)), ((), ()))
TN = (((0,), (0,)), ((), ()))


def dot(a, b, dims):
    return lax.dot_general(a, b, dims, preferred_element_type=jnp.float32)


def swap(block, axis, bit):
    count = lax.axis_size(axis)
    route = [(i, i ^ (1 << bit)) for i in range(count)]
    return lax.ppermute(block, axis, route)


def attend_kernel(sizes, scalars, *refs):
    pieces, rows, n_keep, heads, aliased = sizes
    refs = list(refs)
    q_ref, do_ref, ra_ref, rb_ref = refs[:4]
    pa_refs = refs[4 : 4 + pieces]
    pb_refs = refs[4 + pieces : 4 + 2 * pieces]
    rest = refs[4 + 2 * pieces + (2 if aliased else 0) :]
    n_out = 5 + (1 if pieces > n_keep else 0)
    out_ref, dq_ref, dra_ref, drb_ref, dkeep_ref = rest[:5]
    dsend_ref = rest[5] if n_out == 6 else None
    k_all, v_all, k_t, v_t, weights, probs, dscores, acc_k, acc_v, res_k, res_v = rest[n_out:]

    r = pl.program_id(0)
    head = pl.program_id(1)
    prompt = scalars[r]
    even = scalars[pl.num_programs(0)] == 0
    n_prompt = pieces * rows
    n_query = q_ref.shape[1]

    @pl.when((r == 0) & (head == 0))
    def _():
        acc_k[...] = jnp.zeros_like(acc_k)
        acc_v[...] = jnp.zeros_like(acc_v)

    def gather(dst, piece_refs, resp_ref):
        for i, ref in enumerate(piece_refs):
            dst[i * rows : (i + 1) * rows, :] = ref[0]
        dst[n_prompt:, :] = resp_ref[0]

    @pl.when((head == 0) & even)
    def _():
        gather(k_all, pa_refs, ra_ref)
        gather(v_all, pb_refs, rb_ref)

    @pl.when((head == 0) & jnp.logical_not(even))
    def _():
        gather(k_all, pb_refs, rb_ref)
        gather(v_all, pa_refs, ra_ref)

    @pl.when(head == 0)
    def _():
        res_k[...] = jnp.zeros_like(res_k)
        res_v[...] = jnp.zeros_like(res_v)
        k_t[...] = k_all[...].T
        v_t[...] = v_all[...].T

    n_blocks = n_query // BLOCK
    state = [dict() for _ in range(n_blocks)]

    def span(c):
        return slice(c * BLOCK, (c + 1) * BLOCK)

    def fold(x, op):
        return op(x.reshape(-1, 8, x.shape[-1]), axis=0)

    def stages(i):
        st = state[i]
        t = span(i)
        n_chunks = n_prompt // BLOCK + i + 1
        seen = n_chunks * BLOCK
        q = q_ref[0, t, :]
        do = do_ref[0, t, :]

        def score(c):
            s = dot(k_all[span(c), :], q, NT)
            if c == n_chunks - 1:
                row = lax.broadcasted_iota(jnp.int32, (BLOCK, BLOCK), 0)
                col = lax.broadcasted_iota(jnp.int32, (BLOCK, BLOCK), 1)
                s = jnp.where(row <= col, s, MASKED)
            weights[span(c), t] = s
            top = fold(s, jnp.max)
            st["top"] = top if c == 0 else jnp.maximum(st["top"], top)
            if c == n_chunks - 1:
                st["top"] = jnp.max(st["top"], axis=0, keepdims=True) * (SCALE * LOG2E)

        def weigh(c):
            w = jnp.exp2(weights[span(c), t] * (SCALE * LOG2E) - st["top"])
            weights[span(c), t] = w
            total = fold(w, jnp.sum)
            st["sum"] = total if c == 0 else st["sum"] + total
            if c == n_chunks - 1:
                st["inv"] = 1.0 / jnp.sum(st["sum"], axis=0, keepdims=True)

        def norm(c):
            probs[span(c), t] = (weights[span(c), t] * st["inv"]).astype(jnp.bfloat16)
            if c == n_chunks - 1:
                o = dot(v_t[:, :seen], probs[:seen, t], NN)
                out_ref[0, t, :] = o.T.astype(jnp.bfloat16)
                do_t = do.astype(jnp.float32).T
                st["delta"] = jnp.sum(o * do_t, axis=0, keepdims=True)
                st["inv"] = st["inv"] * SCALE

        def grad(c):
            dp = dot(v_all[span(c), :], do, NT)
            ds = (weights[span(c), t] * st["inv"]) * (dp - st["delta"])
            dscores[span(c), t] = ds.astype(jnp.bfloat16)
            if c == n_chunks - 1:
                dq = dot(k_t[:, :seen], dscores[:seen, t], NN)
                dq_ref[0, t, :] = dq.T.astype(jnp.bfloat16)

        return [[functools.partial(f, c) for c in range(n_chunks)] for f in (score, weigh, norm, grad)]

    plan = [stages(i) for i in range(n_blocks)]
    for slot in range(4 + n_blocks - 1):
        groups = [plan[i][slot - i] for i in reversed(range(n_blocks)) if 0 <= slot - i < 4]
        for c in range(max(len(g) for g in groups)):
            for g in groups:
                if c < len(g):
                    g[c]()

    q_all = q_ref[0]
    do_all = do_ref[0]
    for c in range(n_prompt // BLOCK):
        acc_v[prompt, span(c), :] += dot(probs[span(c), :], do_all, NN)
        acc_k[prompt, span(c), :] += dot(dscores[span(c), :], q_all, NN)
    for i in range(n_blocks):
        u = span(n_prompt // BLOCK + i)
        t0 = i * BLOCK
        res_v[span(i), :] += dot(probs[u, t0:], do_all[t0:], NN)
        res_k[span(i), :] += dot(dscores[u, t0:], q_all[t0:], NN)

    last = head == heads - 1

    @pl.when(last & even)
    def _():
        dra_ref[0] = res_k[...].astype(jnp.bfloat16)
        drb_ref[0] = res_v[...].astype(jnp.bfloat16)

    @pl.when(last & jnp.logical_not(even))
    def _():
        dra_ref[0] = res_v[...].astype(jnp.bfloat16)
        drb_ref[0] = res_k[...].astype(jnp.bfloat16)

    done = last & (r == pl.num_programs(0) - 1)

    def scatter(slot, acc):
        for i in range(pieces):
            for p_id in range(P_SIZE):
                val = acc[p_id, i * rows : (i + 1) * rows, :]
                if i < n_keep:
                    dkeep_ref[i, p_id, :, slot * HD : (slot + 1) * HD] = val
                else:
                    dsend_ref[i - n_keep, p_id, :, slot * HD : (slot + 1) * HD] = val.astype(jnp.bfloat16)

    @pl.when(done & even)
    def _():
        scatter(0, acc_k)
        scatter(1, acc_v)

    @pl.when(done & jnp.logical_not(even))
    def _():
        scatter(0, acc_v)
        scatter(1, acc_k)


def attend(scalars, queries, d_out, resp_a, resp_b, prompt_a, prompt_b, n_keep, chunk, heads, before=None):
    n_resp, n_query, _ = queries.shape
    pieces = len(prompt_a)
    rows = prompt_a[0][0].shape[1]
    n_prompt = pieces * rows
    n_keys = n_prompt + n_query
    n_send = pieces - n_keep

    def query_map(r, j, sc):
        return (r, 0, chunk * heads + j)

    def resp_map(column):
        return lambda r, j, sc: (r, 0, column(sc[n_resp]))

    def prompt_map(column):
        return lambda r, j, sc: (sc[r], 0, column(sc[n_resp]))

    q_spec = pl.BlockSpec((1, n_query, HD), query_map)
    in_specs = [q_spec, q_spec]
    in_specs += [pl.BlockSpec((1, n_query, HD), resp_map(c)) for _, c in (resp_a, resp_b)]
    in_specs += [pl.BlockSpec((1, rows, HD), prompt_map(c)) for _, c in (*prompt_a, *prompt_b)]
    if before is not None:
        in_specs += [pl.BlockSpec(memory_space=pl.ANY)] * 2
    out_specs = [
        q_spec,
        q_spec,
        pl.BlockSpec((1, n_query, HD), lambda r, j, sc: (r, 0, 0)),
        pl.BlockSpec((1, n_query, HD), lambda r, j, sc: (r, 0, 0)),
        pl.BlockSpec((n_keep, P_SIZE, rows, 2 * HD), lambda r, j, sc: (0, 0, 0, 0)),
    ]
    shape = jax.ShapeDtypeStruct
    out_shape = [
        shape(queries.shape, jnp.bfloat16),
        shape(queries.shape, jnp.bfloat16),
        shape((n_resp, n_query, HD), jnp.bfloat16),
        shape((n_resp, n_query, HD), jnp.bfloat16),
        shape((n_keep, P_SIZE, rows, 2 * HD), jnp.float32),
    ]
    if n_send:
        out_specs.append(pl.BlockSpec((n_send, P_SIZE, rows, 2 * HD), lambda r, j, sc: (0, 0, 0, 0)))
        out_shape.append(shape((n_send, P_SIZE, rows, 2 * HD), jnp.bfloat16))
    scratch = [
        pltpu.VMEM((n_keys, HD), jnp.bfloat16),
        pltpu.VMEM((n_keys, HD), jnp.bfloat16),
        pltpu.VMEM((HD, n_keys), jnp.bfloat16),
        pltpu.VMEM((HD, n_keys), jnp.bfloat16),
        pltpu.VMEM((n_keys, n_query), jnp.float32),
        pltpu.VMEM((n_keys, n_query), jnp.bfloat16),
        pltpu.VMEM((n_keys, n_query), jnp.bfloat16),
        pltpu.VMEM((P_SIZE, n_prompt, HD), jnp.float32),
        pltpu.VMEM((P_SIZE, n_prompt, HD), jnp.float32),
        pltpu.VMEM((n_query, HD), jnp.float32),
        pltpu.VMEM((n_query, HD), jnp.float32),
    ]
    extra = () if before is None else before
    n_in = 5 + 2 * pieces
    aliases = {} if before is None else {n_in: 0, n_in + 1: 1}
    flops = 12 * n_resp * heads * n_query * n_keys * HD
    return pl.pallas_call(
        functools.partial(attend_kernel, (pieces, rows, n_keep, heads, before is not None)),
        grid_spec=pltpu.PrefetchScalarGridSpec(
            num_scalar_prefetch=1,
            grid=(n_resp, heads),
            in_specs=in_specs,
            out_specs=out_specs,
            scratch_shapes=scratch,
        ),
        out_shape=out_shape,
        input_output_aliases=aliases,
        compiler_params=pltpu.CompilerParams(vmem_limit_bytes=48 * 2**20),
        cost_estimate=pl.CostEstimate(flops=2 * flops, bytes_accessed=8 * 2**20, transcendentals=0),
    )(scalars, queries, d_out, resp_a[0], resp_b[0], *[a for a, _ in (*prompt_a, *prompt_b)], *extra)


def per_device(queries, resp_kv, prompt_kv, prompt_of, d_out):
    n_resp, n_query, width = queries.shape
    pair_heads = prompt_kv.shape[2] // HD
    parity = lax.axis_index("prefix") % 2
    scalars = jnp.concatenate([prompt_of, parity[None].astype(jnp.int32)])
    if lax.axis_size("dp") == 4 and pair_heads % 2 == 0:
        return whole_heads(queries, resp_kv, prompt_kv, scalars, parity, d_out)
    return shared_head(queries, resp_kv, prompt_kv, scalars, parity, d_out)


def whole_heads(queries, resp_kv, prompt_kv, scalars, parity, d_out):
    n_own = prompt_kv.shape[2] // HD // 2

    def column(array, which):
        return lax.dynamic_slice_in_dim(array, which * HD, HD, axis=array.ndim - 1)

    d_resp, d_prompt, before = [], [], None
    for h in range(n_own):
        own = lambda par, h=h: par * n_own + h
        theirs = (1 - parity) * n_own + h
        first = lambda par: 0
        pa0 = column(prompt_kv, own(parity))
        pb0 = swap(column(prompt_kv, theirs), "prefix", 0)
        rb = swap(column(resp_kv, theirs), "prefix", 0)
        pa2 = swap(pa0, "dp", 1)
        pb2 = swap(pb0, "dp", 1)
        pa1 = swap(pa0, "dp", 0)
        pb1 = swap(pb0, "dp", 0)
        pa3 = swap(pa2, "dp", 0)
        pb3 = swap(pb2, "dp", 0)
        att, dq, dra, drb, dkeep, dsend = attend(
            scalars,
            queries,
            d_out,
            (resp_kv, own),
            (rb, first),
            [(prompt_kv, own), (pa2, first), (pa1, first), (pa3, first)],
            [(pb0, first), (pb2, first), (pb1, first), (pb3, first)],
            2,
            h,
            GROUP,
            before,
        )
        before = (att, dq)
        d_resp.append((dra, swap(drb, "prefix", 0)))
        part = swap(dsend, "dp", 0)
        sums = dkeep + part.astype(jnp.float32)
        across = swap(sums[1].astype(jnp.bfloat16), "dp", 1)
        total = sums[0] + across.astype(jnp.float32)
        mine = total[:, :, :HD]
        other = swap(total[:, :, HD:].astype(jnp.bfloat16), "prefix", 0)
        d_prompt.append((mine, other.astype(jnp.float32)))

    def place(parts):
        mine = jnp.concatenate([a for a, _ in parts], axis=-1)
        other = jnp.concatenate([b for _, b in parts], axis=-1)
        even = parity == 0
        return jnp.concatenate([jnp.where(even, mine, other), jnp.where(even, other, mine)], axis=-1)

    return (
        *before,
        place(d_resp),
        place(d_prompt),
    )


def shared_head(queries, resp_kv, prompt_kv, scalars, parity, d_out):
    pair_heads = prompt_kv.shape[2] // HD
    local_heads = queries.shape[2] // HD
    prompt_a = lax.all_gather(prompt_kv, "dp", axis=1, tiled=True)
    prompt_b = swap(prompt_a, "prefix", 0)
    resp_b = swap(resp_kv, "prefix", 0)
    first = lambda par: 0
    att, dq, dra, drb, dkeep = attend(
        scalars,
        queries,
        d_out,
        (resp_kv, first),
        (resp_b, first),
        [(prompt_a, first)],
        [(prompt_b, first)],
        1,
        0,
        local_heads,
    )
    d_resp = (dra.astype(jnp.float32) + swap(drb, "prefix", 0).astype(jnp.float32)).astype(jnp.bfloat16)
    other = swap(dkeep[0, :, :, HD:].astype(jnp.bfloat16), "prefix", 0)
    paired = dkeep[0, :, :, :HD] + other.astype(jnp.float32)
    d_prompt = lax.psum_scatter(paired, "dp", scatter_dimension=1, tiled=True)
    return att, dq, d_resp, d_prompt


def solution(mesh):
    in_specs = (
        P(("groups", "dp"), None, "prefix"),
        P(("groups", "dp"), None, "prefix"),
        P("groups", "dp", "prefix"),
        P(("groups", "dp")),
        P(("groups", "dp"), None, "prefix"),
    )
    out_specs = (
        P(("groups", "dp"), None, "prefix"),
        P(("groups", "dp"), None, "prefix"),
        P(("groups", "dp"), None, "prefix"),
        P("groups", "dp", "prefix"),
    )
    return jax.shard_map(
        per_device, mesh=mesh, in_specs=in_specs, out_specs=out_specs, check_vma=False
    )
```

```python
import functools

import jax
import jax.numpy as jnp
from jax import lax
from jax.experimental import pallas as pl
from jax.experimental.pallas import tpu as pltpu
from jax.sharding import PartitionSpec as P

H = 32
KVH = 8
HD = 128
P_SIZE = 2
GROUP = H // KVH
BLOCK = 256
MASKED = -1e30
SCALE = HD ** (-0.5)

NT = (((1,), (1,)), ((), ()))
NN = (((1,), (0,)), ((), ()))


def dot(a, b, dims):
    return lax.dot_general(a, b, dims, preferred_element_type=jnp.float32)


def swap(block, axis, step):
    return lax.ppermute(block, axis, [(i, i ^ step) for i in range(lax.axis_size(axis))])


def attend_kernel(sizes, scalars, *refs):
    pieces, rows, n_keep, heads, turn, n_resp, n_pass = sizes
    refs = list(refs)
    q_ref, do_ref, ra_ref, rb_ref = refs[:4]
    pa_refs = refs[4 : 4 + pieces]
    pb_refs = refs[4 + pieces : 4 + 2 * pieces]
    prior_ref = refs[4 + 2 * pieces] if turn > 0 else None
    rest = refs[4 + 2 * pieces + (1 if turn > 0 else 0) + n_pass :]
    out_ref, dq_ref, dra_ref, drb_ref = rest[:4]
    final = turn == n_resp - 1
    n_out = 4 + (1 if not final or pieces == n_keep else 2)
    grads = rest[4:n_out]
    k_all, v_all, k_t, v_t, weights, probs, dscores, acc_k, acc_v, res_k, res_v = rest[n_out:]

    head = pl.program_id(0)
    prompt = scalars[turn]
    even = scalars[n_resp] == 0
    n_prompt = pieces * rows
    n_query = q_ref.shape[1]

    @pl.when(head == 0)
    def _():
        if turn == 0:
            acc_k[...] = jnp.zeros_like(acc_k)
            acc_v[...] = jnp.zeros_like(acc_v)
        elif turn == 1:
            before = scalars[0]
            acc_k[1 - before] = jnp.zeros(acc_k.shape[1:], jnp.float32)
            acc_v[1 - before] = jnp.zeros(acc_v.shape[1:], jnp.float32)
            acc_k[before] = prior_ref[0, 0]
            acc_v[before] = prior_ref[1, 0]
        else:
            acc_k[...] = prior_ref[0]
            acc_v[...] = prior_ref[1]

    def gather(dst, piece_refs, resp_ref):
        for i, ref in enumerate(piece_refs):
            dst[i * rows : (i + 1) * rows, :] = ref[0]
        dst[n_prompt:, :] = resp_ref[0]

    @pl.when((head == 0) & even)
    def _():
        gather(k_all, pa_refs, ra_ref)
        gather(v_all, pb_refs, rb_ref)

    @pl.when((head == 0) & jnp.logical_not(even))
    def _():
        gather(k_all, pb_refs, rb_ref)
        gather(v_all, pa_refs, ra_ref)

    @pl.when(head == 0)
    def _():
        res_k[...] = jnp.zeros_like(res_k)
        res_v[...] = jnp.zeros_like(res_v)
        k_t[...] = k_all[...].T
        v_t[...] = v_all[...].T

    n_blocks = n_query // BLOCK
    state = [dict() for _ in range(n_blocks)]

    def span(c):
        return slice(c * BLOCK, (c + 1) * BLOCK)

    def fold(x, op):
        return op(x.reshape(-1, 8, x.shape[-1]), axis=0)

    def stages(i):
        st = state[i]
        t = span(i)
        n_chunks = n_prompt // BLOCK + i + 1
        seen = n_chunks * BLOCK
        q = q_ref[0, t, :]
        do = do_ref[0, t, :]

        def score(c):
            if c == 0:
                st["s"] = dot(k_all[:seen, :], q, NT)
            s = st["s"][span(c), :]
            if c == n_chunks - 1:
                row = lax.broadcasted_iota(jnp.int32, (BLOCK, BLOCK), 0)
                col = lax.broadcasted_iota(jnp.int32, (BLOCK, BLOCK), 1)
                s = jnp.where(row <= col, s, MASKED)
            weights[span(c), t] = s
            top = fold(s, jnp.max)
            st["top"] = top if c == 0 else jnp.maximum(st["top"], top)
            if c == n_chunks - 1:
                st["top"] = jnp.max(st["top"], axis=0, keepdims=True) * SCALE

        def weigh(c):
            w = jnp.exp(weights[span(c), t] * SCALE - st["top"])
            weights[span(c), t] = w
            total = fold(w, jnp.sum)
            st["sum"] = total if c == 0 else st["sum"] + total
            if c == n_chunks - 1:
                st["inv"] = 1.0 / jnp.sum(st["sum"], axis=0, keepdims=True)

        def norm(c):
            probs[span(c), t] = (weights[span(c), t] * st["inv"]).astype(jnp.bfloat16)
            if c == n_chunks - 1:
                o = dot(v_t[:, :seen], probs[:seen, t], NN)
                out_ref[0, t, :] = o.T.astype(jnp.bfloat16)
                do_t = do.astype(jnp.float32).T
                st["delta"] = jnp.sum(o * do_t, axis=0, keepdims=True)
                st["inv"] = st["inv"] * SCALE

        def grad(c):
            if c == 0:
                st["dp"] = dot(v_all[:seen, :], do, NT)
            dp = st["dp"][span(c), :]
            ds = (weights[span(c), t] * st["inv"]) * (dp - st["delta"])
            dscores[span(c), t] = ds.astype(jnp.bfloat16)
            if c == n_chunks - 1:
                dq = dot(k_t[:, :seen], dscores[:seen, t], NN)
                dq_ref[0, t, :] = dq.T.astype(jnp.bfloat16)

        return [[functools.partial(f, c) for c in range(n_chunks)] for f in (score, weigh, norm, grad)]

    plan = [stages(i) for i in range(n_blocks)]
    for slot in range(4 + n_blocks - 1):
        groups = [plan[i][slot - i] for i in reversed(range(n_blocks)) if 0 <= slot - i < 4]
        for c in range(max(len(g) for g in groups)):
            for g in groups:
                if c < len(g):
                    g[c]()

    q_all = q_ref[0]
    do_all = do_ref[0]
    acc_v[prompt] += dot(probs[:n_prompt, :], do_all, NN)
    acc_k[prompt] += dot(dscores[:n_prompt, :], q_all, NN)
    for i in range(n_blocks):
        u = span(n_prompt // BLOCK + i)
        t0 = i * BLOCK
        res_v[span(i), :] += dot(probs[u, t0:], do_all[t0:], NN)
        res_k[span(i), :] += dot(dscores[u, t0:], q_all[t0:], NN)

    last = head == heads - 1

    @pl.when(last & even)
    def _():
        dra_ref[0] = res_k[...].astype(jnp.bfloat16)
        drb_ref[0] = res_v[...].astype(jnp.bfloat16)

    @pl.when(last & jnp.logical_not(even))
    def _():
        dra_ref[0] = res_v[...].astype(jnp.bfloat16)
        drb_ref[0] = res_k[...].astype(jnp.bfloat16)

    if not final:

        @pl.when(last)
        def _():
            if turn == 0:
                grads[0][0, 0] = acc_k[prompt]
                grads[0][1, 0] = acc_v[prompt]
            else:
                grads[0][0] = acc_k[...]
                grads[0][1] = acc_v[...]

        return

    def scatter(slot, acc):
        for i in range(pieces):
            for p_id in range(P_SIZE):
                val = acc[p_id, i * rows : (i + 1) * rows, :]
                if i < n_keep:
                    grads[0][i, p_id, :, slot * HD : (slot + 1) * HD] = val
                else:
                    grads[1][i - n_keep, p_id, :, slot * HD : (slot + 1) * HD] = val.astype(jnp.bfloat16)

    @pl.when(last & even)
    def _():
        scatter(0, acc_k)
        scatter(1, acc_v)

    @pl.when(last & jnp.logical_not(even))
    def _():
        scatter(0, acc_v)
        scatter(1, acc_k)


def attend(scalars, queries, d_out, resp_a, resp_b, prompt_a, prompt_b, n_keep, chunk, heads, turn, prior, shared, after=()):
    n_resp, n_query, _ = queries.shape
    pieces = len(prompt_a)
    rows = prompt_a[0][0].shape[1]
    n_prompt = pieces * rows
    n_keys = n_prompt + n_query
    n_send = pieces - n_keep
    final = turn == n_resp - 1
    shape = jax.ShapeDtypeStruct

    def resp_map(place):
        return lambda j, sc: (turn if place[0] else 0, 0, place[1](sc[n_resp]))

    def prompt_map(place):
        return lambda j, sc: (sc[turn], 0, place[1](sc[n_resp]))

    q_spec = pl.BlockSpec((1, n_query, HD), lambda j, sc: (turn, 0, chunk * heads + j))
    in_specs = [q_spec, q_spec]
    in_specs += [pl.BlockSpec((1, n_query, HD), resp_map(c)) for _, c in (resp_a, resp_b)]
    in_specs += [pl.BlockSpec((1, rows, HD), prompt_map(c)) for _, c in (*prompt_a, *prompt_b)]
    args = [queries, d_out, resp_a[0], resp_b[0], *[a for a, _ in (*prompt_a, *prompt_b)]]
    if turn > 0:
        in_specs.append(pl.BlockSpec(prior.shape, lambda j, sc: (0, 0, 0, 0)))
        args.append(prior)
    aliases = {}
    if shared is not None:
        aliases = {1 + len(args) + i: i for i in range(3)}
        args += list(shared)
    args += list(after)
    n_pass = len(args) - len(in_specs)
    in_specs += [pl.BlockSpec(memory_space=pl.ANY)] * n_pass
    out_specs = [
        q_spec,
        q_spec,
        pl.BlockSpec((1, n_query, HD), lambda j, sc: (turn, 0, resp_a[1][1](sc[n_resp]))),
        pl.BlockSpec((1, n_query, HD), lambda j, sc: (0, 0, 0)),
    ]
    out_shape = [
        shape(queries.shape, jnp.bfloat16),
        shape(queries.shape, jnp.bfloat16),
        shape(resp_a[0].shape, jnp.bfloat16),
        shape((1, n_query, HD), jnp.bfloat16),
    ]
    if final:
        grads = [shape((n_keep, P_SIZE, rows, 2 * HD), jnp.float32)]
        if n_send:
            grads.append(shape((n_send, P_SIZE, rows, 2 * HD), jnp.bfloat16))
    else:
        grads = [shape((2, 1 if turn == 0 else P_SIZE, n_prompt, HD), jnp.float32)]
    out_shape += grads
    out_specs += [pl.BlockSpec(g.shape, lambda j, sc: (0, 0, 0, 0)) for g in grads]
    scratch = [
        pltpu.VMEM((n_keys, HD), jnp.bfloat16),
        pltpu.VMEM((n_keys, HD), jnp.bfloat16),
        pltpu.VMEM((HD, n_keys), jnp.bfloat16),
        pltpu.VMEM((HD, n_keys), jnp.bfloat16),
        pltpu.VMEM((n_keys, n_query), jnp.float32),
        pltpu.VMEM((n_keys, n_query), jnp.bfloat16),
        pltpu.VMEM((n_keys, n_query), jnp.bfloat16),
        pltpu.VMEM((P_SIZE, n_prompt, HD), jnp.float32),
        pltpu.VMEM((P_SIZE, n_prompt, HD), jnp.float32),
        pltpu.VMEM((n_query, HD), jnp.float32),
        pltpu.VMEM((n_query, HD), jnp.float32),
    ]
    flops = 12 * heads * n_query * n_keys * HD
    return pl.pallas_call(
        functools.partial(attend_kernel, (pieces, rows, n_keep, heads, turn, n_resp, n_pass)),
        grid_spec=pltpu.PrefetchScalarGridSpec(
            num_scalar_prefetch=1,
            grid=(heads,),
            in_specs=in_specs,
            out_specs=out_specs,
            scratch_shapes=scratch,
        ),
        out_shape=out_shape,
        input_output_aliases=aliases,
        compiler_params=pltpu.CompilerParams(vmem_limit_bytes=40 * 2**20),
        cost_estimate=pl.CostEstimate(flops=2 * flops, bytes_accessed=4 * 2**20, transcendentals=0),
    )(scalars, *args)


def first(par):
    return 0


def per_device(queries, resp_kv, prompt_kv, prompt_of, d_out):
    pair_heads = prompt_kv.shape[2] // HD
    parity = lax.axis_index("prefix") % 2
    scalars = jnp.concatenate([prompt_of, parity[None].astype(jnp.int32)])
    if lax.axis_size("dp") == 4 and pair_heads % 2 == 0:
        return whole_heads(queries, resp_kv, prompt_kv, scalars, parity, d_out)
    return shared_head(queries, resp_kv, prompt_kv, scalars, parity, d_out)


def whole_heads(queries, resp_kv, prompt_kv, scalars, parity, d_out):
    n_own = prompt_kv.shape[2] // HD // 2
    n_resp, n_query, _ = queries.shape
    z = functools.partial(swap, axis="prefix", step=1)
    core, x, both = [functools.partial(swap, axis="dp", step=k) for k in (1, 2, 3)]
    own = [lambda par, h=h: par * n_own + h for h in range(n_own)]
    theirs = [(1 - parity) * n_own + h for h in range(n_own)]

    def resp_column(r, h):
        return lax.dynamic_slice(resp_kv, (r, 0, theirs[h] * HD), (1, n_query, HD))

    def prompt_column(which):
        return lax.dynamic_slice_in_dim(prompt_kv, which * HD, HD, axis=2)

    def order(values, done):
        return lax.optimization_barrier((tuple(values), tuple(done)))[0]

    pa, pb, resp_b = [], [], {}
    a0 = prompt_column(own[0](parity))
    b0 = z(prompt_column(theirs[0]))
    a2 = x(a0)
    resp_b[0, 0] = z(resp_column(0, 0))
    (b0,) = order([b0], [a2])
    b2 = x(b0)
    pa.append([a2, core(a0), core(a2)])
    pb.append([b0, b2, core(b0), core(b2)])

    shared, ready = None, ()
    d_resp, d_prompt = {}, []
    for h in range(n_own):
        prior = None
        if h + 1 < n_own:
            a0, b0, *rest = order(
                [prompt_column(own[h + 1](parity)), prompt_column(theirs[h + 1])]
                + [resp_column(r, h) for r in range(1, n_resp)],
                [pb[h][1]],
            )
            b0 = z(b0)
            for r in range(1, n_resp):
                resp_b[r, h] = z(rest[r - 1])
            a2 = x(a0)
        here = (True, own[h])
        for r in range(n_resp):
            att, dq, dra, drb, *grads = attend(
                scalars,
                queries,
                d_out,
                (resp_kv, here),
                (resp_b[r, h], (False, first)),
                [(prompt_kv, here)] + [(a, (False, first)) for a in pa[h]],
                [(a, (False, first)) for a in pb[h]],
                2,
                h,
                GROUP,
                r,
                prior,
                shared,
                ready if r == n_resp - 1 else (),
            )
            prior = grads[0]
            shared = (att, dq, dra)
            if r == 0 and h + 1 < n_own:
                a0, b0, *rest = order([a0, b0] + [resp_column(i, h + 1) for i in range(n_resp)], [drb])
                pb.append([b0, x(b0), core(b0), both(b0)])
                pa.append([a2, core(a0), core(a2)])
                for i in range(n_resp):
                    resp_b[i, h + 1] = z(rest[i])
            if (r, h) != (n_resp - 1, n_own - 1):
                d_resp[r, h] = z(drb)
        keep, send = grads
        if h == n_own - 1:
            (send, drb) = order([send, drb], [across, d_resp[0, h]])
            d_resp[n_resp - 1, h] = z(drb)
        sums = keep + core(send).astype(jnp.float32)
        part = sums[1].astype(jnp.bfloat16)
        across = x(part)
        ready = (part, *[d_resp[r, h] for r in range(n_resp)])
        total = sums[0] + across.astype(jnp.float32)
        other = z(total[:, :, HD:].astype(jnp.bfloat16))
        d_prompt.append((total[:, :, :HD], other.astype(jnp.float32)))

    even = parity == 0
    mine = jnp.concatenate([a for a, _ in d_prompt], axis=-1)
    other = jnp.concatenate([b for _, b in d_prompt], axis=-1)
    d_prompt = jnp.concatenate([jnp.where(even, mine, other), jnp.where(even, other, mine)], axis=-1)
    att, dq, d_resp_kv = shared
    received = jnp.concatenate(
        [jnp.concatenate([d_resp[r, h] for r in range(n_resp)], axis=0) for h in range(n_own)], axis=-1
    )
    d_resp_kv = lax.dynamic_update_slice_in_dim(d_resp_kv, received, (1 - parity) * n_own * HD, axis=2)
    return att, dq, d_resp_kv, d_prompt


def shared_head(queries, resp_kv, prompt_kv, scalars, parity, d_out):
    n_resp = queries.shape[0]
    local_heads = queries.shape[2] // HD
    prompt_a = lax.all_gather(prompt_kv, "dp", axis=1, tiled=True)
    prompt_b = swap(prompt_a, "prefix", 1)
    resp_b = swap(resp_kv, "prefix", 1)
    shared, prior, d_resp = None, None, []
    for r in range(n_resp):
        att, dq, dra, drb, prior = attend(
            scalars,
            queries,
            d_out,
            (resp_kv, (True, first)),
            (resp_b, (True, first)),
            [(prompt_a, (True, first))],
            [(prompt_b, (True, first))],
            1,
            0,
            local_heads,
            r,
            prior,
            shared,
        )
        shared = (att, dq, dra)
        d_resp.append(swap(drb, "prefix", 1))
    att, dq, dra = shared
    d_resp = (dra.astype(jnp.float32) + jnp.concatenate(d_resp, axis=0).astype(jnp.float32)).astype(jnp.bfloat16)
    other = swap(prior[0, :, :, HD:].astype(jnp.bfloat16), "prefix", 1)
    paired = prior[0, :, :, :HD] + other.astype(jnp.float32)
    d_prompt = lax.psum_scatter(paired, "dp", scatter_dimension=1, tiled=True)
    return att, dq, d_resp, d_prompt


def solution(mesh):
    in_specs = (
        P(("groups", "dp"), None, "prefix"),
        P(("groups", "dp"), None, "prefix"),
        P("groups", "dp", "prefix"),
        P(("groups", "dp")),
        P(("groups", "dp"), None, "prefix"),
    )
    out_specs = (
        P(("groups", "dp"), None, "prefix"),
        P(("groups", "dp"), None, "prefix"),
        P(("groups", "dp"), None, "prefix"),
        P("groups", "dp", "prefix"),
    )
    return jax.shard_map(
        per_device, mesh=mesh, in_specs=in_specs, out_specs=out_specs, check_vma=False
    )
```

```python
import functools

import jax
import jax.numpy as jnp
from jax import lax
from jax.experimental import pallas as pl
from jax.experimental.pallas import tpu as pltpu
from jax.sharding import PartitionSpec as P

H = 32
KVH = 8
HD = 128
P_SIZE = 2
GROUP = H // KVH
BLOCK = 256
MASKED = -1e30
SCALE = HD ** (-0.5)

NT = (((1,), (1,)), ((), ()))
NN = (((1,), (0,)), ((), ()))


def dot(a, b, dims):
    return lax.dot_general(a, b, dims, preferred_element_type=jnp.float32)


def swap(block, axis, step):
    return lax.ppermute(block, axis, [(i, i ^ step) for i in range(lax.axis_size(axis))])


def attend_kernel(sizes, scalars, *refs):
    pieces, rows, n_keep, heads, turn, n_resp, n_pass = sizes
    refs = list(refs)
    q_ref, do_ref, ra_ref, rb_ref = refs[:4]
    pa_refs = refs[4 : 4 + pieces]
    pb_refs = refs[4 + pieces : 4 + 2 * pieces]
    prior_ref = refs[4 + 2 * pieces] if turn > 0 else None
    rest = refs[4 + 2 * pieces + (1 if turn > 0 else 0) + n_pass :]
    out_ref, dq_ref, dra_ref, drb_ref = rest[:4]
    final = turn == n_resp - 1
    n_out = 4 + (1 if not final or pieces == n_keep else 2)
    grads = rest[4:n_out]
    k_all, v_all, k_t, v_t, weights, probs, dscores, q_scaled, do_scaled, acc_k, acc_v = rest[n_out:]

    head = pl.program_id(0)
    even = scalars[n_resp] == 0
    n_prompt = pieces * rows
    n_query = q_ref.shape[1]
    n_blocks = n_query // BLOCK
    n_first = n_prompt // BLOCK
    n_all = n_first + n_blocks

    def gather(dst, piece_refs, resp_ref):
        for i, ref in enumerate(piece_refs):
            dst[i * rows : (i + 1) * rows, :] = ref[0]
        dst[n_prompt:, :] = resp_ref[0]

    @pl.when((head == 0) & even)
    def _():
        gather(k_all, pa_refs, ra_ref)
        gather(v_all, pb_refs, rb_ref)

    @pl.when((head == 0) & jnp.logical_not(even))
    def _():
        gather(k_all, pb_refs, rb_ref)
        gather(v_all, pa_refs, ra_ref)

    @pl.when(head == 0)
    def _():
        k_t[...] = k_all[...].T
        v_t[...] = v_all[...].T

    def span(c):
        return slice(c * BLOCK, (c + 1) * BLOCK)

    def fold(x, op):
        return op(x.reshape(-1, 8, x.shape[-1]), axis=0)

    def stages(i):
        st = {}
        t = span(i)
        n_chunks = n_first + i + 1
        seen = n_chunks * BLOCK
        q = q_ref[0, t, :]
        do = do_ref[0, t, :]

        def score(c):
            s = dot(k_all[span(c), :], q, NT)
            if c == n_chunks - 1:
                row = lax.broadcasted_iota(jnp.int32, (BLOCK, BLOCK), 0)
                col = lax.broadcasted_iota(jnp.int32, (BLOCK, BLOCK), 1)
                s = jnp.where(row <= col, s, MASKED)
            weights[span(c), t] = s
            top = fold(s, jnp.max)
            st["top"] = top if c == 0 else jnp.maximum(st["top"], top)
            if c == n_chunks - 1:
                st["top"] = jnp.max(st["top"], axis=0, keepdims=True) * SCALE

        def weigh(c):
            w = jnp.exp(weights[span(c), t] * SCALE - st["top"])
            weights[span(c), t] = w
            probs[span(c), t] = w.astype(jnp.bfloat16)
            total = fold(w, jnp.sum)
            st["sum"] = total if c == 0 else st["sum"] + total

        def output(c):
            if c > 0:
                return
            st["inv"] = 1.0 / jnp.sum(st["sum"], axis=0, keepdims=True)
            o = dot(v_t[:, :seen], probs[:seen, t], NN) * st["inv"]
            do_t = do.astype(jnp.float32).T
            st["delta"] = jnp.sum(o * do_t, axis=0, keepdims=True)
            out_ref[0, t, :] = o.T.astype(jnp.bfloat16)
            inv_rows = jnp.broadcast_to(st["inv"], (HD, BLOCK)).T
            do_scaled[t, :] = (do.astype(jnp.float32) * inv_rows).astype(jnp.bfloat16)
            q_scaled[t, :] = (q.astype(jnp.float32) * (inv_rows * SCALE)).astype(jnp.bfloat16)

        def grad(c):
            dp = dot(v_all[span(c), :], do, NT)
            ds = weights[span(c), t] * (dp - st["delta"])
            dscores[span(c), t] = ds.astype(jnp.bfloat16)

        def query(c):
            if c > 0:
                return
            dq = dot(k_t[:, :seen], dscores[:seen, t], NN) * (st["inv"] * SCALE)
            dq_ref[0, t, :] = dq.T.astype(jnp.bfloat16)

        return [[functools.partial(f, c) for c in range(n_chunks)] for f in (score, weigh, output, grad, query)]

    def add_values(c):
        t0 = max(c - n_first, 0) * BLOCK
        acc_v[span(c), :] += dot(probs[span(c), t0:], do_scaled[t0:, :], NN)

    def add_keys(c):
        t0 = max(c - n_first, 0) * BLOCK
        acc_k[span(c), :] += dot(dscores[span(c), t0:], q_scaled[t0:, :], NN)

    plan = [stages(i) for i in range(n_blocks)]
    former = [[functools.partial(add_values, c) for c in range(n_all)]]
    former += [[functools.partial(add_keys, c) for c in range(n_all)]]
    for slot in range(5 + n_blocks - 1):
        groups = [former[slot]] if slot < 2 else []
        groups += [plan[i][slot - i] for i in reversed(range(n_blocks)) if 0 <= slot - i < 5]
        for c in range(max(len(g) for g in groups)):
            for g in groups:
                if c < len(g):
                    g[c]()

    @pl.when(head == 0)
    def _():
        acc_k[...] = jnp.zeros_like(acc_k)
        acc_v[...] = jnp.zeros_like(acc_v)

    last = head == heads - 1

    @pl.when(last)
    def _():
        for c in range(n_all):
            add_values(c)
            add_keys(c)

    def respond(ref, acc):
        ref[0] = acc[n_prompt:, :].astype(jnp.bfloat16)

    @pl.when(last & even)
    def _():
        respond(dra_ref, acc_k)
        respond(drb_ref, acc_v)

    @pl.when(last & jnp.logical_not(even))
    def _():
        respond(dra_ref, acc_v)
        respond(drb_ref, acc_k)

    def total(which, acc, p_id, at):
        val = jnp.where(scalars[turn] == p_id, acc[at, :], 0.0)
        if turn == 1:
            val += jnp.where(scalars[0] == p_id, prior_ref[which, 0, at, :], 0.0)
        elif turn > 1:
            val += prior_ref[which, p_id, at, :]
        return val

    if not final:

        @pl.when(last)
        def _():
            for which, acc in enumerate((acc_k, acc_v)):
                if turn == 0:
                    grads[0][which, 0] = acc[:n_prompt, :]
                else:
                    for p_id in range(P_SIZE):
                        grads[0][which, p_id] = total(which, acc, p_id, slice(0, n_prompt))

        return

    def scatter(slot, which, acc):
        lanes = slice(slot * HD, (slot + 1) * HD)
        for i in range(pieces):
            for p_id in range(P_SIZE):
                val = total(which, acc, p_id, slice(i * rows, (i + 1) * rows))
                if i < n_keep:
                    grads[0][i, p_id, :, lanes] = val
                else:
                    grads[1][i - n_keep, p_id, :, lanes] = val.astype(jnp.bfloat16)

    @pl.when(last & even)
    def _():
        scatter(0, 0, acc_k)
        scatter(1, 1, acc_v)

    @pl.when(last & jnp.logical_not(even))
    def _():
        scatter(0, 1, acc_v)
        scatter(1, 0, acc_k)


def attend(scalars, queries, d_out, resp_a, resp_b, prompt_a, prompt_b, n_keep, chunk, heads, turn, prior, shared, after=()):
    n_resp, n_query, _ = queries.shape
    pieces = len(prompt_a)
    rows = prompt_a[0][0].shape[1]
    n_prompt = pieces * rows
    n_keys = n_prompt + n_query
    n_send = pieces - n_keep
    final = turn == n_resp - 1
    shape = jax.ShapeDtypeStruct

    def resp_map(place):
        return lambda j, sc: (turn if place[0] else 0, 0, place[1](sc[n_resp]))

    def prompt_map(place):
        return lambda j, sc: (sc[turn], 0, place[1](sc[n_resp]))

    q_spec = pl.BlockSpec((1, n_query, HD), lambda j, sc: (turn, 0, chunk * heads + j))
    in_specs = [q_spec, q_spec]
    in_specs += [pl.BlockSpec((1, n_query, HD), resp_map(c)) for _, c in (resp_a, resp_b)]
    in_specs += [pl.BlockSpec((1, rows, HD), prompt_map(c)) for _, c in (*prompt_a, *prompt_b)]
    args = [queries, d_out, resp_a[0], resp_b[0], *[a for a, _ in (*prompt_a, *prompt_b)]]
    if turn > 0:
        in_specs.append(pl.BlockSpec(prior.shape, lambda j, sc: (0, 0, 0, 0)))
        args.append(prior)
    aliases = {}
    if shared is not None:
        aliases = {1 + len(args) + i: i for i in range(3)}
        args += list(shared)
    args += list(after)
    n_pass = len(args) - len(in_specs)
    in_specs += [pl.BlockSpec(memory_space=pl.ANY)] * n_pass
    out_specs = [
        q_spec,
        q_spec,
        pl.BlockSpec((1, n_query, HD), lambda j, sc: (turn, 0, resp_a[1][1](sc[n_resp]))),
        pl.BlockSpec((1, n_query, HD), lambda j, sc: (0, 0, 0)),
    ]
    out_shape = [
        shape(queries.shape, jnp.bfloat16),
        shape(queries.shape, jnp.bfloat16),
        shape(resp_a[0].shape, jnp.bfloat16),
        shape((1, n_query, HD), jnp.bfloat16),
    ]
    if final:
        grads = [shape((n_keep, P_SIZE, rows, 2 * HD), jnp.float32)]
        if n_send:
            grads.append(shape((n_send, P_SIZE, rows, 2 * HD), jnp.bfloat16))
    else:
        grads = [shape((2, 1 if turn == 0 else P_SIZE, n_prompt, HD), jnp.float32)]
    out_shape += grads
    out_specs += [pl.BlockSpec(g.shape, lambda j, sc: (0, 0, 0, 0)) for g in grads]
    scratch = [
        pltpu.VMEM((n_keys, HD), jnp.bfloat16),
        pltpu.VMEM((n_keys, HD), jnp.bfloat16),
        pltpu.VMEM((HD, n_keys), jnp.bfloat16),
        pltpu.VMEM((HD, n_keys), jnp.bfloat16),
        pltpu.VMEM((n_keys, n_query), jnp.float32),
        pltpu.VMEM((n_keys, n_query), jnp.bfloat16),
        pltpu.VMEM((n_keys, n_query), jnp.bfloat16),
        pltpu.VMEM((n_query, HD), jnp.bfloat16),
        pltpu.VMEM((n_query, HD), jnp.bfloat16),
        pltpu.VMEM((n_keys, HD), jnp.float32),
        pltpu.VMEM((n_keys, HD), jnp.float32),
    ]
    flops = 12 * heads * n_query * n_keys * HD
    return pl.pallas_call(
        functools.partial(attend_kernel, (pieces, rows, n_keep, heads, turn, n_resp, n_pass)),
        grid_spec=pltpu.PrefetchScalarGridSpec(
            num_scalar_prefetch=1,
            grid=(heads,),
            in_specs=in_specs,
            out_specs=out_specs,
            scratch_shapes=scratch,
        ),
        out_shape=out_shape,
        input_output_aliases=aliases,
        compiler_params=pltpu.CompilerParams(vmem_limit_bytes=40 * 2**20),
        cost_estimate=pl.CostEstimate(flops=2 * flops, bytes_accessed=4 * 2**20, transcendentals=0),
    )(scalars, *args)


def first(par):
    return 0


def per_device(queries, resp_kv, prompt_kv, prompt_of, d_out):
    pair_heads = prompt_kv.shape[2] // HD
    parity = lax.axis_index("prefix") % 2
    scalars = jnp.concatenate([prompt_of, parity[None].astype(jnp.int32)])
    if lax.axis_size("dp") == 4 and pair_heads % 2 == 0:
        return whole_heads(queries, resp_kv, prompt_kv, scalars, parity, d_out)
    return shared_head(queries, resp_kv, prompt_kv, scalars, parity, d_out)


def whole_heads(queries, resp_kv, prompt_kv, scalars, parity, d_out):
    n_own = prompt_kv.shape[2] // HD // 2
    n_resp, n_query, _ = queries.shape
    z = functools.partial(swap, axis="prefix", step=1)
    core, x, both = [functools.partial(swap, axis="dp", step=k) for k in (1, 2, 3)]
    own = [lambda par, h=h: par * n_own + h for h in range(n_own)]
    theirs = [(1 - parity) * n_own + h for h in range(n_own)]

    def resp_column(r, h):
        return lax.dynamic_slice(resp_kv, (r, 0, theirs[h] * HD), (1, n_query, HD))

    def prompt_column(which):
        return lax.dynamic_slice_in_dim(prompt_kv, which * HD, HD, axis=2)

    def order(values, done):
        return lax.optimization_barrier((tuple(values), tuple(done)))[0]

    pa, pb, resp_b = [], [], {}
    a0 = prompt_column(own[0](parity))
    b0 = z(prompt_column(theirs[0]))
    a2 = x(a0)
    resp_b[0, 0] = z(resp_column(0, 0))
    (b0,) = order([b0], [a2])
    b2 = x(b0)
    pa.append([a2, core(a0), core(a2)])
    pb.append([b0, b2, core(b0), core(b2)])

    shared, ready = None, ()
    d_resp, d_prompt = {}, []
    for h in range(n_own):
        prior = None
        if h + 1 < n_own:
            a0, b0, *rest = order(
                [prompt_column(own[h + 1](parity)), prompt_column(theirs[h + 1])]
                + [resp_column(r, h) for r in range(1, n_resp)],
                [pb[h][1]],
            )
            b0 = z(b0)
            for r in range(1, n_resp):
                resp_b[r, h] = z(rest[r - 1])
            a2 = x(a0)
        here = (True, own[h])
        for r in range(n_resp):
            att, dq, dra, drb, *grads = attend(
                scalars,
                queries,
                d_out,
                (resp_kv, here),
                (resp_b[r, h], (False, first)),
                [(prompt_kv, here)] + [(a, (False, first)) for a in pa[h]],
                [(a, (False, first)) for a in pb[h]],
                2,
                h,
                GROUP,
                r,
                prior,
                shared,
                ready if r == n_resp - 1 else (),
            )
            prior = grads[0]
            shared = (att, dq, dra)
            if r == 0 and h + 1 < n_own:
                a0, b0, *rest = order([a0, b0] + [resp_column(i, h + 1) for i in range(n_resp)], [drb])
                pb.append([b0, x(b0), core(b0), both(b0)])
                pa.append([a2, core(a0), core(a2)])
                for i in range(n_resp):
                    resp_b[i, h + 1] = z(rest[i])
            if (r, h) != (n_resp - 1, n_own - 1):
                d_resp[r, h] = z(drb)
        keep, send = grads
        if h == n_own - 1:
            (send, drb) = order([send, drb], [across, d_resp[0, h]])
            d_resp[n_resp - 1, h] = z(drb)
        sums = keep + core(send).astype(jnp.float32)
        part = sums[1].astype(jnp.bfloat16)
        across = x(part)
        ready = (part, *[d_resp[r, h] for r in range(n_resp)])
        total = sums[0] + across.astype(jnp.float32)
        other = z(total[:, :, HD:].astype(jnp.bfloat16))
        d_prompt.append((total[:, :, :HD], other.astype(jnp.float32)))

    even = parity == 0
    mine = jnp.concatenate([a for a, _ in d_prompt], axis=-1)
    other = jnp.concatenate([b for _, b in d_prompt], axis=-1)
    d_prompt = jnp.concatenate([jnp.where(even, mine, other), jnp.where(even, other, mine)], axis=-1)
    att, dq, d_resp_kv = shared
    received = jnp.concatenate(
        [jnp.concatenate([d_resp[r, h] for r in range(n_resp)], axis=0) for h in range(n_own)], axis=-1
    )
    d_resp_kv = lax.dynamic_update_slice_in_dim(d_resp_kv, received, (1 - parity) * n_own * HD, axis=2)
    return att, dq, d_resp_kv, d_prompt


def shared_head(queries, resp_kv, prompt_kv, scalars, parity, d_out):
    n_resp = queries.shape[0]
    local_heads = queries.shape[2] // HD
    prompt_a = lax.all_gather(prompt_kv, "dp", axis=1, tiled=True)
    prompt_b = swap(prompt_a, "prefix", 1)
    resp_b = swap(resp_kv, "prefix", 1)
    shared, prior, d_resp = None, None, []
    for r in range(n_resp):
        att, dq, dra, drb, prior = attend(
            scalars,
            queries,
            d_out,
            (resp_kv, (True, first)),
            (resp_b, (True, first)),
            [(prompt_a, (True, first))],
            [(prompt_b, (True, first))],
            1,
            0,
            local_heads,
            r,
            prior,
            shared,
        )
        shared = (att, dq, dra)
        d_resp.append(swap(drb, "prefix", 1))
    att, dq, dra = shared
    d_resp = (dra.astype(jnp.float32) + jnp.concatenate(d_resp, axis=0).astype(jnp.float32)).astype(jnp.bfloat16)
    other = swap(prior[0, :, :, HD:].astype(jnp.bfloat16), "prefix", 1)
    paired = prior[0, :, :, :HD] + other.astype(jnp.float32)
    d_prompt = lax.psum_scatter(paired, "dp", scatter_dimension=1, tiled=True)
    return att, dq, d_resp, d_prompt


def solution(mesh):
    in_specs = (
        P(("groups", "dp"), None, "prefix"),
        P(("groups", "dp"), None, "prefix"),
        P("groups", "dp", "prefix"),
        P(("groups", "dp")),
        P(("groups", "dp"), None, "prefix"),
    )
    out_specs = (
        P(("groups", "dp"), None, "prefix"),
        P(("groups", "dp"), None, "prefix"),
        P(("groups", "dp"), None, "prefix"),
        P("groups", "dp", "prefix"),
    )
    return jax.shard_map(
        per_device, mesh=mesh, in_specs=in_specs, out_specs=out_specs, check_vma=False
    )
```

```python
import functools

import jax
import jax.numpy as jnp
from jax import lax
from jax.experimental import pallas as pl
from jax.experimental.pallas import tpu as pltpu
from jax.sharding import PartitionSpec as P

H = 32
KVH = 8
HD = 128
P_SIZE = 2
GROUP = H // KVH
BLOCK = 256
CHUNK = 512
MASKED = -1e30
SCALE = HD ** (-0.5)

NT = (((1,), (1,)), ((), ()))
NN = (((1,), (0,)), ((), ()))


def dot(a, b, dims):
    return lax.dot_general(a, b, dims, preferred_element_type=jnp.float32)


def swap(block, axis, step):
    return lax.ppermute(block, axis, [(i, i ^ step) for i in range(lax.axis_size(axis))])


def attend_kernel(sizes, scalars, *refs):
    pieces, rows, n_keep, heads, turn, n_resp, n_pass = sizes
    refs = list(refs)
    q_ref, do_ref, ra_ref, rb_ref = refs[:4]
    pa_refs = refs[4 : 4 + pieces]
    pb_refs = refs[4 + pieces : 4 + 2 * pieces]
    prior_ref = refs[4 + 2 * pieces] if turn > 0 else None
    rest = refs[4 + 2 * pieces + (1 if turn > 0 else 0) + n_pass :]
    out_ref, dq_ref, dra_ref, drb_ref = rest[:4]
    final = turn == n_resp - 1
    n_out = 4 + (1 if not final or pieces == n_keep else 2)
    grads = rest[4:n_out]
    k_all, v_all, k_t, v_t, weights, probs, dscores, acc_k, acc_v = rest[n_out:]

    head = pl.program_id(0)
    even = scalars[n_resp] == 0
    n_prompt = pieces * rows
    n_query = q_ref.shape[1]
    n_blocks = n_query // BLOCK
    n_first = n_prompt // BLOCK

    def gather(dst, piece_refs, resp_ref):
        for i, ref in enumerate(piece_refs):
            dst[i * rows : (i + 1) * rows, :] = ref[0]
        dst[n_prompt:, :] = resp_ref[0]

    @pl.when((head == 0) & even)
    def _():
        gather(k_all, pa_refs, ra_ref)
        gather(v_all, pb_refs, rb_ref)

    @pl.when((head == 0) & jnp.logical_not(even))
    def _():
        gather(k_all, pb_refs, rb_ref)
        gather(v_all, pa_refs, ra_ref)

    @pl.when(head == 0)
    def _():
        k_t[...] = k_all[...].T
        v_t[...] = v_all[...].T

    def span(c):
        return slice(c * BLOCK, (c + 1) * BLOCK)

    def fold(x, op):
        return op(x.reshape(-1, 8, x.shape[-1]), axis=0)

    def stages(i):
        st = {}
        t = span(i)
        seen = n_prompt + (i + 1) * BLOCK
        parts = [slice(u, min(u + CHUNK, seen)) for u in range(0, seen, CHUNK)]
        n_parts = len(parts)
        q = q_ref[0, t, :]
        do = do_ref[0, t, :]

        def score(c):
            s = dot(k_all[parts[c], :], q, NT)
            if c == n_parts - 1:
                row = lax.broadcasted_iota(jnp.int32, (BLOCK, BLOCK), 0)
                col = lax.broadcasted_iota(jnp.int32, (BLOCK, BLOCK), 1)
                diag = jnp.where(row <= col, s[-BLOCK:], MASKED)
                s = diag if s.shape[0] == BLOCK else jnp.concatenate([s[:-BLOCK], diag], axis=0)
            weights[parts[c], t] = s
            top = fold(s, jnp.max)
            st["top"] = top if c == 0 else jnp.maximum(st["top"], top)
            if c == n_parts - 1:
                st["top"] = jnp.max(st["top"], axis=0, keepdims=True) * SCALE

        def weigh(c):
            w = jnp.exp(weights[parts[c], t] * SCALE - st["top"])
            weights[parts[c], t] = w
            total = fold(w, jnp.sum)
            st["sum"] = total if c == 0 else st["sum"] + total
            if c == n_parts - 1:
                st["inv"] = 1.0 / jnp.sum(st["sum"], axis=0, keepdims=True)

        def norm(c):
            probs[parts[c], t] = (weights[parts[c], t] * st["inv"]).astype(jnp.bfloat16)
            if c == n_parts - 1:
                o = dot(v_t[:, :seen], probs[:seen, t], NN)
                out_ref[0, t, :] = o.T.astype(jnp.bfloat16)
                do_t = do.astype(jnp.float32).T
                st["delta"] = jnp.sum(o * do_t, axis=0, keepdims=True)
                st["inv"] = st["inv"] * SCALE

        def grad(c):
            dp = dot(v_all[parts[c], :], do, NT)
            ds = (weights[parts[c], t] * st["inv"]) * (dp - st["delta"])
            dscores[parts[c], t] = ds.astype(jnp.bfloat16)
            if c == n_parts - 1:
                dq = dot(k_t[:, :seen], dscores[:seen, t], NN)
                dq_ref[0, t, :] = dq.T.astype(jnp.bfloat16)

        return [[functools.partial(f, c) for c in range(n_parts)] for f in (score, weigh, norm, grad)]

    plan = [stages(i) for i in range(n_blocks)]
    for slot in range(4 + n_blocks - 1):
        groups = [plan[i][slot - i] for i in reversed(range(n_blocks)) if 0 <= slot - i < 4]
        for c in range(max(len(g) for g in groups)):
            for g in groups:
                if c < len(g):
                    g[c]()

    @pl.when(head == 0)
    def _():
        acc_k[...] = jnp.zeros_like(acc_k)
        acc_v[...] = jnp.zeros_like(acc_v)

    q_all = q_ref[0]
    do_all = do_ref[0]
    bounds = [(slice(u, min(u + CHUNK, n_prompt)), 0) for u in range(0, n_prompt, CHUNK)]
    bounds += [(span(n_first + i), i * BLOCK) for i in range(n_blocks)]
    for u, t0 in bounds:
        acc_v[u, :] += dot(probs[u, t0:], do_all[t0:], NN)
        acc_k[u, :] += dot(dscores[u, t0:], q_all[t0:], NN)

    last = head == heads - 1

    def respond(ref, acc):
        ref[0] = acc[n_prompt:, :].astype(jnp.bfloat16)

    @pl.when(last & even)
    def _():
        respond(dra_ref, acc_k)
        respond(drb_ref, acc_v)

    @pl.when(last & jnp.logical_not(even))
    def _():
        respond(dra_ref, acc_v)
        respond(drb_ref, acc_k)

    def total(which, acc, p_id, at):
        val = jnp.where(scalars[turn] == p_id, acc[at, :], 0.0)
        if turn == 1:
            val += jnp.where(scalars[0] == p_id, prior_ref[which, 0, at, :], 0.0)
        elif turn > 1:
            val += prior_ref[which, p_id, at, :]
        return val

    if not final:

        @pl.when(last)
        def _():
            for which, acc in enumerate((acc_k, acc_v)):
                if turn == 0:
                    grads[0][which, 0] = acc[:n_prompt, :]
                else:
                    for p_id in range(P_SIZE):
                        grads[0][which, p_id] = total(which, acc, p_id, slice(0, n_prompt))

        return

    def scatter(slot, which, acc):
        lanes = slice(slot * HD, (slot + 1) * HD)
        for i in range(pieces):
            for p_id in range(P_SIZE):
                val = total(which, acc, p_id, slice(i * rows, (i + 1) * rows))
                if i < n_keep:
                    grads[0][i, p_id, :, lanes] = val
                else:
                    grads[1][i - n_keep, p_id, :, lanes] = val.astype(jnp.bfloat16)

    @pl.when(last & even)
    def _():
        scatter(0, 0, acc_k)
        scatter(1, 1, acc_v)

    @pl.when(last & jnp.logical_not(even))
    def _():
        scatter(0, 1, acc_v)
        scatter(1, 0, acc_k)


def attend(scalars, queries, d_out, resp_a, resp_b, prompt_a, prompt_b, n_keep, chunk, heads, turn, prior, shared, after=()):
    n_resp, n_query, _ = queries.shape
    pieces = len(prompt_a)
    rows = prompt_a[0][0].shape[1]
    n_prompt = pieces * rows
    n_keys = n_prompt + n_query
    n_send = pieces - n_keep
    final = turn == n_resp - 1
    shape = jax.ShapeDtypeStruct

    def resp_map(place):
        return lambda j, sc: (turn if place[0] else 0, 0, place[1](sc[n_resp]))

    def prompt_map(place):
        return lambda j, sc: (sc[turn], 0, place[1](sc[n_resp]))

    q_spec = pl.BlockSpec((1, n_query, HD), lambda j, sc: (turn, 0, chunk * heads + j))
    in_specs = [q_spec, q_spec]
    in_specs += [pl.BlockSpec((1, n_query, HD), resp_map(c)) for _, c in (resp_a, resp_b)]
    in_specs += [pl.BlockSpec((1, rows, HD), prompt_map(c)) for _, c in (*prompt_a, *prompt_b)]
    args = [queries, d_out, resp_a[0], resp_b[0], *[a for a, _ in (*prompt_a, *prompt_b)]]
    if turn > 0:
        in_specs.append(pl.BlockSpec(prior.shape, lambda j, sc: (0, 0, 0, 0)))
        args.append(prior)
    aliases = {}
    if shared is not None:
        aliases = {1 + len(args) + i: i for i in range(3)}
        args += list(shared)
    args += list(after)
    n_pass = len(args) - len(in_specs)
    in_specs += [pl.BlockSpec(memory_space=pl.ANY)] * n_pass
    out_specs = [
        q_spec,
        q_spec,
        pl.BlockSpec((1, n_query, HD), lambda j, sc: (turn, 0, resp_a[1][1](sc[n_resp]))),
        pl.BlockSpec((1, n_query, HD), lambda j, sc: (0, 0, 0)),
    ]
    out_shape = [
        shape(queries.shape, jnp.bfloat16),
        shape(queries.shape, jnp.bfloat16),
        shape(resp_a[0].shape, jnp.bfloat16),
        shape((1, n_query, HD), jnp.bfloat16),
    ]
    if final:
        grads = [shape((n_keep, P_SIZE, rows, 2 * HD), jnp.float32)]
        if n_send:
            grads.append(shape((n_send, P_SIZE, rows, 2 * HD), jnp.bfloat16))
    else:
        grads = [shape((2, 1 if turn == 0 else P_SIZE, n_prompt, HD), jnp.float32)]
    out_shape += grads
    out_specs += [pl.BlockSpec(g.shape, lambda j, sc: (0, 0, 0, 0)) for g in grads]
    scratch = [
        pltpu.VMEM((n_keys, HD), jnp.bfloat16),
        pltpu.VMEM((n_keys, HD), jnp.bfloat16),
        pltpu.VMEM((HD, n_keys), jnp.bfloat16),
        pltpu.VMEM((HD, n_keys), jnp.bfloat16),
        pltpu.VMEM((n_keys, n_query), jnp.float32),
        pltpu.VMEM((n_keys, n_query), jnp.bfloat16),
        pltpu.VMEM((n_keys, n_query), jnp.bfloat16),
        pltpu.VMEM((n_keys, HD), jnp.float32),
        pltpu.VMEM((n_keys, HD), jnp.float32),
    ]
    flops = 12 * heads * n_query * n_keys * HD
    return pl.pallas_call(
        functools.partial(attend_kernel, (pieces, rows, n_keep, heads, turn, n_resp, n_pass)),
        grid_spec=pltpu.PrefetchScalarGridSpec(
            num_scalar_prefetch=1,
            grid=(heads,),
            in_specs=in_specs,
            out_specs=out_specs,
            scratch_shapes=scratch,
        ),
        out_shape=out_shape,
        input_output_aliases=aliases,
        compiler_params=pltpu.CompilerParams(vmem_limit_bytes=60 * 2**20),
        cost_estimate=pl.CostEstimate(flops=2 * flops, bytes_accessed=4 * 2**20, transcendentals=0),
    )(scalars, *args)


def first(par):
    return 0


def per_device(queries, resp_kv, prompt_kv, prompt_of, d_out):
    pair_heads = prompt_kv.shape[2] // HD
    parity = lax.axis_index("prefix") % 2
    scalars = jnp.concatenate([prompt_of, parity[None].astype(jnp.int32)])
    if lax.axis_size("dp") == 4 and pair_heads % 2 == 0:
        return whole_heads(queries, resp_kv, prompt_kv, scalars, parity, d_out)
    return shared_head(queries, resp_kv, prompt_kv, scalars, parity, d_out)


def whole_heads(queries, resp_kv, prompt_kv, scalars, parity, d_out):
    n_own = prompt_kv.shape[2] // HD // 2
    n_resp, n_query, _ = queries.shape
    z = functools.partial(swap, axis="prefix", step=1)
    core, x, both = [functools.partial(swap, axis="dp", step=k) for k in (1, 2, 3)]
    own = [lambda par, h=h: par * n_own + h for h in range(n_own)]
    theirs = [(1 - parity) * n_own + h for h in range(n_own)]

    def resp_column(r, h):
        return lax.dynamic_slice(resp_kv, (r, 0, theirs[h] * HD), (1, n_query, HD))

    def prompt_column(which):
        return lax.dynamic_slice_in_dim(prompt_kv, which * HD, HD, axis=2)

    def order(values, done):
        return lax.optimization_barrier((tuple(values), tuple(done)))[0]

    pa, pb, resp_b = [], [], {}
    a0 = prompt_column(own[0](parity))
    b0 = z(prompt_column(theirs[0]))
    a2 = x(a0)
    resp_b[0, 0] = z(resp_column(0, 0))
    (b0,) = order([b0], [a2])
    b2 = x(b0)
    pa.append([a2, core(a0), core(a2)])
    pb.append([b0, b2, core(b0), core(b2)])

    shared, ready = None, ()
    d_resp, d_prompt = {}, []
    for h in range(n_own):
        prior = None
        if h + 1 < n_own:
            a0, b0, *rest = order(
                [prompt_column(own[h + 1](parity)), prompt_column(theirs[h + 1])]
                + [resp_column(r, h) for r in range(1, n_resp)],
                [pb[h][1]],
            )
            b0 = z(b0)
            for r in range(1, n_resp):
                resp_b[r, h] = z(rest[r - 1])
            a2 = x(a0)
        here = (True, own[h])
        for r in range(n_resp):
            att, dq, dra, drb, *grads = attend(
                scalars,
                queries,
                d_out,
                (resp_kv, here),
                (resp_b[r, h], (False, first)),
                [(prompt_kv, here)] + [(a, (False, first)) for a in pa[h]],
                [(a, (False, first)) for a in pb[h]],
                2,
                h,
                GROUP,
                r,
                prior,
                shared,
                ready if r == n_resp - 1 else (),
            )
            prior = grads[0]
            shared = (att, dq, dra)
            if r == 0 and h + 1 < n_own:
                a0, b0, *rest = order([a0, b0] + [resp_column(i, h + 1) for i in range(n_resp)], [drb])
                pb.append([b0, x(b0), core(b0), both(b0)])
                pa.append([a2, core(a0), core(a2)])
                for i in range(n_resp):
                    resp_b[i, h + 1] = z(rest[i])
            if (r, h) != (n_resp - 1, n_own - 1):
                d_resp[r, h] = z(drb)
        keep, send = grads
        if h == n_own - 1:
            (send, drb) = order([send, drb], [across, d_resp[0, h]])
            d_resp[n_resp - 1, h] = z(drb)
        sums = keep + core(send).astype(jnp.float32)
        part = sums[1].astype(jnp.bfloat16)
        across = x(part)
        ready = (part, *[d_resp[r, h] for r in range(n_resp)])
        total = sums[0] + across.astype(jnp.float32)
        other = z(total[:, :, HD:].astype(jnp.bfloat16))
        d_prompt.append((total[:, :, :HD], other.astype(jnp.float32)))

    even = parity == 0
    mine = jnp.concatenate([a for a, _ in d_prompt], axis=-1)
    other = jnp.concatenate([b for _, b in d_prompt], axis=-1)
    d_prompt = jnp.concatenate([jnp.where(even, mine, other), jnp.where(even, other, mine)], axis=-1)
    att, dq, d_resp_kv = shared
    received = jnp.concatenate(
        [jnp.concatenate([d_resp[r, h] for r in range(n_resp)], axis=0) for h in range(n_own)], axis=-1
    )
    d_resp_kv = lax.dynamic_update_slice_in_dim(d_resp_kv, received, (1 - parity) * n_own * HD, axis=2)
    return att, dq, d_resp_kv, d_prompt


def shared_head(queries, resp_kv, prompt_kv, scalars, parity, d_out):
    n_resp = queries.shape[0]
    local_heads = queries.shape[2] // HD
    prompt_a = lax.all_gather(prompt_kv, "dp", axis=1, tiled=True)
    prompt_b = swap(prompt_a, "prefix", 1)
    resp_b = swap(resp_kv, "prefix", 1)
    shared, prior, d_resp = None, None, []
    for r in range(n_resp):
        att, dq, dra, drb, prior = attend(
            scalars,
            queries,
            d_out,
            (resp_kv, (True, first)),
            (resp_b, (True, first)),
            [(prompt_a, (True, first))],
            [(prompt_b, (True, first))],
            1,
            0,
            local_heads,
            r,
            prior,
            shared,
        )
        shared = (att, dq, dra)
        d_resp.append(swap(drb, "prefix", 1))
    att, dq, dra = shared
    d_resp = (dra.astype(jnp.float32) + jnp.concatenate(d_resp, axis=0).astype(jnp.float32)).astype(jnp.bfloat16)
    other = swap(prior[0, :, :, HD:].astype(jnp.bfloat16), "prefix", 1)
    paired = prior[0, :, :, :HD] + other.astype(jnp.float32)
    d_prompt = lax.psum_scatter(paired, "dp", scatter_dimension=1, tiled=True)
    return att, dq, d_resp, d_prompt


def solution(mesh):
    in_specs = (
        P(("groups", "dp"), None, "prefix"),
        P(("groups", "dp"), None, "prefix"),
        P("groups", "dp", "prefix"),
        P(("groups", "dp")),
        P(("groups", "dp"), None, "prefix"),
    )
    out_specs = (
        P(("groups", "dp"), None, "prefix"),
        P(("groups", "dp"), None, "prefix"),
        P(("groups", "dp"), None, "prefix"),
        P("groups", "dp", "prefix"),
    )
    return jax.shard_map(
        per_device, mesh=mesh, in_specs=in_specs, out_specs=out_specs, check_vma=False
    )
```

```python
import functools

import jax
import jax.numpy as jnp
from jax import lax
from jax.experimental import pallas as pl
from jax.experimental.pallas import tpu as pltpu
from jax.sharding import PartitionSpec as P

H = 32
KVH = 8
HD = 128
P_SIZE = 2
GROUP = H // KVH
BLOCK = 256
CHUNK = 128
MASKED = -1e30
SCALE = HD ** (-0.5)

NT = (((1,), (1,)), ((), ()))
NN = (((1,), (0,)), ((), ()))


def dot(a, b, dims):
    return lax.dot_general(a, b, dims, preferred_element_type=jnp.float32)


def swap(block, axis, step):
    return lax.ppermute(block, axis, [(i, i ^ step) for i in range(lax.axis_size(axis))])


def attend_kernel(sizes, scalars, *refs):
    pieces, rows, keep, sends, n_pass = sizes
    refs = list(refs)
    q_ref, do_ref, ra_ref, rb_ref = refs[:4]
    pa_refs = refs[4 : 4 + pieces]
    pb_refs = refs[4 + pieces : 4 + 2 * pieces]
    rest = refs[4 + 2 * pieces + n_pass :]
    out_ref, dq_ref, dra_ref, drb_ref, keep_ref = rest[:5]
    send_refs = rest[5 : 5 + len(sends)]
    k_all, v_all, k_t, v_t, weights, probs, dscores, acc_k, acc_v, sum_k, sum_v = rest[5 + len(sends) :]

    r = pl.program_id(0)
    head = pl.program_id(1)
    n_resp = pl.num_programs(0)
    last = head == pl.num_programs(1) - 1
    prompt = scalars[r]
    even = scalars[n_resp] == 0
    n_prompt = pieces * rows
    n_query = q_ref.shape[1]
    n_blocks = n_query // BLOCK

    def gather(dst, piece_refs, resp_ref):
        for i, ref in enumerate(piece_refs):
            dst[i * rows : (i + 1) * rows, :] = ref[0]
        dst[n_prompt:, :] = resp_ref[0]

    @pl.when((head == 0) & even)
    def _():
        gather(k_all, pa_refs, ra_ref)
        gather(v_all, pb_refs, rb_ref)

    @pl.when((head == 0) & jnp.logical_not(even))
    def _():
        gather(k_all, pb_refs, rb_ref)
        gather(v_all, pa_refs, ra_ref)

    @pl.when(head == 0)
    def _():
        k_t[...] = k_all[...].T
        v_t[...] = v_all[...].T
        acc_k[...] = jnp.zeros_like(acc_k)
        acc_v[...] = jnp.zeros_like(acc_v)

    def fold(x, op):
        return op(x.reshape(-1, 8, x.shape[-1]), axis=0)

    def stages(i):
        st = {}
        t = slice(i * BLOCK, (i + 1) * BLOCK)
        seen = n_prompt + (i + 1) * BLOCK
        parts = [slice(u, u + CHUNK) for u in range(0, seen, CHUNK)]
        n_parts = len(parts)
        q = q_ref[0, t, :]
        do = do_ref[0, t, :]

        def score(c):
            s = dot(k_all[parts[c], :], q, NT)
            below = parts[c].start - (seen - BLOCK)
            if below >= 0:
                row = lax.broadcasted_iota(jnp.int32, (CHUNK, BLOCK), 0) + below
                col = lax.broadcasted_iota(jnp.int32, (CHUNK, BLOCK), 1)
                s = jnp.where(row <= col, s, MASKED)
            weights[parts[c], t] = s
            top = fold(s, jnp.max)
            st["top"] = top if c == 0 else jnp.maximum(st["top"], top)
            if c == n_parts - 1:
                st["top"] = jnp.max(st["top"], axis=0, keepdims=True) * SCALE

        def weigh(c):
            w = jnp.exp(weights[parts[c], t] * SCALE - st["top"])
            weights[parts[c], t] = w
            total = fold(w, jnp.sum)
            st["sum"] = total if c == 0 else st["sum"] + total
            if c == n_parts - 1:
                st["inv"] = 1.0 / jnp.sum(st["sum"], axis=0, keepdims=True)

        def norm(c):
            probs[parts[c], t] = (weights[parts[c], t] * st["inv"]).astype(jnp.bfloat16)
            if c == n_parts - 1:
                o = dot(v_t[:, :seen], probs[:seen, t], NN)
                out_ref[0, t, :] = o.T.astype(jnp.bfloat16)
                do_t = do.astype(jnp.float32).T
                st["delta"] = jnp.sum(o * do_t, axis=0, keepdims=True)
                st["inv"] = st["inv"] * SCALE

        def grad(c):
            dp = dot(v_all[parts[c], :], do, NT)
            ds = (weights[parts[c], t] * st["inv"]) * (dp - st["delta"])
            dscores[parts[c], t] = ds.astype(jnp.bfloat16)
            if c == n_parts - 1:
                dq = dot(k_t[:, :seen], dscores[:seen, t], NN)
                dq_ref[0, t, :] = dq.T.astype(jnp.bfloat16)

        return [[functools.partial(f, c) for c in range(n_parts)] for f in (score, weigh, norm, grad)]

    plan = [stages(i) for i in range(n_blocks)]
    for slot in range(4 + n_blocks - 1):
        groups = [plan[i][slot - i] for i in reversed(range(n_blocks)) if 0 <= slot - i < 4]
        for c in range(max(len(g) for g in groups)):
            for g in groups:
                if c < len(g):
                    g[c]()

    q_all = q_ref[0]
    do_all = do_ref[0]
    for u in range(0, n_prompt + n_query, BLOCK):
        t0 = max(u - n_prompt, 0)
        acc_v[u : u + BLOCK, :] += dot(probs[u : u + BLOCK, t0:], do_all[t0:], NN)
        acc_k[u : u + BLOCK, :] += dot(dscores[u : u + BLOCK, t0:], q_all[t0:], NN)

    def respond(ref, acc):
        ref[0] = acc[n_prompt:, :].astype(jnp.bfloat16)

    @pl.when(last & even)
    def _():
        respond(dra_ref, acc_k)
        respond(drb_ref, acc_v)

    @pl.when(last & jnp.logical_not(even))
    def _():
        respond(dra_ref, acc_v)
        respond(drb_ref, acc_k)

    @pl.when(last & (r == 0))
    def _():
        for whole, acc in ((sum_k, acc_k), (sum_v, acc_v)):
            whole[prompt] = acc[:n_prompt, :]
            whole[1 - prompt] = jnp.zeros((n_prompt, HD), jnp.float32)

    @pl.when(last & (r > 0))
    def _():
        for whole, acc in ((sum_k, acc_k), (sum_v, acc_v)):
            whole[prompt] += acc[:n_prompt, :]

    done = last & (r == n_resp - 1)

    def scatter(slot, whole):
        lanes = slice(slot * HD, (slot + 1) * HD)
        for ref, group in ((keep_ref, keep), *zip(send_refs, sends)):
            for at, i in enumerate(group):
                ref[at, :, :, lanes] = whole[:, i * rows : (i + 1) * rows, :].astype(ref.dtype)

    @pl.when(done & even)
    def _():
        scatter(0, sum_k)
        scatter(1, sum_v)

    @pl.when(done & jnp.logical_not(even))
    def _():
        scatter(0, sum_v)
        scatter(1, sum_k)


def attend(scalars, queries, d_out, resp_a, resp_b, prompt_a, prompt_b, keep, sends, chunk, heads, shared):
    n_resp, n_query, _ = queries.shape
    pieces = len(prompt_a)
    rows = prompt_a[0][0].shape[1]
    n_prompt = pieces * rows
    n_keys = n_prompt + n_query
    shape = jax.ShapeDtypeStruct

    def resp_map(column):
        return lambda r, j, sc: (r, 0, column(sc[n_resp]))

    def prompt_map(column):
        return lambda r, j, sc: (sc[r], 0, column(sc[n_resp]))

    q_spec = pl.BlockSpec((1, n_query, HD), lambda r, j, sc: (r, 0, chunk * heads + j))
    in_specs = [q_spec, q_spec]
    in_specs += [pl.BlockSpec((1, n_query, HD), resp_map(c)) for _, c in (resp_a, resp_b)]
    in_specs += [pl.BlockSpec((1, rows, HD), prompt_map(c)) for _, c in (*prompt_a, *prompt_b)]
    args = [queries, d_out, resp_a[0], resp_b[0], *[a for a, _ in (*prompt_a, *prompt_b)]]
    aliases = {}
    if shared is not None:
        aliases = {1 + len(args) + i: i for i in range(3)}
        args += list(shared)
    n_pass = len(args) - len(in_specs)
    in_specs += [pl.BlockSpec(memory_space=pl.ANY)] * n_pass
    grads = [shape((len(keep), P_SIZE, rows, 2 * HD), jnp.float32)]
    grads += [shape((len(g), P_SIZE, rows, 2 * HD), jnp.bfloat16) for g in sends]
    out_specs = [
        q_spec,
        q_spec,
        pl.BlockSpec((1, n_query, HD), resp_map(resp_a[1])),
        pl.BlockSpec((1, n_query, HD), lambda r, j, sc: (r, 0, 0)),
    ]
    out_specs += [pl.BlockSpec(g.shape, lambda r, j, sc: (0, 0, 0, 0)) for g in grads]
    out_shape = [
        shape(queries.shape, jnp.bfloat16),
        shape(queries.shape, jnp.bfloat16),
        shape(resp_a[0].shape, jnp.bfloat16),
        shape((n_resp, n_query, HD), jnp.bfloat16),
    ] + grads
    scratch = [
        pltpu.VMEM((n_keys, HD), jnp.bfloat16),
        pltpu.VMEM((n_keys, HD), jnp.bfloat16),
        pltpu.VMEM((HD, n_keys), jnp.bfloat16),
        pltpu.VMEM((HD, n_keys), jnp.bfloat16),
        pltpu.VMEM((n_keys, n_query), jnp.float32),
        pltpu.VMEM((n_keys, n_query), jnp.bfloat16),
        pltpu.VMEM((n_keys, n_query), jnp.bfloat16),
        pltpu.VMEM((n_keys, HD), jnp.float32),
        pltpu.VMEM((n_keys, HD), jnp.float32),
        pltpu.VMEM((P_SIZE, n_prompt, HD), jnp.float32),
        pltpu.VMEM((P_SIZE, n_prompt, HD), jnp.float32),
    ]
    flops = 12 * n_resp * heads * n_query * n_keys * HD
    return pl.pallas_call(
        functools.partial(attend_kernel, (pieces, rows, keep, sends, n_pass)),
        grid_spec=pltpu.PrefetchScalarGridSpec(
            num_scalar_prefetch=1,
            grid=(n_resp, heads),
            in_specs=in_specs,
            out_specs=out_specs,
            scratch_shapes=scratch,
        ),
        out_shape=out_shape,
        input_output_aliases=aliases,
        compiler_params=pltpu.CompilerParams(vmem_limit_bytes=48 * 2**20),
        cost_estimate=pl.CostEstimate(flops=2 * flops, bytes_accessed=4 * 2**20, transcendentals=0),
    )(scalars, *args)


def per_device(queries, resp_kv, prompt_kv, prompt_of, d_out):
    pair_heads = prompt_kv.shape[2] // HD
    parity = lax.axis_index("prefix") % 2
    scalars = jnp.concatenate([prompt_of, parity[None].astype(jnp.int32)])
    if lax.axis_size("dp") == 4 and pair_heads % 2 == 0:
        return whole_heads(queries, resp_kv, prompt_kv, scalars, parity, d_out)
    return shared_head(queries, resp_kv, prompt_kv, scalars, parity, d_out)


def whole_heads(queries, resp_kv, prompt_kv, scalars, parity, d_out):
    n_own = prompt_kv.shape[2] // HD // 2
    width = n_own * HD
    z = functools.partial(swap, axis="prefix", step=1)
    core, x, both = [functools.partial(swap, axis="dp", step=k) for k in (1, 2, 3)]
    own, theirs = parity * n_own, (1 - parity) * n_own

    def columns(array, which, count):
        return lax.dynamic_slice_in_dim(array, which * HD, count * HD, axis=2)

    def order(values, done):
        return lax.optimization_barrier((tuple(values), tuple(done)))[0]

    b0 = z(columns(prompt_kv, theirs, n_own))
    a0 = columns(prompt_kv, own, n_own)
    a2 = x(a0)
    resp_b = [z(columns(resp_kv, theirs, 1))]
    a0, b0 = order([a0, b0], [a2])
    b2 = x(b0)
    pa = [a0, core(a0), a2, core(a2)]
    pb = [b0, core(b0), b2, core(b2)]
    for h in range(1, n_own):
        (later,) = order([resp_kv], [resp_b[h - 1], b2])
        resp_b.append(z(columns(later, theirs + h, 1)))

    shared = None
    d_resp, d_prompt = [], []
    for h in range(n_own):
        final = h == n_own - 1
        here = lambda par, h=h: par * n_own + h
        at = lambda par, h=h: h
        att, dq, dra, drb, keep, *sends = attend(
            scalars,
            queries,
            d_out,
            (resp_kv, here),
            (resp_b[h], lambda par: 0),
            [(prompt_kv, here)] + [(a, at) for a in pa[1:]],
            [(b, at) for b in pb],
            (0, 2) if final else (0,),
            ((1, 3),) if final else ((1,), (2,), (3,)),
            h,
            GROUP,
            shared,
        )
        shared = (att, dq, dra)
        if final:
            (send, drb) = order([sends[0], drb], arrived)
            sums = keep + core(send).astype(jnp.float32)
            total = sums[0] + x(sums[1].astype(jnp.bfloat16)).astype(jnp.float32)
            d_resp.append(z(drb))
        else:
            parts = [move(part[0]) for move, part in zip((core, x, both), sends)]
            d_resp.append(z(drb))
            arrived = [*parts, d_resp[-1]]
            total = keep[0] + sum(p.astype(jnp.float32) for p in parts)
        other = z(total[:, :, HD:].astype(jnp.bfloat16))
        d_prompt.append((total[:, :, :HD], other.astype(jnp.float32)))

    even = parity == 0
    mine = jnp.concatenate([a for a, _ in d_prompt], axis=-1)
    other = jnp.concatenate([b for _, b in d_prompt], axis=-1)
    d_prompt = jnp.concatenate([jnp.where(even, mine, other), jnp.where(even, other, mine)], axis=-1)
    att, dq, d_resp_kv = shared
    received = jnp.concatenate(d_resp, axis=-1)
    d_resp_kv = lax.dynamic_update_slice_in_dim(d_resp_kv, received, theirs * HD, axis=2)
    return att, dq, d_resp_kv, d_prompt


def shared_head(queries, resp_kv, prompt_kv, scalars, parity, d_out):
    first = lambda par: 0
    prompt_a = lax.all_gather(prompt_kv, "dp", axis=1, tiled=True)
    prompt_b = swap(prompt_a, "prefix", 1)
    resp_b = swap(resp_kv, "prefix", 1)
    att, dq, dra, drb, keep = attend(
        scalars,
        queries,
        d_out,
        (resp_kv, first),
        (resp_b, first),
        [(prompt_a, first)],
        [(prompt_b, first)],
        (0,),
        (),
        0,
        queries.shape[2] // HD,
        None,
    )
    d_resp = (dra.astype(jnp.float32) + swap(drb, "prefix", 1).astype(jnp.float32)).astype(jnp.bfloat16)
    other = swap(keep[0, :, :, HD:].astype(jnp.bfloat16), "prefix", 1)
    paired = keep[0, :, :, :HD] + other.astype(jnp.float32)
    d_prompt = lax.psum_scatter(paired, "dp", scatter_dimension=1, tiled=True)
    return att, dq, d_resp, d_prompt


def solution(mesh):
    in_specs = (
        P(("groups", "dp"), None, "prefix"),
        P(("groups", "dp"), None, "prefix"),
        P("groups", "dp", "prefix"),
        P(("groups", "dp")),
        P(("groups", "dp"), None, "prefix"),
    )
    out_specs = (
        P(("groups", "dp"), None, "prefix"),
        P(("groups", "dp"), None, "prefix"),
        P(("groups", "dp"), None, "prefix"),
        P("groups", "dp", "prefix"),
    )
    return jax.shard_map(
        per_device, mesh=mesh, in_specs=in_specs, out_specs=out_specs, check_vma=False
    )
```

```python
import functools

import jax
import jax.numpy as jnp
from jax import lax
from jax.experimental import pallas as pl
from jax.experimental.pallas import tpu as pltpu
from jax.sharding import PartitionSpec as P

H = 32
KVH = 8
HD = 128
P_SIZE = 2
GROUP = H // KVH
BLOCK = 256
STRIP = 16
MASKED = -1e30
SCALE = HD ** (-0.5)

NT = (((1,), (1,)), ((), ()))
NN = (((1,), (0,)), ((), ()))
TN = (((0,), (0,)), ((), ()))


def dot(a, b, dims):
    return lax.dot_general(a, b, dims, preferred_element_type=jnp.float32)


def swap(block, axis, step):
    return lax.ppermute(block, axis, [(i, i ^ step) for i in range(lax.axis_size(axis))])


def attend_kernel(sizes, scalars, *refs):
    pieces, rows, keep, sends, n_pass = sizes
    refs = list(refs)
    q_ref, do_ref, ra_ref, rb_ref = refs[:4]
    pa_refs = refs[4 : 4 + pieces]
    pb_refs = refs[4 + pieces : 4 + 2 * pieces]
    rest = refs[4 + 2 * pieces + n_pass :]
    out_ref, dq_ref, dra_ref, drb_ref, keep_ref = rest[:5]
    send_refs = rest[5 : 5 + len(sends)]
    k_all, v_all, scores, grad_probs, probs, dscores, acc_k, acc_v, sum_k, sum_v = rest[5 + len(sends) :]

    r = pl.program_id(0)
    head = pl.program_id(1)
    n_resp = pl.num_programs(0)
    last = head == pl.num_programs(1) - 1
    prompt = scalars[r]
    even = scalars[n_resp] == 0
    n_prompt = pieces * rows
    n_query = q_ref.shape[1]
    n_blocks = n_query // BLOCK

    def gather(dst, piece_refs, resp_ref):
        for i, ref in enumerate(piece_refs):
            dst[i * rows : (i + 1) * rows, :] = ref[0]
        dst[n_prompt:, :] = resp_ref[0]

    @pl.when((head == 0) & even)
    def _():
        gather(k_all, pa_refs, ra_ref)
        gather(v_all, pb_refs, rb_ref)

    @pl.when((head == 0) & jnp.logical_not(even))
    def _():
        gather(k_all, pb_refs, rb_ref)
        gather(v_all, pa_refs, ra_ref)

    @pl.when(head == 0)
    def _():
        acc_k[...] = jnp.zeros_like(acc_k)
        acc_v[...] = jnp.zeros_like(acc_v)

    def stages(i):
        st = {}
        t0 = i * BLOCK
        t = slice(t0, t0 + BLOCK)
        seen = n_prompt + t0 + BLOCK
        edge = seen - BLOCK
        q = q_ref[0, t, :]
        do = do_ref[0, t, :]

        def score(u):
            scores[t, u : u + BLOCK] = dot(q, k_all[u : u + BLOCK, :], NT)

        def softmax(row):
            at = slice(t0 + row, t0 + row + STRIP)
            left = scores[at, :edge]
            rows_at = lax.broadcasted_iota(jnp.int32, (STRIP, BLOCK), 0) + row
            columns = lax.broadcasted_iota(jnp.int32, (STRIP, BLOCK), 1)
            right = jnp.where(columns <= rows_at, scores[at, edge:seen], MASKED)
            top = jnp.maximum(jnp.max(left, axis=1, keepdims=True), jnp.max(right, axis=1, keepdims=True)) * SCALE
            left = jnp.exp(left * SCALE - top)
            right = jnp.exp(right * SCALE - top)
            inv = 1.0 / (jnp.sum(left, axis=1, keepdims=True) + jnp.sum(right, axis=1, keepdims=True))
            for part, u in ((left * inv, slice(0, edge)), (right * inv, slice(edge, seen))):
                scores[at, u] = part
                probs[at, u] = part.astype(jnp.bfloat16)

        def grad_prob(u):
            grad_probs[t, u : u + BLOCK] = dot(do, v_all[u : u + BLOCK, :], NT)

        def output():
            o = dot(probs[t, :seen], v_all[:seen, :], NN)
            out_ref[0, t, :] = o.astype(jnp.bfloat16)
            st["delta"] = jnp.sum(o * do.astype(jnp.float32), axis=1, keepdims=True)

        def grad_score(row):
            at = slice(t0 + row, t0 + row + STRIP)
            delta = st["delta"][row : row + STRIP]
            ds = (scores[at, :seen] * SCALE) * (grad_probs[at, :seen] - delta)
            dscores[at, :seen] = ds.astype(jnp.bfloat16)

        def query():
            dq_ref[0, t, :] = dot(dscores[t, :seen], k_all[:seen, :], NN).astype(jnp.bfloat16)

        blocks = range(0, seen, BLOCK)
        strips = range(0, BLOCK, STRIP)
        each = lambda f, xs: [functools.partial(f, x) for x in xs]
        return [
            each(score, blocks),
            each(softmax, strips),
            each(grad_prob, blocks) + [output],
            each(grad_score, strips),
            [query],
        ]

    def mix(lists):
        steps = [((at + 0.5) / len(x), k, f) for k, x in enumerate(lists) for at, f in enumerate(x)]
        return [f for _, _, f in sorted(steps, key=lambda e: e[:2])]

    plan = [stages(i) for i in range(n_blocks)]
    depth = len(plan[0])
    for slot in range(depth + n_blocks - 1):
        for step in mix([plan[i][slot - i] for i in range(n_blocks) if 0 <= slot - i < depth]):
            step()

    q_all = q_ref[0]
    do_all = do_ref[0]
    for u in range(0, n_prompt + n_query, BLOCK):
        t0 = max(u - n_prompt, 0)
        acc_v[u : u + BLOCK, :] += dot(probs[t0:, u : u + BLOCK], do_all[t0:], TN)
        acc_k[u : u + BLOCK, :] += dot(dscores[t0:, u : u + BLOCK], q_all[t0:], TN)

    def respond(ref, acc):
        ref[0] = acc[n_prompt:, :].astype(jnp.bfloat16)

    @pl.when(last & even)
    def _():
        respond(dra_ref, acc_k)
        respond(drb_ref, acc_v)

    @pl.when(last & jnp.logical_not(even))
    def _():
        respond(dra_ref, acc_v)
        respond(drb_ref, acc_k)

    @pl.when(last & (r == 0))
    def _():
        for whole, acc in ((sum_k, acc_k), (sum_v, acc_v)):
            whole[prompt] = acc[:n_prompt, :]
            whole[1 - prompt] = jnp.zeros((n_prompt, HD), jnp.float32)

    @pl.when(last & (r > 0))
    def _():
        for whole, acc in ((sum_k, acc_k), (sum_v, acc_v)):
            whole[prompt] += acc[:n_prompt, :]

    done = last & (r == n_resp - 1)

    def scatter(slot, whole):
        lanes = slice(slot * HD, (slot + 1) * HD)
        for ref, group in ((keep_ref, keep), *zip(send_refs, sends)):
            for at, i in enumerate(group):
                ref[at, :, :, lanes] = whole[:, i * rows : (i + 1) * rows, :].astype(ref.dtype)

    @pl.when(done & even)
    def _():
        scatter(0, sum_k)
        scatter(1, sum_v)

    @pl.when(done & jnp.logical_not(even))
    def _():
        scatter(0, sum_v)
        scatter(1, sum_k)


def attend(scalars, queries, d_out, resp_a, resp_b, prompt_a, prompt_b, keep, sends, chunk, heads, shared):
    n_resp, n_query, _ = queries.shape
    pieces = len(prompt_a)
    rows = prompt_a[0][0].shape[1]
    n_prompt = pieces * rows
    n_keys = n_prompt + n_query
    shape = jax.ShapeDtypeStruct

    def resp_map(column):
        return lambda r, j, sc: (r, 0, column(sc[n_resp]))

    def prompt_map(column):
        return lambda r, j, sc: (sc[r], 0, column(sc[n_resp]))

    q_spec = pl.BlockSpec((1, n_query, HD), lambda r, j, sc: (r, 0, chunk * heads + j))
    in_specs = [q_spec, q_spec]
    in_specs += [pl.BlockSpec((1, n_query, HD), resp_map(c)) for _, c in (resp_a, resp_b)]
    in_specs += [pl.BlockSpec((1, rows, HD), prompt_map(c)) for _, c in (*prompt_a, *prompt_b)]
    args = [queries, d_out, resp_a[0], resp_b[0], *[a for a, _ in (*prompt_a, *prompt_b)]]
    aliases = {}
    if shared is not None:
        aliases = {1 + len(args) + i: i for i in range(3)}
        args += list(shared)
    n_pass = len(args) - len(in_specs)
    in_specs += [pl.BlockSpec(memory_space=pl.ANY)] * n_pass
    grads = [shape((len(keep), P_SIZE, rows, 2 * HD), jnp.float32)]
    grads += [shape((len(g), P_SIZE, rows, 2 * HD), jnp.bfloat16) for g in sends]
    out_specs = [
        q_spec,
        q_spec,
        pl.BlockSpec((1, n_query, HD), resp_map(resp_a[1])),
        pl.BlockSpec((1, n_query, HD), lambda r, j, sc: (r, 0, 0)),
    ]
    out_specs += [pl.BlockSpec(g.shape, lambda r, j, sc: (0, 0, 0, 0)) for g in grads]
    out_shape = [
        shape(queries.shape, jnp.bfloat16),
        shape(queries.shape, jnp.bfloat16),
        shape(resp_a[0].shape, jnp.bfloat16),
        shape((n_resp, n_query, HD), jnp.bfloat16),
    ] + grads
    scratch = [
        pltpu.VMEM((n_keys, HD), jnp.bfloat16),
        pltpu.VMEM((n_keys, HD), jnp.bfloat16),
        pltpu.VMEM((n_query, n_keys), jnp.float32),
        pltpu.VMEM((n_query, n_keys), jnp.float32),
        pltpu.VMEM((n_query, n_keys), jnp.bfloat16),
        pltpu.VMEM((n_query, n_keys), jnp.bfloat16),
        pltpu.VMEM((n_keys, HD), jnp.float32),
        pltpu.VMEM((n_keys, HD), jnp.float32),
        pltpu.VMEM((P_SIZE, n_prompt, HD), jnp.float32),
        pltpu.VMEM((P_SIZE, n_prompt, HD), jnp.float32),
    ]
    flops = 12 * n_resp * heads * n_query * n_keys * HD
    return pl.pallas_call(
        functools.partial(attend_kernel, (pieces, rows, keep, sends, n_pass)),
        grid_spec=pltpu.PrefetchScalarGridSpec(
            num_scalar_prefetch=1,
            grid=(n_resp, heads),
            in_specs=in_specs,
            out_specs=out_specs,
            scratch_shapes=scratch,
        ),
        out_shape=out_shape,
        input_output_aliases=aliases,
        compiler_params=pltpu.CompilerParams(vmem_limit_bytes=48 * 2**20),
        cost_estimate=pl.CostEstimate(flops=2 * flops, bytes_accessed=4 * 2**20, transcendentals=0),
    )(scalars, *args)


def per_device(queries, resp_kv, prompt_kv, prompt_of, d_out):
    pair_heads = prompt_kv.shape[2] // HD
    parity = lax.axis_index("prefix") % 2
    scalars = jnp.concatenate([prompt_of, parity[None].astype(jnp.int32)])
    if lax.axis_size("dp") == 4 and pair_heads % 2 == 0:
        return whole_heads(queries, resp_kv, prompt_kv, scalars, parity, d_out)
    return shared_head(queries, resp_kv, prompt_kv, scalars, parity, d_out)


def whole_heads(queries, resp_kv, prompt_kv, scalars, parity, d_out):
    n_own = prompt_kv.shape[2] // HD // 2
    width = n_own * HD
    z = functools.partial(swap, axis="prefix", step=1)
    core, x, both = [functools.partial(swap, axis="dp", step=k) for k in (1, 2, 3)]
    own, theirs = parity * n_own, (1 - parity) * n_own

    def columns(array, which, count):
        return lax.dynamic_slice_in_dim(array, which * HD, count * HD, axis=2)

    def order(values, done):
        return lax.optimization_barrier((tuple(values), tuple(done)))[0]

    b0 = z(columns(prompt_kv, theirs, n_own))
    a0 = columns(prompt_kv, own, n_own)
    a2 = x(a0)
    resp_b = [z(columns(resp_kv, theirs, 1))]
    a0, b0 = order([a0, b0], [a2])
    b2 = x(b0)
    pa = [a0, core(a0), a2, core(a2)]
    pb = [b0, core(b0), b2, core(b2)]
    for h in range(1, n_own):
        (later,) = order([resp_kv], [resp_b[h - 1], b2])
        resp_b.append(z(columns(later, theirs + h, 1)))

    shared = None
    d_resp, d_prompt = [], []
    for h in range(n_own):
        final = h == n_own - 1
        here = lambda par, h=h: par * n_own + h
        at = lambda par, h=h: h
        att, dq, dra, drb, keep, *sends = attend(
            scalars,
            queries,
            d_out,
            (resp_kv, here),
            (resp_b[h], lambda par: 0),
            [(prompt_kv, here)] + [(a, at) for a in pa[1:]],
            [(b, at) for b in pb],
            (0, 2) if final else (0,),
            ((1, 3),) if final else ((1,), (2,), (3,)),
            h,
            GROUP,
            shared,
        )
        shared = (att, dq, dra)
        if final:
            (send, drb) = order([sends[0], drb], arrived)
            sums = keep + core(send).astype(jnp.float32)
            total = sums[0] + x(sums[1].astype(jnp.bfloat16)).astype(jnp.float32)
            d_resp.append(z(drb))
        else:
            parts = [move(part[0]) for move, part in zip((core, x, both), sends)]
            d_resp.append(z(drb))
            arrived = [*parts, d_resp[-1]]
            total = keep[0] + sum(p.astype(jnp.float32) for p in parts)
        other = z(total[:, :, HD:].astype(jnp.bfloat16))
        d_prompt.append((total[:, :, :HD], other.astype(jnp.float32)))

    even = parity == 0
    mine = jnp.concatenate([a for a, _ in d_prompt], axis=-1)
    other = jnp.concatenate([b for _, b in d_prompt], axis=-1)
    d_prompt = jnp.concatenate([jnp.where(even, mine, other), jnp.where(even, other, mine)], axis=-1)
    att, dq, d_resp_kv = shared
    received = jnp.concatenate(d_resp, axis=-1)
    d_resp_kv = lax.dynamic_update_slice_in_dim(d_resp_kv, received, theirs * HD, axis=2)
    return att, dq, d_resp_kv, d_prompt


def shared_head(queries, resp_kv, prompt_kv, scalars, parity, d_out):
    first = lambda par: 0
    prompt_a = lax.all_gather(prompt_kv, "dp", axis=1, tiled=True)
    prompt_b = swap(prompt_a, "prefix", 1)
    resp_b = swap(resp_kv, "prefix", 1)
    att, dq, dra, drb, keep = attend(
        scalars,
        queries,
        d_out,
        (resp_kv, first),
        (resp_b, first),
        [(prompt_a, first)],
        [(prompt_b, first)],
        (0,),
        (),
        0,
        queries.shape[2] // HD,
        None,
    )
    d_resp = (dra.astype(jnp.float32) + swap(drb, "prefix", 1).astype(jnp.float32)).astype(jnp.bfloat16)
    other = swap(keep[0, :, :, HD:].astype(jnp.bfloat16), "prefix", 1)
    paired = keep[0, :, :, :HD] + other.astype(jnp.float32)
    d_prompt = lax.psum_scatter(paired, "dp", scatter_dimension=1, tiled=True)
    return att, dq, d_resp, d_prompt


def solution(mesh):
    in_specs = (
        P(("groups", "dp"), None, "prefix"),
        P(("groups", "dp"), None, "prefix"),
        P("groups", "dp", "prefix"),
        P(("groups", "dp")),
        P(("groups", "dp"), None, "prefix"),
    )
    out_specs = (
        P(("groups", "dp"), None, "prefix"),
        P(("groups", "dp"), None, "prefix"),
        P(("groups", "dp"), None, "prefix"),
        P("groups", "dp", "prefix"),
    )
    return jax.shard_map(
        per_device, mesh=mesh, in_specs=in_specs, out_specs=out_specs, check_vma=False
    )
```

```python
import functools

import jax
import jax.numpy as jnp
from jax import lax
from jax.experimental import pallas as pl
from jax.experimental.pallas import tpu as pltpu
from jax.sharding import PartitionSpec as P

H = 32
KVH = 8
HD = 128
P_SIZE = 2
GROUP = H // KVH
BLOCK = 256
STRIP = 16
MASKED = -1e30
SCALE = HD ** (-0.5)

NT = (((1,), (1,)), ((), ()))
NN = (((1,), (0,)), ((), ()))


def dot(a, b, dims):
    return lax.dot_general(a, b, dims, preferred_element_type=jnp.float32)


def swap(block, axis, step):
    return lax.ppermute(block, axis, [(i, i ^ step) for i in range(lax.axis_size(axis))])


def attend_kernel(sizes, scalars, *refs):
    pieces, rows, keep, sends, n_pass = sizes
    refs = list(refs)
    q_ref, do_ref, ra_ref, rb_ref = refs[:4]
    pa_refs = refs[4 : 4 + pieces]
    pb_refs = refs[4 + pieces : 4 + 2 * pieces]
    rest = refs[4 + 2 * pieces + n_pass :]
    out_ref, dq_ref, dra_ref, drb_ref, keep_ref = rest[:5]
    send_refs = rest[5 : 5 + len(sends)]
    k_all, v_all, q_t, do_t, scores, grad_probs, probs, dscores, acc_k, acc_v, sum_k, sum_v = rest[5 + len(sends) :]

    r = pl.program_id(0)
    head = pl.program_id(1)
    n_resp = pl.num_programs(0)
    last = head == pl.num_programs(1) - 1
    prompt = scalars[r]
    even = scalars[n_resp] == 0
    n_prompt = pieces * rows
    n_query = q_ref.shape[1]
    n_blocks = n_query // BLOCK

    def gather(dst, piece_refs, resp_ref):
        for i, ref in enumerate(piece_refs):
            dst[i * rows : (i + 1) * rows, :] = ref[0]
        dst[n_prompt:, :] = resp_ref[0]

    @pl.when((head == 0) & even)
    def _():
        gather(k_all, pa_refs, ra_ref)
        gather(v_all, pb_refs, rb_ref)

    @pl.when((head == 0) & jnp.logical_not(even))
    def _():
        gather(k_all, pb_refs, rb_ref)
        gather(v_all, pa_refs, ra_ref)

    @pl.when(head == 0)
    def _():
        acc_k[...] = jnp.zeros_like(acc_k)
        acc_v[...] = jnp.zeros_like(acc_v)

    def score(u):
        t = slice(max(u - n_prompt, 0), n_query)
        scores[t, u : u + BLOCK] = dot(q_ref[0, t, :], k_all[u : u + BLOCK, :], NT)

    def grad_prob(u):
        t = slice(max(u - n_prompt, 0), n_query)
        grad_probs[t, u : u + BLOCK] = dot(do_ref[0, t, :], v_all[u : u + BLOCK, :], NT)

    def grad_value(u):
        t = slice(max(u - n_prompt, 0), n_query)
        acc_v[:, u : u + BLOCK] += dot(do_t[:, t], probs[t, u : u + BLOCK], NN)

    def grad_key(u):
        t = slice(max(u - n_prompt, 0), n_query)
        acc_k[:, u : u + BLOCK] += dot(q_t[:, t], dscores[t, u : u + BLOCK], NN)

    def turn():
        q_t[...] = q_ref[0].T
        do_t[...] = do_ref[0].T

    def stages(i):
        st = {}
        t0 = i * BLOCK
        t = slice(t0, t0 + BLOCK)
        edge = n_prompt + t0
        seen = edge + BLOCK

        def softmax(row):
            at = slice(t0 + row, t0 + row + STRIP)
            left = scores[at, :edge]
            rows_at = lax.broadcasted_iota(jnp.int32, (STRIP, BLOCK), 0) + row
            columns = lax.broadcasted_iota(jnp.int32, (STRIP, BLOCK), 1)
            right = jnp.where(columns <= rows_at, scores[at, edge:seen], MASKED)
            top = jnp.maximum(jnp.max(left, axis=1, keepdims=True), jnp.max(right, axis=1, keepdims=True)) * SCALE
            left = jnp.exp(left * SCALE - top)
            right = jnp.exp(right * SCALE - top)
            inv = 1.0 / (jnp.sum(left, axis=1, keepdims=True) + jnp.sum(right, axis=1, keepdims=True))
            for part, u in ((left * inv, slice(0, edge)), (right * inv, slice(edge, seen))):
                scores[at, u] = part
                probs[at, u] = part.astype(jnp.bfloat16)

        def output():
            o = dot(probs[t, :seen], v_all[:seen, :], NN)
            out_ref[0, t, :] = o.astype(jnp.bfloat16)
            st["delta"] = jnp.sum(o * do_ref[0, t, :].astype(jnp.float32), axis=1, keepdims=True)

        def grad_score(row):
            at = slice(t0 + row, t0 + row + STRIP)
            delta = st["delta"][row : row + STRIP]
            ds = (scores[at, :seen] * SCALE) * (grad_probs[at, :seen] - delta)
            dscores[at, :seen] = ds.astype(jnp.bfloat16)

        def query():
            dq_ref[0, t, :] = dot(dscores[t, :seen], k_all[:seen, :], NN).astype(jnp.bfloat16)

        strips = range(0, BLOCK, STRIP)
        each = lambda f: [functools.partial(f, x) for x in strips]
        return {"softmax": each(softmax), "output": [output], "grad": each(grad_score), "query": [query]}

    def mix(*lists):
        order = [((at + 0.5) / len(x), k, f) for k, x in enumerate(lists) for at, f in enumerate(x)]
        for _, _, f in sorted(order, key=lambda e: e[:2]):
            f()

    plan = [stages(i) for i in range(n_blocks)]
    over = lambda f: [functools.partial(f, u) for u in range(0, n_prompt + n_query, BLOCK)]
    mix(over(score), [turn])
    mix(plan[0]["softmax"], over(grad_prob))
    for i in range(1, n_blocks):
        mix(plan[i]["softmax"], plan[i - 1]["output"])
        mix(plan[i - 1]["grad"], plan[i]["output"] if i == n_blocks - 1 else [])
    if n_blocks == 1:
        mix(plan[0]["output"])
    mix(plan[-1]["grad"], *[p["query"] for p in plan[:-1]], over(grad_value))
    mix(plan[-1]["query"], over(grad_key))

    def respond(ref, acc):
        ref[0] = acc[:, n_prompt:].T.astype(jnp.bfloat16)

    @pl.when(last & even)
    def _():
        respond(dra_ref, acc_k)
        respond(drb_ref, acc_v)

    @pl.when(last & jnp.logical_not(even))
    def _():
        respond(dra_ref, acc_v)
        respond(drb_ref, acc_k)

    @pl.when(last & (r == 0))
    def _():
        for whole, acc in ((sum_k, acc_k), (sum_v, acc_v)):
            whole[prompt] = acc[:, :n_prompt].T
            whole[1 - prompt] = jnp.zeros((n_prompt, HD), jnp.float32)

    @pl.when(last & (r > 0))
    def _():
        for whole, acc in ((sum_k, acc_k), (sum_v, acc_v)):
            whole[prompt] += acc[:, :n_prompt].T

    done = last & (r == n_resp - 1)

    def scatter(slot, whole):
        lanes = slice(slot * HD, (slot + 1) * HD)
        for ref, group in ((keep_ref, keep), *zip(send_refs, sends)):
            for at, i in enumerate(group):
                ref[at, :, :, lanes] = whole[:, i * rows : (i + 1) * rows, :].astype(ref.dtype)

    @pl.when(done & even)
    def _():
        scatter(0, sum_k)
        scatter(1, sum_v)

    @pl.when(done & jnp.logical_not(even))
    def _():
        scatter(0, sum_v)
        scatter(1, sum_k)


def attend(scalars, queries, d_out, resp_a, resp_b, prompt_a, prompt_b, keep, sends, chunk, heads, shared):
    n_resp, n_query, _ = queries.shape
    pieces = len(prompt_a)
    rows = prompt_a[0][0].shape[1]
    n_prompt = pieces * rows
    n_keys = n_prompt + n_query
    shape = jax.ShapeDtypeStruct

    def resp_map(column):
        return lambda r, j, sc: (r, 0, column(sc[n_resp]))

    def prompt_map(column):
        return lambda r, j, sc: (sc[r], 0, column(sc[n_resp]))

    q_spec = pl.BlockSpec((1, n_query, HD), lambda r, j, sc: (r, 0, chunk * heads + j))
    in_specs = [q_spec, q_spec]
    in_specs += [pl.BlockSpec((1, n_query, HD), resp_map(c)) for _, c in (resp_a, resp_b)]
    in_specs += [pl.BlockSpec((1, rows, HD), prompt_map(c)) for _, c in (*prompt_a, *prompt_b)]
    args = [queries, d_out, resp_a[0], resp_b[0], *[a for a, _ in (*prompt_a, *prompt_b)]]
    aliases = {}
    if shared is not None:
        aliases = {1 + len(args) + i: i for i in range(3)}
        args += list(shared)
    n_pass = len(args) - len(in_specs)
    in_specs += [pl.BlockSpec(memory_space=pl.ANY)] * n_pass
    grads = [shape((len(keep), P_SIZE, rows, 2 * HD), jnp.float32)]
    grads += [shape((len(g), P_SIZE, rows, 2 * HD), jnp.bfloat16) for g in sends]
    out_specs = [
        q_spec,
        q_spec,
        pl.BlockSpec((1, n_query, HD), resp_map(resp_a[1])),
        pl.BlockSpec((1, n_query, HD), lambda r, j, sc: (r, 0, 0)),
    ]
    out_specs += [pl.BlockSpec(g.shape, lambda r, j, sc: (0, 0, 0, 0)) for g in grads]
    out_shape = [
        shape(queries.shape, jnp.bfloat16),
        shape(queries.shape, jnp.bfloat16),
        shape(resp_a[0].shape, jnp.bfloat16),
        shape((n_resp, n_query, HD), jnp.bfloat16),
    ] + grads
    scratch = [
        pltpu.VMEM((n_keys, HD), jnp.bfloat16),
        pltpu.VMEM((n_keys, HD), jnp.bfloat16),
        pltpu.VMEM((HD, n_query), jnp.bfloat16),
        pltpu.VMEM((HD, n_query), jnp.bfloat16),
        pltpu.VMEM((n_query, n_keys), jnp.float32),
        pltpu.VMEM((n_query, n_keys), jnp.float32),
        pltpu.VMEM((n_query, n_keys), jnp.bfloat16),
        pltpu.VMEM((n_query, n_keys), jnp.bfloat16),
        pltpu.VMEM((HD, n_keys), jnp.float32),
        pltpu.VMEM((HD, n_keys), jnp.float32),
        pltpu.VMEM((P_SIZE, n_prompt, HD), jnp.float32),
        pltpu.VMEM((P_SIZE, n_prompt, HD), jnp.float32),
    ]
    flops = 12 * n_resp * heads * n_query * n_keys * HD
    return pl.pallas_call(
        functools.partial(attend_kernel, (pieces, rows, keep, sends, n_pass)),
        grid_spec=pltpu.PrefetchScalarGridSpec(
            num_scalar_prefetch=1,
            grid=(n_resp, heads),
            in_specs=in_specs,
            out_specs=out_specs,
            scratch_shapes=scratch,
        ),
        out_shape=out_shape,
        input_output_aliases=aliases,
        compiler_params=pltpu.CompilerParams(vmem_limit_bytes=48 * 2**20),
        cost_estimate=pl.CostEstimate(flops=2 * flops, bytes_accessed=4 * 2**20, transcendentals=0),
    )(scalars, *args)


def pack_kernel(n_own, n_resp, scalars, prompt_ref, resp_ref, *rest):
    outs, sems = rest[:-1], rest[-1]
    own = scalars[n_resp] * n_own
    theirs = (1 - scalars[n_resp]) * n_own
    copies = []
    for h in range(n_own):
        for ref, at in ((prompt_ref, own + h), (prompt_ref, theirs + h), (resp_ref, theirs + h)):
            lanes = pl.ds(pl.multiple_of(at * HD, HD), HD)
            k = len(copies)
            copies.append(pltpu.make_async_copy(ref.at[:, :, lanes], outs[k], sems.at[k]))
    for copy in copies:
        copy.start()
    for copy in copies:
        copy.wait()


def pack(scalars, prompt_kv, resp_kv, n_own):
    shape = lambda x: jax.ShapeDtypeStruct(x.shape[:2] + (HD,), x.dtype)
    anywhere = pl.BlockSpec(memory_space=pltpu.HBM)
    return pl.pallas_call(
        functools.partial(pack_kernel, n_own, resp_kv.shape[0]),
        grid_spec=pltpu.PrefetchScalarGridSpec(
            num_scalar_prefetch=1,
            grid=(1,),
            in_specs=[anywhere, anywhere],
            out_specs=[anywhere] * (3 * n_own),
            scratch_shapes=[pltpu.SemaphoreType.DMA((3 * n_own,))],
        ),
        out_shape=[shape(prompt_kv), shape(prompt_kv), shape(resp_kv)] * n_own,
        compiler_params=pltpu.CompilerParams(vmem_limit_bytes=60 * 2**20),
    )(scalars, prompt_kv, resp_kv)


def per_device(queries, resp_kv, prompt_kv, prompt_of, d_out):
    pair_heads = prompt_kv.shape[2] // HD
    parity = lax.axis_index("prefix") % 2
    scalars = jnp.concatenate([prompt_of, parity[None].astype(jnp.int32)])
    if lax.axis_size("dp") == 4 and pair_heads % 2 == 0:
        return whole_heads(queries, resp_kv, prompt_kv, scalars, parity, d_out)
    return shared_head(queries, resp_kv, prompt_kv, scalars, parity, d_out)


def whole_heads(queries, resp_kv, prompt_kv, scalars, parity, d_out):
    n_own = prompt_kv.shape[2] // HD // 2
    z = functools.partial(swap, axis="prefix", step=1)
    core, x, both = [functools.partial(swap, axis="dp", step=k) for k in (1, 2, 3)]
    theirs = (1 - parity) * n_own

    def order(values, done):
        return lax.optimization_barrier((tuple(values), tuple(done)))[0]

    packed = pack(scalars, prompt_kv, resp_kv, n_own)
    pa, pb, resp_b = [], [], []
    for h in range(n_own):
        a0, b0, rb = packed[3 * h : 3 * h + 3]
        if h > 0:
            (b0,) = order([b0], [pb[h - 1][0]])
            (a0,) = order([a0], [pb[h - 1][2]])
            (rb,) = order([rb], [resp_b[h - 1]])
        b0 = z(b0)
        a2 = x(a0)
        resp_b.append(z(rb))
        (ready,) = order([b0], [a2])
        b2 = x(ready)
        pa.append([a0, core(a0), a2, core(a2)])
        pb.append([b0, core(b0), b2, core(b2) if h == 0 else None])

    shared = None
    d_resp, d_prompt = [], []
    for h in range(n_own):
        final = h == n_own - 1
        here = lambda par, h=h: par * n_own + h
        at = lambda par: 0
        att, dq, dra, drb, keep, *sends = attend(
            scalars,
            queries,
            d_out,
            (resp_kv, here),
            (resp_b[h], at),
            [(prompt_kv, here)] + [(a, at) for a in pa[h][1:]],
            [(b, at) for b in pb[h]],
            (0, 2) if final else (0,),
            ((1, 3),) if final else ((1,), (2,), (3,)),
            h,
            GROUP,
            shared,
        )
        shared = (att, dq, dra)
        d_resp.append(z(drb))
        if not final:
            pb[h + 1][3] = core(order([pb[h + 1][2]], [drb])[0])
        if final:
            (send,) = order([sends[0]], arrived)
            sums = keep + core(send).astype(jnp.float32)
            (across,) = order([x(sums[1].astype(jnp.bfloat16))], [d_resp[-1], *[b for _, b in d_prompt]])
            total = sums[0] + across.astype(jnp.float32)
        else:
            parts = [move(part[0]) for move, part in zip((core, x, both), sends)]
            arrived = [*parts, d_resp[-1]]
            total = keep[0] + sum(p.astype(jnp.float32) for p in parts)
        other = z(total[:, :, HD:].astype(jnp.bfloat16))
        d_prompt.append((total[:, :, :HD], other))

    even = parity == 0
    mine = jnp.concatenate([a for a, _ in d_prompt], axis=-1)
    other = jnp.concatenate([b.astype(jnp.float32) for _, b in d_prompt], axis=-1)
    d_prompt = jnp.concatenate([jnp.where(even, mine, other), jnp.where(even, other, mine)], axis=-1)
    att, dq, d_resp_kv = shared
    received = jnp.concatenate(d_resp, axis=-1)
    d_resp_kv = lax.dynamic_update_slice_in_dim(d_resp_kv, received, theirs * HD, axis=2)
    return att, dq, d_resp_kv, d_prompt


def shared_head(queries, resp_kv, prompt_kv, scalars, parity, d_out):
    first = lambda par: 0
    prompt_a = lax.all_gather(prompt_kv, "dp", axis=1, tiled=True)
    prompt_b = swap(prompt_a, "prefix", 1)
    resp_b = swap(resp_kv, "prefix", 1)
    att, dq, dra, drb, keep = attend(
        scalars,
        queries,
        d_out,
        (resp_kv, first),
        (resp_b, first),
        [(prompt_a, first)],
        [(prompt_b, first)],
        (0,),
        (),
        0,
        queries.shape[2] // HD,
        None,
    )
    d_resp = (dra.astype(jnp.float32) + swap(drb, "prefix", 1).astype(jnp.float32)).astype(jnp.bfloat16)
    other = swap(keep[0, :, :, HD:].astype(jnp.bfloat16), "prefix", 1)
    paired = keep[0, :, :, :HD] + other.astype(jnp.float32)
    d_prompt = lax.psum_scatter(paired, "dp", scatter_dimension=1, tiled=True)
    return att, dq, d_resp, d_prompt


def solution(mesh):
    in_specs = (
        P(("groups", "dp"), None, "prefix"),
        P(("groups", "dp"), None, "prefix"),
        P("groups", "dp", "prefix"),
        P(("groups", "dp")),
        P(("groups", "dp"), None, "prefix"),
    )
    out_specs = (
        P(("groups", "dp"), None, "prefix"),
        P(("groups", "dp"), None, "prefix"),
        P(("groups", "dp"), None, "prefix"),
        P("groups", "dp", "prefix"),
    )
    return jax.shard_map(
        per_device, mesh=mesh, in_specs=in_specs, out_specs=out_specs, check_vma=False
    )
```

```python
import functools

import jax
import jax.numpy as jnp
from jax import lax
from jax.experimental import pallas as pl
from jax.experimental.pallas import tpu as pltpu
from jax.sharding import PartitionSpec as P

H = 32
KVH = 8
HD = 128
P_SIZE = 2
GROUP = H // KVH
BLOCK = 256
STRIP = 16
MASKED = -1e30
SCALE = HD ** (-0.5)

NT = (((1,), (1,)), ((), ()))
NN = (((1,), (0,)), ((), ()))


def dot(a, b, dims):
    return lax.dot_general(a, b, dims, preferred_element_type=jnp.float32)


def swap(block, axis, step):
    return lax.ppermute(block, axis, [(i, i ^ step) for i in range(lax.axis_size(axis))])


def attend_kernel(sizes, scalars, *refs):
    pieces, rows, keep, sends, n_pass = sizes
    refs = list(refs)
    q_ref, do_ref, ra_ref, rb_ref = refs[:4]
    pa_refs = refs[4 : 4 + pieces]
    pb_refs = refs[4 + pieces : 4 + 2 * pieces]
    rest = refs[4 + 2 * pieces + n_pass :]
    out_ref, dq_ref, dra_ref, drb_ref, keep_ref = rest[:5]
    send_refs = rest[5 : 5 + len(sends)]
    k_all, v_all, q_t, do_t, scores, grad_probs, probs, dscores, acc_k, acc_v, sum_k, sum_v = rest[5 + len(sends) :]

    r = pl.program_id(0)
    head = pl.program_id(1)
    n_resp = pl.num_programs(0)
    last = head == pl.num_programs(1) - 1
    prompt = scalars[r]
    even = scalars[n_resp] == 0
    n_prompt = pieces * rows
    n_query = q_ref.shape[1]
    n_blocks = n_query // BLOCK

    def gather(dst, piece_refs, resp_ref):
        for i, ref in enumerate(piece_refs):
            dst[i * rows : (i + 1) * rows, :] = ref[0]
        dst[n_prompt:, :] = resp_ref[0]

    @pl.when((head == 0) & even)
    def _():
        gather(k_all, pa_refs, ra_ref)
        gather(v_all, pb_refs, rb_ref)

    @pl.when((head == 0) & jnp.logical_not(even))
    def _():
        gather(k_all, pb_refs, rb_ref)
        gather(v_all, pa_refs, ra_ref)

    @pl.when(head == 0)
    def _():
        acc_k[...] = jnp.zeros_like(acc_k)
        acc_v[...] = jnp.zeros_like(acc_v)

    def score(u):
        t = slice(max(u - n_prompt, 0), n_query)
        scores[t, u : u + BLOCK] = dot(q_ref[0, t, :], k_all[u : u + BLOCK, :], NT)

    def grad_prob(u):
        t = slice(max(u - n_prompt, 0), n_query)
        grad_probs[t, u : u + BLOCK] = dot(do_ref[0, t, :], v_all[u : u + BLOCK, :], NT)

    def grad_value(u):
        t = slice(max(u - n_prompt, 0), n_query)
        acc_v[:, u : u + BLOCK] += dot(do_t[:, t], probs[t, u : u + BLOCK], NN)

    def grad_key(u):
        t = slice(max(u - n_prompt, 0), n_query)
        acc_k[:, u : u + BLOCK] += dot(q_t[:, t], dscores[t, u : u + BLOCK], NN)

    def turn():
        q_t[...] = q_ref[0].T
        do_t[...] = do_ref[0].T

    def stages(i):
        st = {}
        t0 = i * BLOCK
        t = slice(t0, t0 + BLOCK)
        edge = n_prompt + t0
        seen = edge + BLOCK

        def softmax(row):
            at = slice(t0 + row, t0 + row + STRIP)
            left = scores[at, :edge]
            rows_at = lax.broadcasted_iota(jnp.int32, (STRIP, BLOCK), 0) + row
            columns = lax.broadcasted_iota(jnp.int32, (STRIP, BLOCK), 1)
            right = jnp.where(columns <= rows_at, scores[at, edge:seen], MASKED)
            top = jnp.maximum(jnp.max(left, axis=1, keepdims=True), jnp.max(right, axis=1, keepdims=True)) * SCALE
            left = jnp.exp(left * SCALE - top)
            right = jnp.exp(right * SCALE - top)
            inv = 1.0 / (jnp.sum(left, axis=1, keepdims=True) + jnp.sum(right, axis=1, keepdims=True))
            for part, u in ((left * inv, slice(0, edge)), (right * inv, slice(edge, seen))):
                scores[at, u] = part
                probs[at, u] = part.astype(jnp.bfloat16)

        def output():
            o = dot(probs[t, :seen], v_all[:seen, :], NN)
            out_ref[0, t, :] = o.astype(jnp.bfloat16)
            st["delta"] = jnp.sum(o * do_ref[0, t, :].astype(jnp.float32), axis=1, keepdims=True)

        def grad_score(row):
            at = slice(t0 + row, t0 + row + STRIP)
            delta = st["delta"][row : row + STRIP]
            ds = (scores[at, :seen] * SCALE) * (grad_probs[at, :seen] - delta)
            dscores[at, :seen] = ds.astype(jnp.bfloat16)

        def query():
            dq_ref[0, t, :] = dot(dscores[t, :seen], k_all[:seen, :], NN).astype(jnp.bfloat16)

        strips = range(0, BLOCK, STRIP)
        each = lambda f: [functools.partial(f, x) for x in strips]
        return {"softmax": each(softmax), "output": [output], "grad": each(grad_score), "query": [query]}

    def mix(*lists):
        order = [((at + 0.5) / len(x), k, f) for k, x in enumerate(lists) for at, f in enumerate(x)]
        for _, _, f in sorted(order, key=lambda e: e[:2]):
            f()

    plan = [stages(i) for i in range(n_blocks)]
    over = lambda f: [functools.partial(f, u) for u in range(0, n_prompt + n_query, BLOCK)]
    mix(over(score), [turn])
    mix(plan[0]["softmax"], over(grad_prob))
    for i in range(1, n_blocks):
        mix(plan[i]["softmax"], plan[i - 1]["output"])
        mix(plan[i - 1]["grad"], plan[i]["output"] if i == n_blocks - 1 else [])
    if n_blocks == 1:
        mix(plan[0]["output"])
    mix(plan[-1]["grad"], *[p["query"] for p in plan[:-1]], over(grad_value))
    mix(plan[-1]["query"], over(grad_key))

    def respond(ref, acc):
        ref[0] = acc[:, n_prompt:].T.astype(jnp.bfloat16)

    @pl.when(last & even)
    def _():
        respond(dra_ref, acc_k)
        respond(drb_ref, acc_v)

    @pl.when(last & jnp.logical_not(even))
    def _():
        respond(dra_ref, acc_v)
        respond(drb_ref, acc_k)

    @pl.when(last & (r == 0))
    def _():
        for whole, acc in ((sum_k, acc_k), (sum_v, acc_v)):
            whole[prompt] = acc[:, :n_prompt].T
            whole[1 - prompt] = jnp.zeros((n_prompt, HD), jnp.float32)

    @pl.when(last & (r > 0))
    def _():
        for whole, acc in ((sum_k, acc_k), (sum_v, acc_v)):
            whole[prompt] += acc[:, :n_prompt].T

    done = last & (r == n_resp - 1)

    def scatter(slot, whole):
        lanes = slice(slot * HD, (slot + 1) * HD)
        for ref, group in ((keep_ref, keep), *zip(send_refs, sends)):
            for at, i in enumerate(group):
                ref[at, :, :, lanes] = whole[:, i * rows : (i + 1) * rows, :].astype(ref.dtype)

    @pl.when(done & even)
    def _():
        scatter(0, sum_k)
        scatter(1, sum_v)

    @pl.when(done & jnp.logical_not(even))
    def _():
        scatter(0, sum_v)
        scatter(1, sum_k)


def attend(scalars, queries, d_out, resp_a, resp_b, prompt_a, prompt_b, keep, sends, chunk, heads, shared, own):
    n_resp, n_query, _ = queries.shape
    pieces = len(prompt_a)
    rows = prompt_a[0][0].shape[1]
    n_prompt = pieces * rows
    n_keys = n_prompt + n_query
    shape = jax.ShapeDtypeStruct

    def resp_map(column):
        return lambda r, j, sc: (r, 0, column(sc[n_resp]))

    def prompt_map(column):
        return lambda r, j, sc: (sc[r], 0, column(sc[n_resp]))

    q_spec = pl.BlockSpec((1, n_query, HD), lambda r, j, sc: (r, 0, chunk * heads + j))
    in_specs = [q_spec, q_spec]
    in_specs += [pl.BlockSpec((1, n_query, HD), resp_map(c)) for _, c in (resp_a, resp_b)]
    in_specs += [pl.BlockSpec((1, rows, HD), prompt_map(c)) for _, c in (*prompt_a, *prompt_b)]
    args = [queries, d_out, resp_a[0], resp_b[0], *[a for a, _ in (*prompt_a, *prompt_b)]]
    aliases = {}
    if shared is not None:
        aliases = {1 + len(args) + i: i for i in range(3)}
        args += list(shared)
    n_pass = len(args) - len(in_specs)
    in_specs += [pl.BlockSpec(memory_space=pl.ANY)] * n_pass
    grads = [shape((len(keep), P_SIZE, rows, 2 * HD), jnp.float32)]
    grads += [shape((len(g), P_SIZE, rows, 2 * HD), jnp.bfloat16) for g in sends]
    out_specs = [
        q_spec,
        q_spec,
        pl.BlockSpec((1, n_query, HD), resp_map(own[1])),
        pl.BlockSpec((1, n_query, HD), lambda r, j, sc: (r, 0, 0)),
    ]
    out_specs += [pl.BlockSpec(g.shape, lambda r, j, sc: (0, 0, 0, 0)) for g in grads]
    out_shape = [
        shape(queries.shape, jnp.bfloat16),
        shape(queries.shape, jnp.bfloat16),
        shape(own[0].shape, jnp.bfloat16),
        shape((n_resp, n_query, HD), jnp.bfloat16),
    ] + grads
    scratch = [
        pltpu.VMEM((n_keys, HD), jnp.bfloat16),
        pltpu.VMEM((n_keys, HD), jnp.bfloat16),
        pltpu.VMEM((HD, n_query), jnp.bfloat16),
        pltpu.VMEM((HD, n_query), jnp.bfloat16),
        pltpu.VMEM((n_query, n_keys), jnp.float32),
        pltpu.VMEM((n_query, n_keys), jnp.float32),
        pltpu.VMEM((n_query, n_keys), jnp.bfloat16),
        pltpu.VMEM((n_query, n_keys), jnp.bfloat16),
        pltpu.VMEM((HD, n_keys), jnp.float32),
        pltpu.VMEM((HD, n_keys), jnp.float32),
        pltpu.VMEM((P_SIZE, n_prompt, HD), jnp.float32),
        pltpu.VMEM((P_SIZE, n_prompt, HD), jnp.float32),
    ]
    flops = 12 * n_resp * heads * n_query * n_keys * HD
    return pl.pallas_call(
        functools.partial(attend_kernel, (pieces, rows, keep, sends, n_pass)),
        grid_spec=pltpu.PrefetchScalarGridSpec(
            num_scalar_prefetch=1,
            grid=(n_resp, heads),
            in_specs=in_specs,
            out_specs=out_specs,
            scratch_shapes=scratch,
        ),
        out_shape=out_shape,
        input_output_aliases=aliases,
        compiler_params=pltpu.CompilerParams(vmem_limit_bytes=48 * 2**20),
        cost_estimate=pl.CostEstimate(flops=2 * flops, bytes_accessed=4 * 2**20, transcendentals=0),
    )(scalars, *args)


def pack_kernel(n_own, n_resp, scalars, prompt_ref, resp_ref, *outs):
    width = n_own * HD

    def split(own):
        for h in range(n_own):
            mine = slice(own + h * HD, own + (h + 1) * HD)
            theirs = slice(width - own + h * HD, width - own + (h + 1) * HD)
            for k, (ref, lanes) in enumerate(
                ((prompt_ref, mine), (prompt_ref, theirs), (resp_ref, mine), (resp_ref, theirs))
            ):
                outs[4 * h + k][...] = ref[:, :, lanes]

    @pl.when(scalars[n_resp] == 0)
    def _():
        split(0)

    @pl.when(scalars[n_resp] != 0)
    def _():
        split(width)


def pack(scalars, prompt_kv, resp_kv, n_own):
    block = lambda shape: pl.BlockSpec(shape, lambda i, sc: (0, 0, 0))
    shapes = [x.shape[:2] + (HD,) for x in (prompt_kv, prompt_kv, resp_kv, resp_kv)] * n_own
    return pl.pallas_call(
        functools.partial(pack_kernel, n_own, resp_kv.shape[0]),
        grid_spec=pltpu.PrefetchScalarGridSpec(
            num_scalar_prefetch=1,
            grid=(1,),
            in_specs=[block(prompt_kv.shape), block(resp_kv.shape)],
            out_specs=[block(s) for s in shapes],
        ),
        out_shape=[jax.ShapeDtypeStruct(s, prompt_kv.dtype) for s in shapes],
        compiler_params=pltpu.CompilerParams(vmem_limit_bytes=48 * 2**20),
    )(scalars, prompt_kv, resp_kv)


def per_device(queries, resp_kv, prompt_kv, prompt_of, d_out):
    pair_heads = prompt_kv.shape[2] // HD
    parity = lax.axis_index("prefix") % 2
    scalars = jnp.concatenate([prompt_of, parity[None].astype(jnp.int32)])
    if lax.axis_size("dp") == 4 and pair_heads % 2 == 0:
        return whole_heads(queries, resp_kv, prompt_kv, scalars, parity, d_out)
    return shared_head(queries, resp_kv, prompt_kv, scalars, parity, d_out)


def whole_heads(queries, resp_kv, prompt_kv, scalars, parity, d_out):
    n_own = prompt_kv.shape[2] // HD // 2
    z = functools.partial(swap, axis="prefix", step=1)
    core, x, both = [functools.partial(swap, axis="dp", step=k) for k in (1, 2, 3)]
    theirs = (1 - parity) * n_own

    def order(values, done):
        return lax.optimization_barrier((tuple(values), tuple(done)))[0]

    packed = pack(scalars, prompt_kv, resp_kv, n_own)
    pa, pb, resp_a, resp_b = [], [], [], []
    for h in range(n_own):
        a0, b0, ra, rb = packed[4 * h : 4 * h + 4]
        if h > 0:
            (rb,) = order([rb], [resp_b[h - 1]])
        b0 = z(b0)
        a2 = x(a0)
        resp_a.append(ra)
        resp_b.append(z(rb))
        if h == 0:
            (ready,) = order([b0], [a2])
        else:
            (ready,) = order([b0], [pb[0][2]])
        b2 = x(ready)
        pa.append([a0, core(a0), a2, core(a2) if h == 0 else None])
        pb.append([b0, core(b0), b2, core(b2) if h == 0 else None])

    shared = None
    d_resp, d_prompt = [], []
    for h in range(n_own):
        final = h == n_own - 1
        here = lambda par, h=h: par * n_own + h
        at = lambda par: 0
        att, dq, dra, drb, keep, *sends = attend(
            scalars,
            queries,
            d_out,
            (resp_a[h], at),
            (resp_b[h], at),
            [(a, at) for a in pa[h]],
            [(b, at) for b in pb[h]],
            (0, 2) if final else (0,),
            ((1, 3),) if final else ((1,), (2,), (3,)),
            h,
            GROUP,
            shared,
            (resp_kv, here),
        )
        shared = (att, dq, dra)
        d_resp.append(z(drb))
        if not final:
            pa[h + 1][3], pb[h + 1][3] = [core(v) for v in order([pa[h + 1][2], pb[h + 1][2]], [drb])]
        if final:
            (send,) = order([sends[0]], arrived)
            sums = keep + core(send).astype(jnp.float32)
            (across,) = order([x(sums[1].astype(jnp.bfloat16))], [d_resp[-1], *[b for _, b in d_prompt]])
            total = sums[0] + across.astype(jnp.float32)
        else:
            parts = [move(part[0]) for move, part in zip((core, x, both), sends)]
            arrived = [*parts, d_resp[-1]]
            total = keep[0] + sum(p.astype(jnp.float32) for p in parts)
        other = z(total[:, :, HD:].astype(jnp.bfloat16))
        d_prompt.append((total[:, :, :HD], other))

    even = parity == 0
    mine = jnp.concatenate([a for a, _ in d_prompt], axis=-1)
    other = jnp.concatenate([b.astype(jnp.float32) for _, b in d_prompt], axis=-1)
    d_prompt = jnp.concatenate([jnp.where(even, mine, other), jnp.where(even, other, mine)], axis=-1)
    att, dq, d_resp_kv = shared
    received = jnp.concatenate(d_resp, axis=-1)
    d_resp_kv = lax.dynamic_update_slice_in_dim(d_resp_kv, received, theirs * HD, axis=2)
    return att, dq, d_resp_kv, d_prompt


def shared_head(queries, resp_kv, prompt_kv, scalars, parity, d_out):
    first = lambda par: 0
    prompt_a = lax.all_gather(prompt_kv, "dp", axis=1, tiled=True)
    prompt_b = swap(prompt_a, "prefix", 1)
    resp_b = swap(resp_kv, "prefix", 1)
    att, dq, dra, drb, keep = attend(
        scalars,
        queries,
        d_out,
        (resp_kv, first),
        (resp_b, first),
        [(prompt_a, first)],
        [(prompt_b, first)],
        (0,),
        (),
        0,
        queries.shape[2] // HD,
        None,
        (resp_kv, first),
    )
    d_resp = (dra.astype(jnp.float32) + swap(drb, "prefix", 1).astype(jnp.float32)).astype(jnp.bfloat16)
    other = swap(keep[0, :, :, HD:].astype(jnp.bfloat16), "prefix", 1)
    paired = keep[0, :, :, :HD] + other.astype(jnp.float32)
    d_prompt = lax.psum_scatter(paired, "dp", scatter_dimension=1, tiled=True)
    return att, dq, d_resp, d_prompt


def solution(mesh):
    in_specs = (
        P(("groups", "dp"), None, "prefix"),
        P(("groups", "dp"), None, "prefix"),
        P("groups", "dp", "prefix"),
        P(("groups", "dp")),
        P(("groups", "dp"), None, "prefix"),
    )
    out_specs = (
        P(("groups", "dp"), None, "prefix"),
        P(("groups", "dp"), None, "prefix"),
        P(("groups", "dp"), None, "prefix"),
        P("groups", "dp", "prefix"),
    )
    return jax.shard_map(
        per_device, mesh=mesh, in_specs=in_specs, out_specs=out_specs, check_vma=False
    )
```

```python
import functools

import jax
import jax.numpy as jnp
from jax import lax
from jax.experimental import pallas as pl
from jax.experimental.pallas import tpu as pltpu
from jax.sharding import PartitionSpec as P

H = 32
KVH = 8
HD = 128
P_SIZE = 2
GROUP = H // KVH
BLOCK = 256
STRIP = 16
MASKED = -1e30
ATTEND_VMEM = 50 * 2**20
PACK_VMEM = 60 * 2**20
SCALE = HD ** (-0.5)

NT = (((1,), (1,)), ((), ()))
NN = (((1,), (0,)), ((), ()))


def dot(a, b, dims):
    return lax.dot_general(a, b, dims, preferred_element_type=jnp.float32)


def swap(block, axis, step):
    return lax.ppermute(block, axis, [(i, i ^ step) for i in range(lax.axis_size(axis))])


def attend_kernel(sizes, scalars, *refs):
    pieces, rows, keep, sends, n_pass = sizes
    refs = list(refs)
    q_ref, do_ref, ra_ref, rb_ref = refs[:4]
    pa_refs = refs[4 : 4 + pieces]
    pb_refs = refs[4 + pieces : 4 + 2 * pieces]
    rest = refs[4 + 2 * pieces + n_pass :]
    out_ref, dq_ref, dra_ref, drb_ref, keep_ref = rest[:5]
    send_refs = rest[5 : 5 + len(sends)]
    k_all, v_all, q_t, do_t, scores, grad_probs, probs, dscores, acc_k, acc_v, sum_k, sum_v = rest[5 + len(sends) :]

    r = pl.program_id(0)
    head = pl.program_id(1)
    n_resp = pl.num_programs(0)
    last = head == pl.num_programs(1) - 1
    prompt = scalars[r]
    even = scalars[n_resp] == 0
    n_prompt = pieces * rows
    n_query = q_ref.shape[1]
    n_blocks = n_query // BLOCK

    def gather(dst, piece_refs, resp_ref):
        for i, ref in enumerate(piece_refs):
            dst[i * rows : (i + 1) * rows, :] = ref[0]
        dst[n_prompt:, :] = resp_ref[0]

    @pl.when((head == 0) & even)
    def _():
        gather(k_all, pa_refs, ra_ref)
        gather(v_all, pb_refs, rb_ref)

    @pl.when((head == 0) & jnp.logical_not(even))
    def _():
        gather(k_all, pb_refs, rb_ref)
        gather(v_all, pa_refs, ra_ref)

    @pl.when(head == 0)
    def _():
        acc_k[...] = jnp.zeros_like(acc_k)
        acc_v[...] = jnp.zeros_like(acc_v)

    def score(u):
        t = slice(max(u - n_prompt, 0), n_query)
        scores[t, u : u + BLOCK] = dot(q_ref[0, t, :], k_all[u : u + BLOCK, :], NT)

    def grad_prob(u):
        t = slice(max(u - n_prompt, 0), n_query)
        grad_probs[t, u : u + BLOCK] = dot(do_ref[0, t, :], v_all[u : u + BLOCK, :], NT)

    def grad_value(u):
        t = slice(max(u - n_prompt, 0), n_query)
        acc_v[:, u : u + BLOCK] += dot(do_t[:, t], probs[t, u : u + BLOCK], NN)

    def grad_key(u):
        t = slice(max(u - n_prompt, 0), n_query)
        acc_k[:, u : u + BLOCK] += dot(q_t[:, t], dscores[t, u : u + BLOCK], NN)

    def turn():
        q_t[...] = q_ref[0].T
        do_t[...] = do_ref[0].T

    def stages(i):
        st = {}
        t0 = i * BLOCK
        t = slice(t0, t0 + BLOCK)
        edge = n_prompt + t0
        seen = edge + BLOCK

        def softmax(row):
            at = slice(t0 + row, t0 + row + STRIP)
            left = scores[at, :edge]
            rows_at = lax.broadcasted_iota(jnp.int32, (STRIP, BLOCK), 0) + row
            columns = lax.broadcasted_iota(jnp.int32, (STRIP, BLOCK), 1)
            right = jnp.where(columns <= rows_at, scores[at, edge:seen], MASKED)
            top = jnp.maximum(jnp.max(left, axis=1, keepdims=True), jnp.max(right, axis=1, keepdims=True)) * SCALE
            left = jnp.exp(left * SCALE - top)
            right = jnp.exp(right * SCALE - top)
            inv = 1.0 / (jnp.sum(left, axis=1, keepdims=True) + jnp.sum(right, axis=1, keepdims=True))
            for part, u in ((left * inv, slice(0, edge)), (right * inv, slice(edge, seen))):
                scores[at, u] = part
                probs[at, u] = part.astype(jnp.bfloat16)

        def output():
            o = dot(probs[t, :seen], v_all[:seen, :], NN)
            out_ref[0, t, :] = o.astype(jnp.bfloat16)
            st["delta"] = jnp.sum(o * do_ref[0, t, :].astype(jnp.float32), axis=1, keepdims=True)

        def grad_score(row):
            at = slice(t0 + row, t0 + row + STRIP)
            delta = st["delta"][row : row + STRIP]
            ds = (scores[at, :seen] * SCALE) * (grad_probs[at, :seen] - delta)
            dscores[at, :seen] = ds.astype(jnp.bfloat16)

        def query():
            dq_ref[0, t, :] = dot(dscores[t, :seen], k_all[:seen, :], NN).astype(jnp.bfloat16)

        strips = range(0, BLOCK, STRIP)
        each = lambda f: [functools.partial(f, x) for x in strips]
        return {"softmax": each(softmax), "output": [output], "grad": each(grad_score), "query": [query]}

    def mix(*lists):
        order = [((at + 0.5) / len(x), k, f) for k, x in enumerate(lists) for at, f in enumerate(x)]
        for _, _, f in sorted(order, key=lambda e: e[:2]):
            f()

    plan = [stages(i) for i in range(n_blocks)]
    over = lambda f: [functools.partial(f, u) for u in range(0, n_prompt + n_query, BLOCK)]
    mix(over(score), [turn])
    mix(plan[0]["softmax"], over(grad_prob))
    for i in range(1, n_blocks):
        mix(plan[i]["softmax"], plan[i - 1]["output"])
        mix(plan[i - 1]["grad"], plan[i]["output"] if i == n_blocks - 1 else [])
    if n_blocks == 1:
        mix(plan[0]["output"])
    mix(plan[-1]["grad"], *[p["query"] for p in plan[:-1]], over(grad_value))
    mix(plan[-1]["query"], over(grad_key))

    def respond(ref, acc):
        ref[0] = acc[:, n_prompt:].T.astype(jnp.bfloat16)

    @pl.when(last & even)
    def _():
        respond(dra_ref, acc_k)
        respond(drb_ref, acc_v)

    @pl.when(last & jnp.logical_not(even))
    def _():
        respond(dra_ref, acc_v)
        respond(drb_ref, acc_k)

    @pl.when(last & (r == 0))
    def _():
        for whole, acc in ((sum_k, acc_k), (sum_v, acc_v)):
            whole[prompt] = acc[:, :n_prompt].T
            whole[1 - prompt] = jnp.zeros((n_prompt, HD), jnp.float32)

    @pl.when(last & (r > 0))
    def _():
        for whole, acc in ((sum_k, acc_k), (sum_v, acc_v)):
            whole[prompt] += acc[:, :n_prompt].T

    done = last & (r == n_resp - 1)

    def scatter(slot, whole):
        lanes = slice(slot * HD, (slot + 1) * HD)
        for ref, group in ((keep_ref, keep), *zip(send_refs, sends)):
            for at, i in enumerate(group):
                ref[at, :, :, lanes] = whole[:, i * rows : (i + 1) * rows, :].astype(ref.dtype)

    @pl.when(done & even)
    def _():
        scatter(0, sum_k)
        scatter(1, sum_v)

    @pl.when(done & jnp.logical_not(even))
    def _():
        scatter(0, sum_v)
        scatter(1, sum_k)


def attend(scalars, queries, d_out, resp_a, resp_b, prompt_a, prompt_b, keep, sends, chunk, heads, shared, own):
    n_resp, n_query, _ = queries.shape
    pieces = len(prompt_a)
    rows = prompt_a[0][0].shape[1]
    n_prompt = pieces * rows
    n_keys = n_prompt + n_query
    shape = jax.ShapeDtypeStruct

    def resp_map(column):
        return lambda r, j, sc: (r, 0, column(sc[n_resp]))

    def prompt_map(column):
        return lambda r, j, sc: (sc[r], 0, column(sc[n_resp]))

    q_spec = pl.BlockSpec((1, n_query, HD), lambda r, j, sc: (r, 0, chunk * heads + j))
    in_specs = [q_spec, q_spec]
    in_specs += [pl.BlockSpec((1, n_query, HD), resp_map(c)) for _, c in (resp_a, resp_b)]
    in_specs += [pl.BlockSpec((1, rows, HD), prompt_map(c)) for _, c in (*prompt_a, *prompt_b)]
    args = [queries, d_out, resp_a[0], resp_b[0], *[a for a, _ in (*prompt_a, *prompt_b)]]
    aliases = {}
    if shared is not None:
        aliases = {1 + len(args) + i: i for i in range(3)}
        args += list(shared)
    n_pass = len(args) - len(in_specs)
    in_specs += [pl.BlockSpec(memory_space=pl.ANY)] * n_pass
    grads = [shape((len(keep), P_SIZE, rows, 2 * HD), jnp.float32)]
    grads += [shape((len(g), P_SIZE, rows, 2 * HD), jnp.bfloat16) for g in sends]
    out_specs = [
        q_spec,
        q_spec,
        pl.BlockSpec((1, n_query, HD), resp_map(own[1])),
        pl.BlockSpec((1, n_query, HD), lambda r, j, sc: (r, 0, 0)),
    ]
    out_specs += [pl.BlockSpec(g.shape, lambda r, j, sc: (0, 0, 0, 0)) for g in grads]
    out_shape = [
        shape(queries.shape, jnp.bfloat16),
        shape(queries.shape, jnp.bfloat16),
        shape(own[0].shape, jnp.bfloat16),
        shape((n_resp, n_query, HD), jnp.bfloat16),
    ] + grads
    scratch = [
        pltpu.VMEM((n_keys, HD), jnp.bfloat16),
        pltpu.VMEM((n_keys, HD), jnp.bfloat16),
        pltpu.VMEM((HD, n_query), jnp.bfloat16),
        pltpu.VMEM((HD, n_query), jnp.bfloat16),
        pltpu.VMEM((n_query, n_keys), jnp.float32),
        pltpu.VMEM((n_query, n_keys), jnp.float32),
        pltpu.VMEM((n_query, n_keys), jnp.bfloat16),
        pltpu.VMEM((n_query, n_keys), jnp.bfloat16),
        pltpu.VMEM((HD, n_keys), jnp.float32),
        pltpu.VMEM((HD, n_keys), jnp.float32),
        pltpu.VMEM((P_SIZE, n_prompt, HD), jnp.float32),
        pltpu.VMEM((P_SIZE, n_prompt, HD), jnp.float32),
    ]
    flops = 12 * n_resp * heads * n_query * n_keys * HD
    return pl.pallas_call(
        functools.partial(attend_kernel, (pieces, rows, keep, sends, n_pass)),
        grid_spec=pltpu.PrefetchScalarGridSpec(
            num_scalar_prefetch=1,
            grid=(n_resp, heads),
            in_specs=in_specs,
            out_specs=out_specs,
            scratch_shapes=scratch,
        ),
        out_shape=out_shape,
        input_output_aliases=aliases,
        compiler_params=pltpu.CompilerParams(vmem_limit_bytes=ATTEND_VMEM),
        cost_estimate=pl.CostEstimate(flops=2 * flops, bytes_accessed=4 * 2**20, transcendentals=0),
    )(scalars, *args)


def pack_kernel(src, own, *others):
    half = src.shape[2] // 2

    def split(start):
        own[...] = src[:, :, start : start + half]
        for k, out in enumerate(others):
            n = out.shape[2]
            at = half - start + k * n
            out[...] = src[:, :, at : at + n]

    @pl.when(lax.axis_index("prefix") % 2 == 0)
    def _():
        split(0)

    @pl.when(lax.axis_index("prefix") % 2 != 0)
    def _():
        split(half)


def pack(array, sections):
    block = lambda shape: pl.BlockSpec(shape, lambda i: (0, 0, 0))
    half = array.shape[2] // 2
    shapes = [array.shape[:2] + (n,) for n in (half, *[half // sections] * sections)]
    return pl.pallas_call(
        pack_kernel,
        grid=(1,),
        in_specs=[block(array.shape)],
        out_specs=[block(s) for s in shapes],
        out_shape=[jax.ShapeDtypeStruct(s, array.dtype) for s in shapes],
        compiler_params=pltpu.CompilerParams(vmem_limit_bytes=PACK_VMEM),
    )(array)


def per_device(queries, resp_kv, prompt_kv, prompt_of, d_out):
    pair_heads = prompt_kv.shape[2] // HD
    parity = lax.axis_index("prefix") % 2
    scalars = jnp.concatenate([prompt_of, parity[None].astype(jnp.int32)])
    if lax.axis_size("dp") == 4 and pair_heads % 2 == 0:
        return whole_heads(queries, resp_kv, prompt_kv, scalars, parity, d_out)
    return shared_head(queries, resp_kv, prompt_kv, scalars, parity, d_out)


def whole_heads(queries, resp_kv, prompt_kv, scalars, parity, d_out):
    n_own = prompt_kv.shape[2] // HD // 2
    z = functools.partial(swap, axis="prefix", step=1)
    core, x, both = [functools.partial(swap, axis="dp", step=k) for k in (1, 2, 3)]
    theirs = (1 - parity) * n_own

    def order(values, done):
        return lax.optimization_barrier((tuple(values), tuple(done)))[0]

    a0, b0 = pack(prompt_kv, 1)
    b0 = z(b0)
    a2 = x(a0)
    resp_a, *resp_b = pack(resp_kv, n_own)
    resp_b[0] = z(resp_b[0])
    (ready,) = order([b0], [resp_a])
    b2 = x(ready)
    for h in range(1, n_own):
        resp_b[h] = z(order([resp_b[h]], [b0])[0])
    pa = [a0, core(a0), a2, core(a2)]
    pb = [b0, core(b0), b2, core(b2)]

    shared = None
    d_resp, d_prompt = [], []
    for h in range(n_own):
        final = h == n_own - 1
        here = lambda par, h=h: par * n_own + h
        own = lambda par, h=h: h
        at = lambda par: 0
        att, dq, dra, drb, keep, *sends = attend(
            scalars,
            queries,
            d_out,
            (resp_a, own),
            (resp_b[h], at),
            [(a, own) for a in pa],
            [(b, own) for b in pb],
            (0, 2) if final else (0,),
            ((1, 3),) if final else ((1,), (2,), (3,)),
            h,
            GROUP,
            shared,
            (resp_kv, here),
        )
        shared = (att, dq, dra)
        d_resp.append(z(drb))
        if final:
            (send,) = order([sends[0]], arrived)
            sums = keep + core(send).astype(jnp.float32)
            (across,) = order([x(sums[1].astype(jnp.bfloat16))], [d_resp[-1]])
            total = sums[0] + across.astype(jnp.float32)
        else:
            parts = [move(part[0]) for move, part in zip((core, x, both), sends)]
            arrived = [*parts, d_resp[-1]]
            total = keep[0] + sum(p.astype(jnp.float32) for p in parts)
        other = z(total[:, :, HD:].astype(jnp.bfloat16))
        d_prompt.append((total[:, :, :HD], other))

    even = parity == 0
    mine = jnp.concatenate([a for a, _ in d_prompt], axis=-1)
    *others, final = [b.astype(jnp.float32) for _, b in d_prompt]
    other = jnp.concatenate([*others, jnp.zeros_like(final)], axis=-1)
    d_prompt = jnp.concatenate([jnp.where(even, mine, other), jnp.where(even, other, mine)], axis=-1)
    (d_prompt,) = order([d_prompt], [])
    d_prompt = lax.dynamic_update_slice_in_dim(d_prompt, final, (theirs + n_own - 1) * HD, axis=2)
    att, dq, d_resp_kv = shared
    received = jnp.concatenate(d_resp, axis=-1)
    d_resp_kv = lax.dynamic_update_slice_in_dim(d_resp_kv, received, theirs * HD, axis=2)
    return att, dq, d_resp_kv, d_prompt


def shared_head(queries, resp_kv, prompt_kv, scalars, parity, d_out):
    first = lambda par: 0
    prompt_a = lax.all_gather(prompt_kv, "dp", axis=1, tiled=True)
    prompt_b = swap(prompt_a, "prefix", 1)
    resp_b = swap(resp_kv, "prefix", 1)
    att, dq, dra, drb, keep = attend(
        scalars,
        queries,
        d_out,
        (resp_kv, first),
        (resp_b, first),
        [(prompt_a, first)],
        [(prompt_b, first)],
        (0,),
        (),
        0,
        queries.shape[2] // HD,
        None,
        (resp_kv, first),
    )
    d_resp = (dra.astype(jnp.float32) + swap(drb, "prefix", 1).astype(jnp.float32)).astype(jnp.bfloat16)
    other = swap(keep[0, :, :, HD:].astype(jnp.bfloat16), "prefix", 1)
    paired = keep[0, :, :, :HD] + other.astype(jnp.float32)
    d_prompt = lax.psum_scatter(paired, "dp", scatter_dimension=1, tiled=True)
    return att, dq, d_resp, d_prompt


def solution(mesh):
    in_specs = (
        P(("groups", "dp"), None, "prefix"),
        P(("groups", "dp"), None, "prefix"),
        P("groups", "dp", "prefix"),
        P(("groups", "dp")),
        P(("groups", "dp"), None, "prefix"),
    )
    out_specs = (
        P(("groups", "dp"), None, "prefix"),
        P(("groups", "dp"), None, "prefix"),
        P(("groups", "dp"), None, "prefix"),
        P("groups", "dp", "prefix"),
    )
    return jax.shard_map(
        per_device, mesh=mesh, in_specs=in_specs, out_specs=out_specs, check_vma=False
    )
```

```python
import functools

import jax
import jax.numpy as jnp
from jax import lax
from jax.experimental import pallas as pl
from jax.experimental.pallas import tpu as pltpu
from jax.sharding import PartitionSpec as P

H = 32
KVH = 8
HD = 128
P_SIZE = 2
GROUP = H // KVH
BLOCK = 256
STRIP = 16
PAIR = 2
MASKED = -1e30
ATTEND_VMEM = 48 * 2**20
PACK_VMEM = 48 * 2**20
SCALE = HD ** (-0.5)

NT = (((1,), (1,)), ((), ()))
NN = (((1,), (0,)), ((), ()))


def dot(a, b, dims):
    return lax.dot_general(a, b, dims, preferred_element_type=jnp.float32)


def swap(block, axis, step):
    return lax.ppermute(block, axis, [(i, i ^ step) for i in range(lax.axis_size(axis))])


def attend_kernel(sizes, scalars, *refs):
    pieces, rows, keep, sends, n_pass = sizes
    refs = list(refs)
    q_ref, do_ref, ra_ref, rb_ref = refs[:4]
    pa_refs = refs[4 : 4 + pieces]
    pb_refs = refs[4 + pieces : 4 + 2 * pieces]
    rest = refs[4 + 2 * pieces + n_pass :]
    out_ref, dq_ref, dra_ref, drb_ref, keep_ref = rest[:5]
    send_refs = rest[5 : 5 + len(sends)]
    k_all, v_all, q_all, do_all, q_t, do_t, scores, grad_probs, probs, dscores, acc_k, acc_v, sum_k, sum_v = rest[5 + len(sends) :]

    r = pl.program_id(0)
    head = pl.program_id(1)
    n_resp = pl.num_programs(0)
    last = head == pl.num_programs(1) - 1
    prompt = scalars[r]
    even = scalars[n_resp] == 0
    n_prompt = pieces * rows
    n_query = q_ref.shape[1]
    n_blocks = n_query // BLOCK

    def gather(dst, piece_refs, resp_ref):
        for i, ref in enumerate(piece_refs):
            dst[i * rows : (i + 1) * rows, :] = ref[0]
        dst[n_prompt:, :] = resp_ref[0]

    @pl.when((head == 0) & even)
    def _():
        gather(k_all, pa_refs, ra_ref)
        gather(v_all, pb_refs, rb_ref)

    @pl.when((head == 0) & jnp.logical_not(even))
    def _():
        gather(k_all, pb_refs, rb_ref)
        gather(v_all, pa_refs, ra_ref)

    @pl.when(head == 0)
    def _():
        acc_k[...] = jnp.zeros_like(acc_k)
        acc_v[...] = jnp.zeros_like(acc_v)

    size = PAIR * BLOCK

    for i in range(n_blocks):
        for j in range(PAIR):
            at = slice(i * size + j * BLOCK, i * size + (j + 1) * BLOCK)
            from_t, lanes = slice(i * BLOCK, (i + 1) * BLOCK), slice(j * HD, (j + 1) * HD)
            q_all[at, :] = q_ref[0, from_t, lanes]
            do_all[at, :] = do_ref[0, from_t, lanes]

    def seeing(u):
        return slice(max(u - n_prompt, 0) // BLOCK * size, n_blocks * size)

    def score(u):
        t = seeing(u)
        scores[t, u : u + BLOCK] = dot(q_all[t, :], k_all[u : u + BLOCK, :], NT)

    def grad_prob(u):
        t = seeing(u)
        grad_probs[t, u : u + BLOCK] = dot(do_all[t, :], v_all[u : u + BLOCK, :], NT)

    def grad_value(u):
        t = seeing(u)
        acc_v[:, u : u + BLOCK] += dot(do_t[:, t], probs[t, u : u + BLOCK], NN)

    def grad_key(u):
        t = seeing(u)
        acc_k[:, u : u + BLOCK] += dot(q_t[:, t], dscores[t, u : u + BLOCK], NN)

    def turn():
        q_t[...] = q_all[...].T
        do_t[...] = do_all[...].T

    def stages(i):
        st = {}
        t0 = i * size
        t = slice(t0, t0 + size)
        edge = n_prompt + i * BLOCK
        seen = edge + BLOCK

        def put(ref, rows_out):
            for j in range(PAIR):
                part = rows_out[j * BLOCK : (j + 1) * BLOCK].astype(jnp.bfloat16)
                ref[0, i * BLOCK : (i + 1) * BLOCK, j * HD : (j + 1) * HD] = part

        def softmax(row):
            at = slice(t0 + row, t0 + row + STRIP)
            left = scores[at, :edge]
            rows_at = lax.broadcasted_iota(jnp.int32, (STRIP, BLOCK), 0) + row % BLOCK
            columns = lax.broadcasted_iota(jnp.int32, (STRIP, BLOCK), 1)
            right = jnp.where(columns <= rows_at, scores[at, edge:seen], MASKED)
            top = jnp.maximum(jnp.max(left, axis=1, keepdims=True), jnp.max(right, axis=1, keepdims=True)) * SCALE
            left = jnp.exp(left * SCALE - top)
            right = jnp.exp(right * SCALE - top)
            inv = 1.0 / (jnp.sum(left, axis=1, keepdims=True) + jnp.sum(right, axis=1, keepdims=True))
            for part, u in ((left * inv, slice(0, edge)), (right * inv, slice(edge, seen))):
                scores[at, u] = part
                probs[at, u] = part.astype(jnp.bfloat16)

        def output():
            o = dot(probs[t, :seen], v_all[:seen, :], NN)
            put(out_ref, o)
            st["delta"] = jnp.sum(o * do_all[t, :].astype(jnp.float32), axis=1, keepdims=True)

        def grad_score(row):
            at = slice(t0 + row, t0 + row + STRIP)
            delta = st["delta"][row : row + STRIP]
            ds = (scores[at, :seen] * SCALE) * (grad_probs[at, :seen] - delta)
            dscores[at, :seen] = ds.astype(jnp.bfloat16)

        def query():
            put(dq_ref, dot(dscores[t, :seen], k_all[:seen, :], NN))

        strips = range(0, size, STRIP)
        each = lambda f: [functools.partial(f, x) for x in strips]
        return {"softmax": each(softmax), "output": [output], "grad": each(grad_score), "query": [query]}

    def mix(*lists):
        order = [((at + 0.5) / len(x), k, f) for k, x in enumerate(lists) for at, f in enumerate(x)]
        for _, _, f in sorted(order, key=lambda e: e[:2]):
            f()

    plan = [stages(i) for i in range(n_blocks)]
    over = lambda f: [functools.partial(f, u) for u in range(0, n_prompt + n_query, BLOCK)]
    mix(over(score), [turn])
    mix(plan[0]["softmax"], over(grad_prob))
    for i in range(1, n_blocks):
        mix(plan[i]["softmax"], plan[i - 1]["output"])
        mix(plan[i - 1]["grad"], plan[i]["output"] if i == n_blocks - 1 else [])
    if n_blocks == 1:
        mix(plan[0]["output"])
    mix(plan[-1]["grad"], *[p["query"] for p in plan[:-1]], over(grad_value))
    mix(plan[-1]["query"], over(grad_key))

    def respond(ref, acc):
        ref[0] = acc[:, n_prompt:].T.astype(jnp.bfloat16)

    @pl.when(last & even)
    def _():
        respond(dra_ref, acc_k)
        respond(drb_ref, acc_v)

    @pl.when(last & jnp.logical_not(even))
    def _():
        respond(dra_ref, acc_v)
        respond(drb_ref, acc_k)

    @pl.when(last & (r == 0))
    def _():
        for whole, acc in ((sum_k, acc_k), (sum_v, acc_v)):
            whole[prompt] = acc[:, :n_prompt].T
            whole[1 - prompt] = jnp.zeros((n_prompt, HD), jnp.float32)

    @pl.when(last & (r > 0))
    def _():
        for whole, acc in ((sum_k, acc_k), (sum_v, acc_v)):
            whole[prompt] += acc[:, :n_prompt].T

    done = last & (r == n_resp - 1)

    def scatter(slot, whole):
        lanes = slice(slot * HD, (slot + 1) * HD)
        for ref, group in ((keep_ref, keep), *zip(send_refs, sends)):
            for at, i in enumerate(group):
                ref[at, :, :, lanes] = whole[:, i * rows : (i + 1) * rows, :].astype(ref.dtype)

    @pl.when(done & even)
    def _():
        scatter(0, sum_k)
        scatter(1, sum_v)

    @pl.when(done & jnp.logical_not(even))
    def _():
        scatter(0, sum_v)
        scatter(1, sum_k)


def attend(scalars, queries, d_out, resp_a, resp_b, prompt_a, prompt_b, keep, sends, chunk, heads, shared, own):
    n_resp, n_query, _ = queries.shape
    pieces = len(prompt_a)
    rows = prompt_a[0][0].shape[1]
    n_prompt = pieces * rows
    n_keys = n_prompt + n_query
    shape = jax.ShapeDtypeStruct

    def resp_map(column):
        return lambda r, j, sc: (r, 0, column(sc[n_resp]))

    def prompt_map(column):
        return lambda r, j, sc: (sc[r], 0, column(sc[n_resp]))

    steps = heads // PAIR
    n_rows = PAIR * n_query
    q_spec = pl.BlockSpec((1, n_query, PAIR * HD), lambda r, j, sc: (r, 0, chunk * steps + j))
    in_specs = [q_spec, q_spec]
    in_specs += [pl.BlockSpec((1, n_query, HD), resp_map(c)) for _, c in (resp_a, resp_b)]
    in_specs += [pl.BlockSpec((1, rows, HD), prompt_map(c)) for _, c in (*prompt_a, *prompt_b)]
    args = [queries, d_out, resp_a[0], resp_b[0], *[a for a, _ in (*prompt_a, *prompt_b)]]
    aliases = {}
    if shared is not None:
        aliases = {1 + len(args) + i: i for i in range(3)}
        args += list(shared)
    n_pass = len(args) - len(in_specs)
    in_specs += [pl.BlockSpec(memory_space=pl.ANY)] * n_pass
    grads = [shape((len(keep), P_SIZE, rows, 2 * HD), jnp.float32)]
    grads += [shape((len(g), P_SIZE, rows, 2 * HD), jnp.bfloat16) for g in sends]
    out_specs = [
        q_spec,
        q_spec,
        pl.BlockSpec((1, n_query, HD), resp_map(own[1])),
        pl.BlockSpec((1, n_query, HD), lambda r, j, sc: (r, 0, 0)),
    ]
    out_specs += [pl.BlockSpec(g.shape, lambda r, j, sc: (0, 0, 0, 0)) for g in grads]
    out_shape = [
        shape(queries.shape, jnp.bfloat16),
        shape(queries.shape, jnp.bfloat16),
        shape(own[0].shape, jnp.bfloat16),
        shape((n_resp, n_query, HD), jnp.bfloat16),
    ] + grads
    scratch = [
        pltpu.VMEM((n_keys, HD), jnp.bfloat16),
        pltpu.VMEM((n_keys, HD), jnp.bfloat16),
        pltpu.VMEM((n_rows, HD), jnp.bfloat16),
        pltpu.VMEM((n_rows, HD), jnp.bfloat16),
        pltpu.VMEM((HD, n_rows), jnp.bfloat16),
        pltpu.VMEM((HD, n_rows), jnp.bfloat16),
        pltpu.VMEM((n_rows, n_keys), jnp.float32),
        pltpu.VMEM((n_rows, n_keys), jnp.float32),
        pltpu.VMEM((n_rows, n_keys), jnp.bfloat16),
        pltpu.VMEM((n_rows, n_keys), jnp.bfloat16),
        pltpu.VMEM((HD, n_keys), jnp.float32),
        pltpu.VMEM((HD, n_keys), jnp.float32),
        pltpu.VMEM((P_SIZE, n_prompt, HD), jnp.float32),
        pltpu.VMEM((P_SIZE, n_prompt, HD), jnp.float32),
    ]
    flops = 12 * n_resp * heads * n_query * n_keys * HD
    return pl.pallas_call(
        functools.partial(attend_kernel, (pieces, rows, keep, sends, n_pass)),
        grid_spec=pltpu.PrefetchScalarGridSpec(
            num_scalar_prefetch=1,
            grid=(n_resp, steps),
            in_specs=in_specs,
            out_specs=out_specs,
            scratch_shapes=scratch,
        ),
        out_shape=out_shape,
        input_output_aliases=aliases,
        compiler_params=pltpu.CompilerParams(vmem_limit_bytes=ATTEND_VMEM),
        cost_estimate=pl.CostEstimate(flops=2 * flops, bytes_accessed=4 * 2**20, transcendentals=0),
    )(scalars, *args)


def pack_kernel(src, own, *others):
    half = src.shape[2] // 2

    def split(start):
        own[...] = src[:, :, start : start + half]
        for k, out in enumerate(others):
            n = out.shape[2]
            at = half - start + k * n
            out[...] = src[:, :, at : at + n]

    @pl.when(lax.axis_index("prefix") % 2 == 0)
    def _():
        split(0)

    @pl.when(lax.axis_index("prefix") % 2 != 0)
    def _():
        split(half)


def pack(array, sections):
    block = lambda shape: pl.BlockSpec(shape, lambda i: (0, 0, 0))
    half = array.shape[2] // 2
    shapes = [array.shape[:2] + (n,) for n in (half, *[half // sections] * sections)]
    return pl.pallas_call(
        pack_kernel,
        grid=(1,),
        in_specs=[block(array.shape)],
        out_specs=[block(s) for s in shapes],
        out_shape=[jax.ShapeDtypeStruct(s, array.dtype) for s in shapes],
        compiler_params=pltpu.CompilerParams(vmem_limit_bytes=PACK_VMEM),
    )(array)


def per_device(queries, resp_kv, prompt_kv, prompt_of, d_out):
    pair_heads = prompt_kv.shape[2] // HD
    parity = lax.axis_index("prefix") % 2
    scalars = jnp.concatenate([prompt_of, parity[None].astype(jnp.int32)])
    if lax.axis_size("dp") == 4 and pair_heads % 2 == 0:
        return whole_heads(queries, resp_kv, prompt_kv, scalars, parity, d_out)
    return shared_head(queries, resp_kv, prompt_kv, scalars, parity, d_out)


def whole_heads(queries, resp_kv, prompt_kv, scalars, parity, d_out):
    n_own = prompt_kv.shape[2] // HD // 2
    z = functools.partial(swap, axis="prefix", step=1)
    core, x, both = [functools.partial(swap, axis="dp", step=k) for k in (1, 2, 3)]
    theirs = (1 - parity) * n_own

    def order(values, done):
        return lax.optimization_barrier((tuple(values), tuple(done)))[0]

    a0, b0 = pack(prompt_kv, 1)
    b0 = z(b0)
    a2 = x(a0)
    resp_a, *resp_b = pack(resp_kv, n_own)
    resp_b[0] = z(resp_b[0])
    (ready,) = order([b0], [resp_a])
    b2 = x(ready)
    for h in range(1, n_own):
        resp_b[h] = z(order([resp_b[h]], [b0])[0])
    pa = [a0, core(a0), a2, core(a2)]
    pb = [b0, core(b0), b2, core(b2)]

    shared = None
    d_resp, d_prompt = [], []
    for h in range(n_own):
        final = h == n_own - 1
        here = lambda par, h=h: par * n_own + h
        own = lambda par, h=h: h
        at = lambda par: 0
        att, dq, dra, drb, keep, *sends = attend(
            scalars,
            queries,
            d_out,
            (resp_a, own),
            (resp_b[h], at),
            [(a, own) for a in pa],
            [(b, own) for b in pb],
            (0, 2) if final else (0,),
            ((1, 3),) if final else ((1,), (2,), (3,)),
            h,
            GROUP,
            shared,
            (resp_kv, here),
        )
        shared = (att, dq, dra)
        d_resp.append(z(drb))
        if final:
            (send,) = order([sends[0]], arrived)
            sums = keep + core(send).astype(jnp.float32)
            (across,) = order([x(sums[1].astype(jnp.bfloat16))], [d_resp[-1]])
            total = sums[0] + across.astype(jnp.float32)
        else:
            parts = [move(part[0]) for move, part in zip((core, x, both), sends)]
            arrived = [*parts, d_resp[-1]]
            total = keep[0] + sum(p.astype(jnp.float32) for p in parts)
        other = z(total[:, :, HD:].astype(jnp.bfloat16))
        d_prompt.append((total[:, :, :HD], other))

    even = parity == 0
    mine = jnp.concatenate([a for a, _ in d_prompt], axis=-1)
    *others, final = [b.astype(jnp.float32) for _, b in d_prompt]
    other = jnp.concatenate([*others, jnp.zeros_like(final)], axis=-1)
    d_prompt = jnp.concatenate([jnp.where(even, mine, other), jnp.where(even, other, mine)], axis=-1)
    (d_prompt,) = order([d_prompt], [])
    d_prompt = lax.dynamic_update_slice_in_dim(d_prompt, final, (theirs + n_own - 1) * HD, axis=2)
    att, dq, d_resp_kv = shared
    received = jnp.concatenate(d_resp, axis=-1)
    d_resp_kv = lax.dynamic_update_slice_in_dim(d_resp_kv, received, theirs * HD, axis=2)
    return att, dq, d_resp_kv, d_prompt


def shared_head(queries, resp_kv, prompt_kv, scalars, parity, d_out):
    first = lambda par: 0
    prompt_a = lax.all_gather(prompt_kv, "dp", axis=1, tiled=True)
    prompt_b = swap(prompt_a, "prefix", 1)
    resp_b = swap(resp_kv, "prefix", 1)
    att, dq, dra, drb, keep = attend(
        scalars,
        queries,
        d_out,
        (resp_kv, first),
        (resp_b, first),
        [(prompt_a, first)],
        [(prompt_b, first)],
        (0,),
        (),
        0,
        queries.shape[2] // HD,
        None,
        (resp_kv, first),
    )
    d_resp = (dra.astype(jnp.float32) + swap(drb, "prefix", 1).astype(jnp.float32)).astype(jnp.bfloat16)
    other = swap(keep[0, :, :, HD:].astype(jnp.bfloat16), "prefix", 1)
    paired = keep[0, :, :, :HD] + other.astype(jnp.float32)
    d_prompt = lax.psum_scatter(paired, "dp", scatter_dimension=1, tiled=True)
    return att, dq, d_resp, d_prompt


def solution(mesh):
    in_specs = (
        P(("groups", "dp"), None, "prefix"),
        P(("groups", "dp"), None, "prefix"),
        P("groups", "dp", "prefix"),
        P(("groups", "dp")),
        P(("groups", "dp"), None, "prefix"),
    )
    out_specs = (
        P(("groups", "dp"), None, "prefix"),
        P(("groups", "dp"), None, "prefix"),
        P(("groups", "dp"), None, "prefix"),
        P("groups", "dp", "prefix"),
    )
    return jax.shard_map(
        per_device, mesh=mesh, in_specs=in_specs, out_specs=out_specs, check_vma=False
    )
```

```python
import functools

import jax
import jax.numpy as jnp
from jax import lax
from jax.experimental import pallas as pl
from jax.experimental.pallas import tpu as pltpu
from jax.sharding import PartitionSpec as P

H = 32
KVH = 8
HD = 128
P_SIZE = 2
GROUP = H // KVH
BLOCK = 256
STRIP = 16
PAIR = 2
MASKED = -1e30
ATTEND_VMEM = 40 * 2**20
PACK_VMEM = 48 * 2**20
SCALE = HD ** (-0.5)

NT = (((1,), (1,)), ((), ()))
NN = (((1,), (0,)), ((), ()))


def dot(a, b, dims):
    return lax.dot_general(a, b, dims, preferred_element_type=jnp.float32)


def swap(block, axis, step):
    return lax.ppermute(block, axis, [(i, i ^ step) for i in range(lax.axis_size(axis))])


def attend_kernel(sizes, scalars, *refs):
    pieces, rows, keep, sends, n_pass = sizes
    refs = list(refs)
    q_ref, do_ref, ra_ref, rb_ref = refs[:4]
    pa_refs = refs[4 : 4 + pieces]
    pb_refs = refs[4 + pieces : 4 + 2 * pieces]
    rest = refs[4 + 2 * pieces + n_pass :]
    out_ref, dq_ref, dra_ref, drb_ref, keep_ref = rest[:5]
    send_refs = rest[5 : 5 + len(sends)]
    k_all, v_all, q_all, do_all, q_t, do_t, scores, grad_probs, probs, dscores, acc_k, acc_v, sum_k, sum_v = rest[5 + len(sends) :]

    r = pl.program_id(0)
    head = pl.program_id(1)
    n_resp = pl.num_programs(0)
    last = head == pl.num_programs(1) - 1
    prompt = scalars[r]
    even = scalars[n_resp] == 0
    n_prompt = pieces * rows
    n_query = q_ref.shape[1]
    n_blocks = n_query // BLOCK

    def gather(dst, piece_refs, resp_ref):
        for i, ref in enumerate(piece_refs):
            dst[i * rows : (i + 1) * rows, :] = ref[0]
        dst[n_prompt:, :] = resp_ref[0]

    @pl.when((head == 0) & even)
    def _():
        gather(k_all, pa_refs, ra_ref)
        gather(v_all, pb_refs, rb_ref)

    @pl.when((head == 0) & jnp.logical_not(even))
    def _():
        gather(k_all, pb_refs, rb_ref)
        gather(v_all, pa_refs, ra_ref)

    @pl.when(head == 0)
    def _():
        acc_k[...] = jnp.zeros_like(acc_k)
        acc_v[...] = jnp.zeros_like(acc_v)

    size = PAIR * BLOCK

    for i in range(n_blocks):
        for j in range(PAIR):
            at = slice(i * size + j * BLOCK, i * size + (j + 1) * BLOCK)
            from_t, lanes = slice(i * BLOCK, (i + 1) * BLOCK), slice(j * HD, (j + 1) * HD)
            q_all[at, :] = q_ref[0, from_t, lanes]
            do_all[at, :] = do_ref[0, from_t, lanes]

    def seeing(u):
        return slice(max(u - n_prompt, 0) // BLOCK * size, n_blocks * size)

    def score(u):
        t = seeing(u)
        scores[t, u : u + BLOCK] = dot(q_all[t, :], k_all[u : u + BLOCK, :], NT)

    def grad_prob(u):
        t = seeing(u)
        grad_probs[t, u : u + BLOCK] = dot(do_all[t, :], v_all[u : u + BLOCK, :], NT)

    def grad_value(u):
        t = seeing(u)
        acc_v[:, u : u + BLOCK] += dot(do_t[:, t], probs[t, u : u + BLOCK], NN)

    def grad_key(u):
        t = seeing(u)
        acc_k[:, u : u + BLOCK] += dot(q_t[:, t], dscores[t, u : u + BLOCK], NN)

    def turn():
        q_t[...] = q_all[...].T
        do_t[...] = do_all[...].T

    def stages(i):
        st = {}
        t0 = i * size
        t = slice(t0, t0 + size)
        edge = n_prompt + i * BLOCK
        seen = edge + BLOCK

        def put(ref, rows_out):
            for j in range(PAIR):
                part = rows_out[j * BLOCK : (j + 1) * BLOCK].astype(jnp.bfloat16)
                ref[0, i * BLOCK : (i + 1) * BLOCK, j * HD : (j + 1) * HD] = part

        def softmax(row):
            at = slice(t0 + row, t0 + row + STRIP)
            left = scores[at, :edge]
            rows_at = lax.broadcasted_iota(jnp.int32, (STRIP, BLOCK), 0) + row % BLOCK
            columns = lax.broadcasted_iota(jnp.int32, (STRIP, BLOCK), 1)
            right = jnp.where(columns <= rows_at, scores[at, edge:seen], MASKED)
            top = jnp.maximum(jnp.max(left, axis=1, keepdims=True), jnp.max(right, axis=1, keepdims=True)) * SCALE
            left = jnp.exp(left * SCALE - top)
            right = jnp.exp(right * SCALE - top)
            inv = 1.0 / (jnp.sum(left, axis=1, keepdims=True) + jnp.sum(right, axis=1, keepdims=True))
            for part, u in ((left * inv, slice(0, edge)), (right * inv, slice(edge, seen))):
                scores[at, u] = part
                probs[at, u] = part.astype(jnp.bfloat16)

        def output():
            o = dot(probs[t, :seen], v_all[:seen, :], NN)
            put(out_ref, o)
            st["delta"] = jnp.sum(o * do_all[t, :].astype(jnp.float32), axis=1, keepdims=True)

        def grad_score(row):
            at = slice(t0 + row, t0 + row + STRIP)
            delta = st["delta"][row : row + STRIP]
            ds = (scores[at, :seen] * SCALE) * (grad_probs[at, :seen] - delta)
            dscores[at, :seen] = ds.astype(jnp.bfloat16)

        def query():
            put(dq_ref, dot(dscores[t, :seen], k_all[:seen, :], NN))

        strips = range(0, size, STRIP)
        each = lambda f: [functools.partial(f, x) for x in strips]
        return {"softmax": each(softmax), "output": [output], "grad": each(grad_score), "query": [query]}

    def mix(*lists):
        order = [((at + 0.5) / len(x), k, f) for k, x in enumerate(lists) for at, f in enumerate(x)]
        for _, _, f in sorted(order, key=lambda e: e[:2]):
            f()

    plan = [stages(i) for i in range(n_blocks)]
    over = lambda f: [functools.partial(f, u) for u in range(0, n_prompt + n_query, BLOCK)]
    mix(over(score), [turn])
    mix(plan[0]["softmax"], over(grad_prob))
    for i in range(1, n_blocks):
        mix(plan[i]["softmax"], plan[i - 1]["output"])
        mix(plan[i - 1]["grad"], plan[i]["output"] if i == n_blocks - 1 else [])
    if n_blocks == 1:
        mix(plan[0]["output"])
    mix(plan[-1]["grad"], *[p["query"] for p in plan[:-1]], over(grad_value))
    mix(plan[-1]["query"], over(grad_key))

    def respond(ref, acc):
        ref[0] = acc[:, n_prompt:].T.astype(jnp.bfloat16)

    @pl.when(last & even)
    def _():
        respond(dra_ref, acc_k)
        respond(drb_ref, acc_v)

    @pl.when(last & jnp.logical_not(even))
    def _():
        respond(dra_ref, acc_v)
        respond(drb_ref, acc_k)

    @pl.when(last & (r == 0))
    def _():
        for whole, acc in ((sum_k, acc_k), (sum_v, acc_v)):
            whole[prompt] = acc[:, :n_prompt].T
            whole[1 - prompt] = jnp.zeros((n_prompt, HD), jnp.float32)

    @pl.when(last & (r > 0))
    def _():
        for whole, acc in ((sum_k, acc_k), (sum_v, acc_v)):
            whole[prompt] += acc[:, :n_prompt].T

    done = last & (r == n_resp - 1)

    def scatter(slot, whole):
        lanes = slice(slot * HD, (slot + 1) * HD)
        for ref, group in ((keep_ref, keep), *zip(send_refs, sends)):
            for at, i in enumerate(group):
                ref[at, :, :, lanes] = whole[:, i * rows : (i + 1) * rows, :].astype(ref.dtype)

    @pl.when(done & even)
    def _():
        scatter(0, sum_k)
        scatter(1, sum_v)

    @pl.when(done & jnp.logical_not(even))
    def _():
        scatter(0, sum_v)
        scatter(1, sum_k)


def attend(scalars, queries, d_out, resp_a, resp_b, prompt_a, prompt_b, keep, sends, chunk, heads, shared, own):
    n_resp, n_query, _ = queries.shape
    pieces = len(prompt_a)
    rows = prompt_a[0][0].shape[1]
    n_prompt = pieces * rows
    n_keys = n_prompt + n_query
    shape = jax.ShapeDtypeStruct

    def resp_map(column):
        return lambda r, j, sc: (r, 0, column(sc[n_resp]))

    def prompt_map(column):
        return lambda r, j, sc: (sc[r], 0, column(sc[n_resp]))

    steps = heads // PAIR
    n_rows = PAIR * n_query
    q_spec = pl.BlockSpec((1, n_query, PAIR * HD), lambda r, j, sc: (r, 0, chunk * steps + j))
    in_specs = [q_spec, q_spec]
    in_specs += [pl.BlockSpec((1, n_query, HD), resp_map(c)) for _, c in (resp_a, resp_b)]
    in_specs += [pl.BlockSpec((1, rows, HD), prompt_map(c)) for _, c in (*prompt_a, *prompt_b)]
    args = [queries, d_out, resp_a[0], resp_b[0], *[a for a, _ in (*prompt_a, *prompt_b)]]
    aliases = {}
    if shared is not None:
        aliases = {1 + len(args) + i: i for i in range(3)}
        args += list(shared)
    n_pass = len(args) - len(in_specs)
    in_specs += [pl.BlockSpec(memory_space=pl.ANY)] * n_pass
    grads = [shape((len(keep), P_SIZE, rows, 2 * HD), jnp.float32)]
    grads += [shape((len(g), P_SIZE, rows, 2 * HD), jnp.bfloat16) for g in sends]
    out_specs = [
        q_spec,
        q_spec,
        pl.BlockSpec((1, n_query, HD), resp_map(own[1])),
        pl.BlockSpec((1, n_query, HD), lambda r, j, sc: (r, 0, 0)),
    ]
    out_specs += [pl.BlockSpec(g.shape, lambda r, j, sc: (0, 0, 0, 0)) for g in grads]
    out_shape = [
        shape(queries.shape, jnp.bfloat16),
        shape(queries.shape, jnp.bfloat16),
        shape(own[0].shape, jnp.bfloat16),
        shape((n_resp, n_query, HD), jnp.bfloat16),
    ] + grads
    scratch = [
        pltpu.VMEM((n_keys, HD), jnp.bfloat16),
        pltpu.VMEM((n_keys, HD), jnp.bfloat16),
        pltpu.VMEM((n_rows, HD), jnp.bfloat16),
        pltpu.VMEM((n_rows, HD), jnp.bfloat16),
        pltpu.VMEM((HD, n_rows), jnp.bfloat16),
        pltpu.VMEM((HD, n_rows), jnp.bfloat16),
        pltpu.VMEM((n_rows, n_keys), jnp.float32),
        pltpu.VMEM((n_rows, n_keys), jnp.float32),
        pltpu.VMEM((n_rows, n_keys), jnp.bfloat16),
        pltpu.VMEM((n_rows, n_keys), jnp.bfloat16),
        pltpu.VMEM((HD, n_keys), jnp.float32),
        pltpu.VMEM((HD, n_keys), jnp.float32),
        pltpu.VMEM((P_SIZE, n_prompt, HD), jnp.float32),
        pltpu.VMEM((P_SIZE, n_prompt, HD), jnp.float32),
    ]
    flops = 12 * n_resp * heads * n_query * n_keys * HD
    return pl.pallas_call(
        functools.partial(attend_kernel, (pieces, rows, keep, sends, n_pass)),
        grid_spec=pltpu.PrefetchScalarGridSpec(
            num_scalar_prefetch=1,
            grid=(n_resp, steps),
            in_specs=in_specs,
            out_specs=out_specs,
            scratch_shapes=scratch,
        ),
        out_shape=out_shape,
        input_output_aliases=aliases,
        compiler_params=pltpu.CompilerParams(vmem_limit_bytes=ATTEND_VMEM),
        cost_estimate=pl.CostEstimate(flops=2 * flops, bytes_accessed=4 * 2**20, transcendentals=0),
    )(scalars, *args)


def pack_kernel(src, own, *others):
    half = src.shape[2] // 2

    def split(start):
        own[...] = src[:, :, start : start + half]
        for k, out in enumerate(others):
            n = out.shape[2]
            at = half - start + k * n
            out[...] = src[:, :, at : at + n]

    @pl.when(lax.axis_index("prefix") % 2 == 0)
    def _():
        split(0)

    @pl.when(lax.axis_index("prefix") % 2 != 0)
    def _():
        split(half)


def pack(array, sections):
    block = lambda shape: pl.BlockSpec(shape, lambda i: (0, 0, 0))
    half = array.shape[2] // 2
    shapes = [array.shape[:2] + (n,) for n in (half, *[half // sections] * sections)]
    return pl.pallas_call(
        pack_kernel,
        grid=(1,),
        in_specs=[block(array.shape)],
        out_specs=[block(s) for s in shapes],
        out_shape=[jax.ShapeDtypeStruct(s, array.dtype) for s in shapes],
        compiler_params=pltpu.CompilerParams(vmem_limit_bytes=PACK_VMEM),
    )(array)


def per_device(queries, resp_kv, prompt_kv, prompt_of, d_out):
    pair_heads = prompt_kv.shape[2] // HD
    parity = lax.axis_index("prefix") % 2
    scalars = jnp.concatenate([prompt_of, parity[None].astype(jnp.int32)])
    if lax.axis_size("dp") == 4 and pair_heads % 2 == 0:
        return whole_heads(queries, resp_kv, prompt_kv, scalars, parity, d_out)
    return shared_head(queries, resp_kv, prompt_kv, scalars, parity, d_out)


def whole_heads(queries, resp_kv, prompt_kv, scalars, parity, d_out):
    n_own = prompt_kv.shape[2] // HD // 2
    z = functools.partial(swap, axis="prefix", step=1)
    core, x, both = [functools.partial(swap, axis="dp", step=k) for k in (1, 2, 3)]
    theirs = (1 - parity) * n_own

    def order(values, done):
        return lax.optimization_barrier((tuple(values), tuple(done)))[0]

    a0, b0 = pack(prompt_kv, 1)
    b0 = z(b0)
    a2 = x(a0)
    resp_a, *resp_b = pack(resp_kv, n_own)
    resp_b[0] = z(resp_b[0])
    (ready,) = order([b0], [resp_a])
    b2 = x(ready)
    for h in range(1, n_own):
        resp_b[h] = z(order([resp_b[h]], [b0])[0])
    pa = [a0, core(a0), a2, core(a2)]
    pb = [b0, core(b0), b2, core(b2)]

    shared = None
    d_resp, d_prompt = [], []
    for h in range(n_own):
        final = h == n_own - 1
        here = lambda par, h=h: par * n_own + h
        own = lambda par, h=h: h
        at = lambda par: 0
        att, dq, dra, drb, keep, *sends = attend(
            scalars,
            queries,
            d_out,
            (resp_a, own),
            (resp_b[h], at),
            [(a, own) for a in pa],
            [(b, own) for b in pb],
            (0, 2) if final else (0,),
            ((1, 3),) if final else ((1,), (2,), (3,)),
            h,
            GROUP,
            shared,
            (resp_kv, here),
        )
        shared = (att, dq, dra)
        d_resp.append(z(drb))
        if final:
            (send,) = order([sends[0]], arrived)
            sums = keep + core(send).astype(jnp.float32)
            (across,) = order([x(sums[1].astype(jnp.bfloat16))], [d_resp[-1]])
            total = sums[0] + across.astype(jnp.float32)
        else:
            parts = [move(part[0]) for move, part in zip((core, x, both), sends)]
            arrived = [*parts, d_resp[-1]]
            total = keep[0] + sum(p.astype(jnp.float32) for p in parts)
        other = z(total[:, :, HD:].astype(jnp.bfloat16))
        d_prompt.append((total[:, :, :HD], other))

    even = parity == 0
    mine = jnp.concatenate([a for a, _ in d_prompt], axis=-1)
    *others, final = [b.astype(jnp.float32) for _, b in d_prompt]
    other = jnp.concatenate([*others, jnp.zeros_like(final)], axis=-1)
    d_prompt = jnp.concatenate([jnp.where(even, mine, other), jnp.where(even, other, mine)], axis=-1)
    (d_prompt,) = order([d_prompt], [])
    d_prompt = lax.dynamic_update_slice_in_dim(d_prompt, final, (theirs + n_own - 1) * HD, axis=2)
    att, dq, d_resp_kv = shared
    received = jnp.concatenate(d_resp, axis=-1)
    d_resp_kv = lax.dynamic_update_slice_in_dim(d_resp_kv, received, theirs * HD, axis=2)
    return att, dq, d_resp_kv, d_prompt


def shared_head(queries, resp_kv, prompt_kv, scalars, parity, d_out):
    first = lambda par: 0
    prompt_a = lax.all_gather(prompt_kv, "dp", axis=1, tiled=True)
    prompt_b = swap(prompt_a, "prefix", 1)
    resp_b = swap(resp_kv, "prefix", 1)
    att, dq, dra, drb, keep = attend(
        scalars,
        queries,
        d_out,
        (resp_kv, first),
        (resp_b, first),
        [(prompt_a, first)],
        [(prompt_b, first)],
        (0,),
        (),
        0,
        queries.shape[2] // HD,
        None,
        (resp_kv, first),
    )
    d_resp = (dra.astype(jnp.float32) + swap(drb, "prefix", 1).astype(jnp.float32)).astype(jnp.bfloat16)
    other = swap(keep[0, :, :, HD:].astype(jnp.bfloat16), "prefix", 1)
    paired = keep[0, :, :, :HD] + other.astype(jnp.float32)
    d_prompt = lax.psum_scatter(paired, "dp", scatter_dimension=1, tiled=True)
    return att, dq, d_resp, d_prompt


def solution(mesh):
    in_specs = (
        P(("groups", "dp"), None, "prefix"),
        P(("groups", "dp"), None, "prefix"),
        P("groups", "dp", "prefix"),
        P(("groups", "dp")),
        P(("groups", "dp"), None, "prefix"),
    )
    out_specs = (
        P(("groups", "dp"), None, "prefix"),
        P(("groups", "dp"), None, "prefix"),
        P(("groups", "dp"), None, "prefix"),
        P("groups", "dp", "prefix"),
    )
    return jax.shard_map(
        per_device, mesh=mesh, in_specs=in_specs, out_specs=out_specs, check_vma=False
    )
```

```python
import functools

import jax
import jax.numpy as jnp
from jax import lax
from jax.experimental import pallas as pl
from jax.experimental.pallas import tpu as pltpu
from jax.sharding import PartitionSpec as P

H = 32
KVH = 8
HD = 128
P_SIZE = 2
GROUP = H // KVH
BLOCK = 256
STRIP = 16
PAIR = 2
MASKED = -1e30
SCALE = HD ** (-0.5)

NT = (((1,), (1,)), ((), ()))
NN = (((1,), (0,)), ((), ()))


def dot(a, b, dims):
    return lax.dot_general(a, b, dims, preferred_element_type=jnp.float32)


def swap(block, axis, step):
    return lax.ppermute(block, axis, [(i, i ^ step) for i in range(lax.axis_size(axis))])


def attend_kernel(sizes, scalars, *refs):
    pieces, rows, keep, sends, n_pass = sizes
    refs = list(refs)
    q_ref, do_ref, ra_ref, rb_ref = refs[:4]
    pa_refs = refs[4 : 4 + pieces]
    pb_refs = refs[4 + pieces : 4 + 2 * pieces]
    rest = refs[4 + 2 * pieces + n_pass :]
    out_ref, dq_ref, dra_ref, drb_ref, keep_ref = rest[:5]
    send_refs = rest[5 : 5 + len(sends)]
    k_all, v_all, q_all, do_all, q_t, do_t, scores, grad_probs, probs, dscores, acc_k, acc_v, sum_k, sum_v = rest[5 + len(sends) :]

    r = pl.program_id(0)
    head = pl.program_id(1)
    n_resp = pl.num_programs(0)
    last = head == pl.num_programs(1) - 1
    prompt = scalars[r]
    even = scalars[n_resp] == 0
    n_prompt = pieces * rows
    n_query = q_ref.shape[1]
    n_blocks = n_query // BLOCK

    def gather(dst, piece_refs, resp_ref):
        for i, ref in enumerate(piece_refs):
            dst[i * rows : (i + 1) * rows, :] = ref[0]
        dst[n_prompt:, :] = resp_ref[0]

    @pl.when((head == 0) & even)
    def _():
        gather(k_all, pa_refs, ra_ref)
        gather(v_all, pb_refs, rb_ref)

    @pl.when((head == 0) & jnp.logical_not(even))
    def _():
        gather(k_all, pb_refs, rb_ref)
        gather(v_all, pa_refs, ra_ref)

    @pl.when(head == 0)
    def _():
        acc_k[...] = jnp.zeros_like(acc_k)
        acc_v[...] = jnp.zeros_like(acc_v)

    size = PAIR * BLOCK

    for i in range(n_blocks):
        for j in range(PAIR):
            at = slice(i * size + j * BLOCK, i * size + (j + 1) * BLOCK)
            from_t, lanes = slice(i * BLOCK, (i + 1) * BLOCK), slice(j * HD, (j + 1) * HD)
            q_all[at, :] = q_ref[0, from_t, lanes]
            do_all[at, :] = do_ref[0, from_t, lanes]

    def seeing(u):
        return slice(max(u - n_prompt, 0) // BLOCK * size, n_blocks * size)

    def score(u):
        t = seeing(u)
        scores[t, u : u + BLOCK] = dot(q_all[t, :], k_all[u : u + BLOCK, :], NT)

    def grad_prob(u):
        t = seeing(u)
        grad_probs[t, u : u + BLOCK] = dot(do_all[t, :], v_all[u : u + BLOCK, :], NT)

    def grad_value(u):
        t = seeing(u)
        acc_v[:, u : u + BLOCK] += dot(do_t[:, t], probs[t, u : u + BLOCK], NN)

    def grad_key(u):
        t = seeing(u)
        acc_k[:, u : u + BLOCK] += dot(q_t[:, t], dscores[t, u : u + BLOCK], NN)

    def turn():
        q_t[...] = q_all[...].T
        do_t[...] = do_all[...].T

    def stages(i):
        st = {}
        t0 = i * size
        t = slice(t0, t0 + size)
        edge = n_prompt + i * BLOCK
        seen = edge + BLOCK

        def put(ref, rows_out):
            for j in range(PAIR):
                part = rows_out[j * BLOCK : (j + 1) * BLOCK].astype(jnp.bfloat16)
                ref[0, i * BLOCK : (i + 1) * BLOCK, j * HD : (j + 1) * HD] = part

        def softmax(row):
            at = slice(t0 + row, t0 + row + STRIP)
            left = scores[at, :edge]
            rows_at = lax.broadcasted_iota(jnp.int32, (STRIP, BLOCK), 0) + row % BLOCK
            columns = lax.broadcasted_iota(jnp.int32, (STRIP, BLOCK), 1)
            right = jnp.where(columns <= rows_at, scores[at, edge:seen], MASKED)
            top = jnp.maximum(jnp.max(left, axis=1, keepdims=True), jnp.max(right, axis=1, keepdims=True)) * SCALE
            left = jnp.exp(left * SCALE - top)
            right = jnp.exp(right * SCALE - top)
            inv = 1.0 / (jnp.sum(left, axis=1, keepdims=True) + jnp.sum(right, axis=1, keepdims=True))
            for part, u in ((left * inv, slice(0, edge)), (right * inv, slice(edge, seen))):
                scores[at, u] = part
                probs[at, u] = part.astype(jnp.bfloat16)

        def output():
            o = dot(probs[t, :seen], v_all[:seen, :], NN)
            put(out_ref, o)
            st["delta"] = jnp.sum(o * do_all[t, :].astype(jnp.float32), axis=1, keepdims=True)

        def grad_score(row):
            at = slice(t0 + row, t0 + row + STRIP)
            delta = st["delta"][row : row + STRIP]
            ds = (scores[at, :seen] * SCALE) * (grad_probs[at, :seen] - delta)
            dscores[at, :seen] = ds.astype(jnp.bfloat16)

        def query():
            put(dq_ref, dot(dscores[t, :seen], k_all[:seen, :], NN))

        strips = range(0, size, STRIP)
        each = lambda f: [functools.partial(f, x) for x in strips]
        return {"softmax": each(softmax), "output": [output], "grad": each(grad_score), "query": [query]}

    def mix(*lists):
        order = [((at + 0.5) / len(x), k, f) for k, x in enumerate(lists) for at, f in enumerate(x)]
        for _, _, f in sorted(order, key=lambda e: e[:2]):
            f()

    plan = [stages(i) for i in range(n_blocks)]
    over = lambda f: [functools.partial(f, u) for u in range(0, n_prompt + n_query, BLOCK)]
    mix(over(score), [turn])
    mix(plan[0]["softmax"], over(grad_prob))
    for i in range(1, n_blocks):
        mix(plan[i]["softmax"], plan[i - 1]["output"])
        mix(plan[i - 1]["grad"], plan[i]["output"] if i == n_blocks - 1 else [])
    if n_blocks == 1:
        mix(plan[0]["output"])
    mix(plan[-1]["grad"], *[p["query"] for p in plan[:-1]], over(grad_value))
    mix(plan[-1]["query"], over(grad_key))

    def respond(ref, acc):
        ref[0] = acc[:, n_prompt:].T.astype(jnp.bfloat16)

    @pl.when(last & even)
    def _():
        respond(dra_ref, acc_k)
        respond(drb_ref, acc_v)

    @pl.when(last & jnp.logical_not(even))
    def _():
        respond(dra_ref, acc_v)
        respond(drb_ref, acc_k)

    @pl.when(last & (r == 0))
    def _():
        for whole, acc in ((sum_k, acc_k), (sum_v, acc_v)):
            whole[prompt] = acc[:, :n_prompt].T
            whole[1 - prompt] = jnp.zeros((n_prompt, HD), jnp.float32)

    @pl.when(last & (r > 0))
    def _():
        for whole, acc in ((sum_k, acc_k), (sum_v, acc_v)):
            whole[prompt] += acc[:, :n_prompt].T

    done = last & (r == n_resp - 1)

    def scatter(slot, whole):
        lanes = slice(slot * HD, (slot + 1) * HD)
        for ref, group in ((keep_ref, keep), *zip(send_refs, sends)):
            for at, i in enumerate(group):
                ref[at, :, :, lanes] = whole[:, i * rows : (i + 1) * rows, :].astype(ref.dtype)

    @pl.when(done & even)
    def _():
        scatter(0, sum_k)
        scatter(1, sum_v)

    @pl.when(done & jnp.logical_not(even))
    def _():
        scatter(0, sum_v)
        scatter(1, sum_k)


def attend(scalars, queries, d_out, resp_a, resp_b, prompt_a, prompt_b, keep, sends, chunk, heads, shared, own):
    n_resp, n_query, _ = queries.shape
    pieces = len(prompt_a)
    rows = prompt_a[0][0].shape[1]
    n_prompt = pieces * rows
    n_keys = n_prompt + n_query
    shape = jax.ShapeDtypeStruct

    def resp_map(column):
        return lambda r, j, sc: (r, 0, column(sc[n_resp]))

    def prompt_map(column):
        return lambda r, j, sc: (sc[r], 0, column(sc[n_resp]))

    steps = heads // PAIR
    n_rows = PAIR * n_query
    q_spec = pl.BlockSpec((1, n_query, PAIR * HD), lambda r, j, sc: (r, 0, chunk * steps + j))
    in_specs = [q_spec, q_spec]
    in_specs += [pl.BlockSpec((1, n_query, HD), resp_map(c)) for _, c in (resp_a, resp_b)]
    in_specs += [pl.BlockSpec((1, rows, HD), prompt_map(c)) for _, c in (*prompt_a, *prompt_b)]
    args = [queries, d_out, resp_a[0], resp_b[0], *[a for a, _ in (*prompt_a, *prompt_b)]]
    aliases = {}
    if shared is not None:
        aliases = {1 + len(args) + i: i for i in range(3)}
        args += list(shared)
    n_pass = len(args) - len(in_specs)
    in_specs += [pl.BlockSpec(memory_space=pl.ANY)] * n_pass
    grads = [shape((len(keep), P_SIZE, rows, 2 * HD), jnp.float32)]
    grads += [shape((len(g), P_SIZE, rows, 2 * HD), jnp.bfloat16) for g in sends]
    out_specs = [
        q_spec,
        q_spec,
        pl.BlockSpec((1, n_query, HD), resp_map(own[1])),
        pl.BlockSpec((1, n_query, HD), lambda r, j, sc: (r, 0, 0)),
    ]
    out_specs += [pl.BlockSpec(g.shape, lambda r, j, sc: (0, 0, 0, 0)) for g in grads]
    out_shape = [
        shape(queries.shape, jnp.bfloat16),
        shape(queries.shape, jnp.bfloat16),
        shape(own[0].shape, jnp.bfloat16),
        shape((n_resp, n_query, HD), jnp.bfloat16),
    ] + grads
    scratch = [
        pltpu.VMEM((n_keys, HD), jnp.bfloat16),
        pltpu.VMEM((n_keys, HD), jnp.bfloat16),
        pltpu.VMEM((n_rows, HD), jnp.bfloat16),
        pltpu.VMEM((n_rows, HD), jnp.bfloat16),
        pltpu.VMEM((HD, n_rows), jnp.bfloat16),
        pltpu.VMEM((HD, n_rows), jnp.bfloat16),
        pltpu.VMEM((n_rows, n_keys), jnp.float32),
        pltpu.VMEM((n_rows, n_keys), jnp.float32),
        pltpu.VMEM((n_rows, n_keys), jnp.bfloat16),
        pltpu.VMEM((n_rows, n_keys), jnp.bfloat16),
        pltpu.VMEM((HD, n_keys), jnp.float32),
        pltpu.VMEM((HD, n_keys), jnp.float32),
        pltpu.VMEM((P_SIZE, n_prompt, HD), jnp.float32),
        pltpu.VMEM((P_SIZE, n_prompt, HD), jnp.float32),
    ]
    flops = 12 * n_resp * heads * n_query * n_keys * HD
    return pl.pallas_call(
        functools.partial(attend_kernel, (pieces, rows, keep, sends, n_pass)),
        grid_spec=pltpu.PrefetchScalarGridSpec(
            num_scalar_prefetch=1,
            grid=(n_resp, steps),
            in_specs=in_specs,
            out_specs=out_specs,
            scratch_shapes=scratch,
        ),
        out_shape=out_shape,
        input_output_aliases=aliases,
        compiler_params=pltpu.CompilerParams(vmem_limit_bytes=48 * 2**20),
        cost_estimate=pl.CostEstimate(flops=2 * flops, bytes_accessed=4 * 2**20, transcendentals=0),
    )(scalars, *args)


def pack_kernel(n_own, n_resp, scalars, prompt_ref, resp_ref, *outs):
    width = n_own * HD

    def split(own):
        for h in range(n_own):
            mine = slice(own + h * HD, own + (h + 1) * HD)
            theirs = slice(width - own + h * HD, width - own + (h + 1) * HD)
            for k, (ref, lanes) in enumerate(
                ((prompt_ref, mine), (prompt_ref, theirs), (resp_ref, mine), (resp_ref, theirs))
            ):
                outs[4 * h + k][...] = ref[:, :, lanes]

    @pl.when(scalars[n_resp] == 0)
    def _():
        split(0)

    @pl.when(scalars[n_resp] != 0)
    def _():
        split(width)


def pack(scalars, prompt_kv, resp_kv, n_own):
    block = lambda shape: pl.BlockSpec(shape, lambda i, sc: (0, 0, 0))
    shapes = [x.shape[:2] + (HD,) for x in (prompt_kv, prompt_kv, resp_kv, resp_kv)] * n_own
    return pl.pallas_call(
        functools.partial(pack_kernel, n_own, resp_kv.shape[0]),
        grid_spec=pltpu.PrefetchScalarGridSpec(
            num_scalar_prefetch=1,
            grid=(1,),
            in_specs=[block(prompt_kv.shape), block(resp_kv.shape)],
            out_specs=[block(s) for s in shapes],
        ),
        out_shape=[jax.ShapeDtypeStruct(s, prompt_kv.dtype) for s in shapes],
        compiler_params=pltpu.CompilerParams(vmem_limit_bytes=48 * 2**20),
    )(scalars, prompt_kv, resp_kv)


def per_device(queries, resp_kv, prompt_kv, prompt_of, d_out):
    pair_heads = prompt_kv.shape[2] // HD
    parity = lax.axis_index("prefix") % 2
    scalars = jnp.concatenate([prompt_of, parity[None].astype(jnp.int32)])
    if lax.axis_size("dp") == 4 and pair_heads % 2 == 0:
        return whole_heads(queries, resp_kv, prompt_kv, scalars, parity, d_out)
    return shared_head(queries, resp_kv, prompt_kv, scalars, parity, d_out)


def whole_heads(queries, resp_kv, prompt_kv, scalars, parity, d_out):
    n_own = prompt_kv.shape[2] // HD // 2
    z = functools.partial(swap, axis="prefix", step=1)
    core, x, both = [functools.partial(swap, axis="dp", step=k) for k in (1, 2, 3)]
    theirs = (1 - parity) * n_own

    def order(values, done):
        return lax.optimization_barrier((tuple(values), tuple(done)))[0]

    packed = pack(scalars, prompt_kv, resp_kv, n_own)
    pa, pb, resp_a, resp_b = [], [], [], []
    for h in range(n_own):
        a0, b0, ra, rb = packed[4 * h : 4 * h + 4]
        if h > 0:
            (rb,) = order([rb], [resp_b[h - 1]])
        b0 = z(b0)
        a2 = x(a0)
        resp_a.append(ra)
        resp_b.append(z(rb))
        if h == 0:
            (ready,) = order([b0], [a2])
        else:
            (ready,) = order([b0], [pb[0][2]])
        b2 = x(ready)
        pa.append([a0, core(a0), a2, core(a2) if h == 0 else None])
        pb.append([b0, core(b0), b2, core(b2) if h == 0 else None])

    shared = None
    d_resp, d_prompt = [], []
    for h in range(n_own):
        final = h == n_own - 1
        here = lambda par, h=h: par * n_own + h
        at = lambda par: 0
        att, dq, dra, drb, keep, *sends = attend(
            scalars,
            queries,
            d_out,
            (resp_a[h], at),
            (resp_b[h], at),
            [(a, at) for a in pa[h]],
            [(b, at) for b in pb[h]],
            (0, 2) if final else (0,),
            ((1, 3),) if final else ((1,), (2,), (3,)),
            h,
            GROUP,
            shared,
            (resp_kv, here),
        )
        shared = (att, dq, dra)
        d_resp.append(z(drb))
        if not final:
            pa[h + 1][3], pb[h + 1][3] = [core(v) for v in order([pa[h + 1][2], pb[h + 1][2]], [drb])]
        if final:
            (send,) = order([sends[0]], arrived)
            sums = keep + core(send).astype(jnp.float32)
            (across,) = order([x(sums[1].astype(jnp.bfloat16))], [d_resp[-1]])
            total = sums[0] + across.astype(jnp.float32)
        else:
            parts = [move(part[0]) for move, part in zip((core, x, both), sends)]
            arrived = [*parts, d_resp[-1]]
            total = keep[0] + sum(p.astype(jnp.float32) for p in parts)
        other = z(total[:, :, HD:].astype(jnp.bfloat16))
        d_prompt.append((total[:, :, :HD], other))

    even = parity == 0
    mine = jnp.concatenate([a for a, _ in d_prompt], axis=-1)
    other = jnp.concatenate([b.astype(jnp.float32) for _, b in d_prompt], axis=-1)
    d_prompt = jnp.concatenate([jnp.where(even, mine, other), jnp.where(even, other, mine)], axis=-1)
    att, dq, d_resp_kv = shared
    received = jnp.concatenate(d_resp, axis=-1)
    d_resp_kv = lax.dynamic_update_slice_in_dim(d_resp_kv, received, theirs * HD, axis=2)
    return att, dq, d_resp_kv, d_prompt


def shared_head(queries, resp_kv, prompt_kv, scalars, parity, d_out):
    first = lambda par: 0
    prompt_a = lax.all_gather(prompt_kv, "dp", axis=1, tiled=True)
    prompt_b = swap(prompt_a, "prefix", 1)
    resp_b = swap(resp_kv, "prefix", 1)
    att, dq, dra, drb, keep = attend(
        scalars,
        queries,
        d_out,
        (resp_kv, first),
        (resp_b, first),
        [(prompt_a, first)],
        [(prompt_b, first)],
        (0,),
        (),
        0,
        queries.shape[2] // HD,
        None,
        (resp_kv, first),
    )
    d_resp = (dra.astype(jnp.float32) + swap(drb, "prefix", 1).astype(jnp.float32)).astype(jnp.bfloat16)
    other = swap(keep[0, :, :, HD:].astype(jnp.bfloat16), "prefix", 1)
    paired = keep[0, :, :, :HD] + other.astype(jnp.float32)
    d_prompt = lax.psum_scatter(paired, "dp", scatter_dimension=1, tiled=True)
    return att, dq, d_resp, d_prompt


def solution(mesh):
    in_specs = (
        P(("groups", "dp"), None, "prefix"),
        P(("groups", "dp"), None, "prefix"),
        P("groups", "dp", "prefix"),
        P(("groups", "dp")),
        P(("groups", "dp"), None, "prefix"),
    )
    out_specs = (
        P(("groups", "dp"), None, "prefix"),
        P(("groups", "dp"), None, "prefix"),
        P(("groups", "dp"), None, "prefix"),
        P("groups", "dp", "prefix"),
    )
    return jax.shard_map(
        per_device, mesh=mesh, in_specs=in_specs, out_specs=out_specs, check_vma=False
    )
```

```python
import functools

import jax
import jax.numpy as jnp
from jax import lax
from jax.experimental import pallas as pl
from jax.experimental.pallas import tpu as pltpu
from jax.sharding import PartitionSpec as P

H = 32
KVH = 8
HD = 128
P_SIZE = 2
GROUP = H // KVH
BLOCK = 256
STRIP = 16
PAIR = 2
MASKED = -1e30
SCALE = HD ** (-0.5)

NT = (((1,), (1,)), ((), ()))
NN = (((1,), (0,)), ((), ()))


def dot(a, b, dims):
    return lax.dot_general(a, b, dims, preferred_element_type=jnp.float32)


def swap(block, axis, step):
    return lax.ppermute(block, axis, [(i, i ^ step) for i in range(lax.axis_size(axis))])


def attend_kernel(sizes, scalars, *refs):
    pieces, rows, keep, sends, n_pass = sizes
    refs = list(refs)
    q_ref, do_ref, ra_ref, rb_ref = refs[:4]
    pa_refs = refs[4 : 4 + pieces]
    pb_refs = refs[4 + pieces : 4 + 2 * pieces]
    rest = refs[4 + 2 * pieces + n_pass :]
    out_ref, dq_ref, dra_ref, drb_ref, keep_ref = rest[:5]
    send_refs = rest[5 : 5 + len(sends)]
    k_all, v_all, q_all, do_all, q_t, do_t, scores, grad_probs, probs, dscores, acc_k, acc_v, sum_k, sum_v = rest[5 + len(sends) :]

    r = pl.program_id(0)
    head = pl.program_id(1)
    n_resp = pl.num_programs(0)
    last = head == pl.num_programs(1) - 1
    prompt = scalars[r]
    even = scalars[n_resp] == 0
    n_prompt = pieces * rows
    n_query = q_ref.shape[1]
    n_blocks = n_query // BLOCK

    def gather(dst, piece_refs, resp_ref):
        for i, ref in enumerate(piece_refs):
            dst[i * rows : (i + 1) * rows, :] = ref[0]
        dst[n_prompt:, :] = resp_ref[0]

    @pl.when((head == 0) & even)
    def _():
        gather(k_all, pa_refs, ra_ref)
        gather(v_all, pb_refs, rb_ref)

    @pl.when((head == 0) & jnp.logical_not(even))
    def _():
        gather(k_all, pb_refs, rb_ref)
        gather(v_all, pa_refs, ra_ref)

    @pl.when(head == 0)
    def _():
        acc_k[...] = jnp.zeros_like(acc_k)
        acc_v[...] = jnp.zeros_like(acc_v)

    size = PAIR * BLOCK

    for i in range(n_blocks):
        for j in range(PAIR):
            at = slice(i * size + j * BLOCK, i * size + (j + 1) * BLOCK)
            from_t, lanes = slice(i * BLOCK, (i + 1) * BLOCK), slice(j * HD, (j + 1) * HD)
            q_all[at, :] = q_ref[0, from_t, lanes]
            do_all[at, :] = do_ref[0, from_t, lanes]

    def seeing(u):
        return slice(max(u - n_prompt, 0) // BLOCK * size, n_blocks * size)

    def score(u):
        t = seeing(u)
        scores[t, u : u + BLOCK] = dot(q_all[t, :], k_all[u : u + BLOCK, :], NT)

    def grad_prob(u):
        t = seeing(u)
        grad_probs[t, u : u + BLOCK] = dot(do_all[t, :], v_all[u : u + BLOCK, :], NT)

    def grad_value(u):
        t = seeing(u)
        acc_v[:, u : u + BLOCK] += dot(do_t[:, t], probs[t, u : u + BLOCK], NN)

    def grad_key(u):
        t = seeing(u)
        acc_k[:, u : u + BLOCK] += dot(q_t[:, t], dscores[t, u : u + BLOCK], NN)

    def turn():
        q_t[...] = q_all[...].T
        do_t[...] = do_all[...].T

    def stages(i):
        st = {}
        t0 = i * size
        t = slice(t0, t0 + size)
        edge = n_prompt + i * BLOCK
        seen = edge + BLOCK

        def put(ref, rows_out):
            for j in range(PAIR):
                part = rows_out[j * BLOCK : (j + 1) * BLOCK].astype(jnp.bfloat16)
                ref[0, i * BLOCK : (i + 1) * BLOCK, j * HD : (j + 1) * HD] = part

        def softmax(row):
            at = slice(t0 + row, t0 + row + STRIP)
            left = scores[at, :edge]
            rows_at = lax.broadcasted_iota(jnp.int32, (STRIP, BLOCK), 0) + row % BLOCK
            columns = lax.broadcasted_iota(jnp.int32, (STRIP, BLOCK), 1)
            right = jnp.where(columns <= rows_at, scores[at, edge:seen], MASKED)
            top = jnp.maximum(jnp.max(left, axis=1, keepdims=True), jnp.max(right, axis=1, keepdims=True)) * SCALE
            left = jnp.exp(left * SCALE - top)
            right = jnp.exp(right * SCALE - top)
            inv = 1.0 / (jnp.sum(left, axis=1, keepdims=True) + jnp.sum(right, axis=1, keepdims=True))
            for part, u in ((left * inv, slice(0, edge)), (right * inv, slice(edge, seen))):
                scores[at, u] = part
                probs[at, u] = part.astype(jnp.bfloat16)

        def output():
            o = dot(probs[t, :seen], v_all[:seen, :], NN)
            put(out_ref, o)
            st["delta"] = jnp.sum(o * do_all[t, :].astype(jnp.float32), axis=1, keepdims=True)

        def grad_score(row):
            at = slice(t0 + row, t0 + row + STRIP)
            delta = st["delta"][row : row + STRIP]
            ds = (scores[at, :seen] * SCALE) * (grad_probs[at, :seen] - delta)
            dscores[at, :seen] = ds.astype(jnp.bfloat16)

        def query():
            put(dq_ref, dot(dscores[t, :seen], k_all[:seen, :], NN))

        strips = range(0, size, STRIP)
        each = lambda f: [functools.partial(f, x) for x in strips]
        return {"softmax": each(softmax), "output": [output], "grad": each(grad_score), "query": [query]}

    def mix(*lists):
        order = [((at + 0.5) / len(x), k, f) for k, x in enumerate(lists) for at, f in enumerate(x)]
        for _, _, f in sorted(order, key=lambda e: e[:2]):
            f()

    plan = [stages(i) for i in range(n_blocks)]
    over = lambda f: [functools.partial(f, u) for u in range(0, n_prompt + n_query, BLOCK)]
    mix(over(score), [turn])
    mix(plan[0]["softmax"], over(grad_prob))
    for i in range(1, n_blocks):
        mix(plan[i]["softmax"], plan[i - 1]["output"])
        mix(plan[i - 1]["grad"], plan[i]["output"] if i == n_blocks - 1 else [])
    if n_blocks == 1:
        mix(plan[0]["output"])
    mix(plan[-1]["grad"], *[p["query"] for p in plan[:-1]], over(grad_value))
    mix(plan[-1]["query"], over(grad_key))

    def respond(ref, acc):
        ref[0] = acc[:, n_prompt:].T.astype(jnp.bfloat16)

    @pl.when(last & even)
    def _():
        respond(dra_ref, acc_k)
        respond(drb_ref, acc_v)

    @pl.when(last & jnp.logical_not(even))
    def _():
        respond(dra_ref, acc_v)
        respond(drb_ref, acc_k)

    @pl.when(last & (r == 0))
    def _():
        for whole, acc in ((sum_k, acc_k), (sum_v, acc_v)):
            whole[prompt] = acc[:, :n_prompt].T
            whole[1 - prompt] = jnp.zeros((n_prompt, HD), jnp.float32)

    @pl.when(last & (r > 0))
    def _():
        for whole, acc in ((sum_k, acc_k), (sum_v, acc_v)):
            whole[prompt] += acc[:, :n_prompt].T

    done = last & (r == n_resp - 1)

    def scatter(slot, whole):
        lanes = slice(slot * HD, (slot + 1) * HD)
        for ref, group in ((keep_ref, keep), *zip(send_refs, sends)):
            for at, i in enumerate(group):
                ref[at, :, :, lanes] = whole[:, i * rows : (i + 1) * rows, :].astype(ref.dtype)

    @pl.when(done & even)
    def _():
        scatter(0, sum_k)
        scatter(1, sum_v)

    @pl.when(done & jnp.logical_not(even))
    def _():
        scatter(0, sum_v)
        scatter(1, sum_k)


def attend(scalars, queries, d_out, resp_a, resp_b, prompt_a, prompt_b, keep, sends, chunk, heads, shared, own):
    n_resp, n_query, _ = queries.shape
    pieces = len(prompt_a)
    rows = prompt_a[0][0].shape[1]
    n_prompt = pieces * rows
    n_keys = n_prompt + n_query
    shape = jax.ShapeDtypeStruct

    def resp_map(column):
        return lambda r, j, sc: (r, 0, column(sc[n_resp]))

    def prompt_map(column):
        return lambda r, j, sc: (sc[r], 0, column(sc[n_resp]))

    steps = heads // PAIR
    n_rows = PAIR * n_query
    q_spec = pl.BlockSpec((1, n_query, PAIR * HD), lambda r, j, sc: (r, 0, chunk * steps + j))
    in_specs = [q_spec, q_spec]
    in_specs += [pl.BlockSpec((1, n_query, HD), resp_map(c)) for _, c in (resp_a, resp_b)]
    in_specs += [pl.BlockSpec((1, rows, HD), prompt_map(c)) for _, c in (*prompt_a, *prompt_b)]
    args = [queries, d_out, resp_a[0], resp_b[0], *[a for a, _ in (*prompt_a, *prompt_b)]]
    aliases = {}
    if shared is not None:
        aliases = {1 + len(args) + i: i for i in range(3)}
        args += list(shared)
    n_pass = len(args) - len(in_specs)
    in_specs += [pl.BlockSpec(memory_space=pl.ANY)] * n_pass
    grads = [shape((len(keep), P_SIZE, rows, 2 * HD), jnp.float32)]
    grads += [shape((len(g), P_SIZE, rows, 2 * HD), jnp.bfloat16) for g in sends]
    out_specs = [
        q_spec,
        q_spec,
        pl.BlockSpec((1, n_query, HD), resp_map(own[1])),
        pl.BlockSpec((1, n_query, HD), lambda r, j, sc: (r, 0, 0)),
    ]
    out_specs += [pl.BlockSpec(g.shape, lambda r, j, sc: (0, 0, 0, 0)) for g in grads]
    out_shape = [
        shape(queries.shape, jnp.bfloat16),
        shape(queries.shape, jnp.bfloat16),
        shape(own[0].shape, jnp.bfloat16),
        shape((n_resp, n_query, HD), jnp.bfloat16),
    ] + grads
    scratch = [
        pltpu.VMEM((n_keys, HD), jnp.bfloat16),
        pltpu.VMEM((n_keys, HD), jnp.bfloat16),
        pltpu.VMEM((n_rows, HD), jnp.bfloat16),
        pltpu.VMEM((n_rows, HD), jnp.bfloat16),
        pltpu.VMEM((HD, n_rows), jnp.bfloat16),
        pltpu.VMEM((HD, n_rows), jnp.bfloat16),
        pltpu.VMEM((n_rows, n_keys), jnp.float32),
        pltpu.VMEM((n_rows, n_keys), jnp.float32),
        pltpu.VMEM((n_rows, n_keys), jnp.bfloat16),
        pltpu.VMEM((n_rows, n_keys), jnp.bfloat16),
        pltpu.VMEM((HD, n_keys), jnp.float32),
        pltpu.VMEM((HD, n_keys), jnp.float32),
        pltpu.VMEM((P_SIZE, n_prompt, HD), jnp.float32),
        pltpu.VMEM((P_SIZE, n_prompt, HD), jnp.float32),
    ]
    flops = 12 * n_resp * heads * n_query * n_keys * HD
    return pl.pallas_call(
        functools.partial(attend_kernel, (pieces, rows, keep, sends, n_pass)),
        grid_spec=pltpu.PrefetchScalarGridSpec(
            num_scalar_prefetch=1,
            grid=(n_resp, steps),
            in_specs=in_specs,
            out_specs=out_specs,
            scratch_shapes=scratch,
        ),
        out_shape=out_shape,
        input_output_aliases=aliases,
        compiler_params=pltpu.CompilerParams(vmem_limit_bytes=48 * 2**20),
        cost_estimate=pl.CostEstimate(flops=2 * flops, bytes_accessed=4 * 2**20, transcendentals=0),
    )(scalars, *args)


def pack_kernel(n_own, prompt_ref, resp_ref, *outs):
    width = n_own * HD

    def split(own):
        for h in range(n_own):
            mine = slice(own + h * HD, own + (h + 1) * HD)
            theirs = slice(width - own + h * HD, width - own + (h + 1) * HD)
            for k, (ref, lanes) in enumerate(
                ((prompt_ref, mine), (prompt_ref, theirs), (resp_ref, mine), (resp_ref, theirs))
            ):
                outs[4 * h + k][...] = ref[:, :, lanes]

    parity = lax.axis_index("prefix") % 2

    @pl.when(parity == 0)
    def _():
        split(0)

    @pl.when(parity != 0)
    def _():
        split(width)


def pack(prompt_kv, resp_kv, n_own):
    block = lambda shape: pl.BlockSpec(shape, lambda i: (0, 0, 0))
    shapes = [x.shape[:2] + (HD,) for x in (prompt_kv, prompt_kv, resp_kv, resp_kv)] * n_own
    return pl.pallas_call(
        functools.partial(pack_kernel, n_own),
        grid=(1,),
        in_specs=[block(prompt_kv.shape), block(resp_kv.shape)],
        out_specs=[block(s) for s in shapes],
        out_shape=[jax.ShapeDtypeStruct(s, prompt_kv.dtype) for s in shapes],
        compiler_params=pltpu.CompilerParams(vmem_limit_bytes=48 * 2**20),
    )(prompt_kv, resp_kv)


def per_device(queries, resp_kv, prompt_kv, prompt_of, d_out):
    pair_heads = prompt_kv.shape[2] // HD
    parity = lax.axis_index("prefix") % 2
    scalars = jnp.concatenate([prompt_of, parity[None].astype(jnp.int32)])
    if lax.axis_size("dp") == 4 and pair_heads % 2 == 0:
        return whole_heads(queries, resp_kv, prompt_kv, scalars, parity, d_out)
    return shared_head(queries, resp_kv, prompt_kv, scalars, parity, d_out)


def whole_heads(queries, resp_kv, prompt_kv, scalars, parity, d_out):
    n_own = prompt_kv.shape[2] // HD // 2
    z = functools.partial(swap, axis="prefix", step=1)
    core, x, both = [functools.partial(swap, axis="dp", step=k) for k in (1, 2, 3)]
    theirs = (1 - parity) * n_own

    def order(values, done):
        return lax.optimization_barrier((tuple(values), tuple(done)))[0]

    packed = pack(prompt_kv, resp_kv, n_own)
    pa, pb, resp_a, resp_b = [], [], [], []
    for h in range(n_own):
        a0, b0, ra, rb = packed[4 * h : 4 * h + 4]
        if h > 0:
            (rb,) = order([rb], [resp_b[h - 1]])
        b0 = z(b0)
        a2 = x(a0)
        if h == 0:
            (rb,) = order([rb], [b0])
        resp_a.append(ra)
        resp_b.append(z(rb))
        if h == 0:
            (ready,) = order([b0], [a2])
        else:
            (ready,) = order([b0], [pb[0][2]])
        b2 = x(ready)
        pa.append([a0, core(a0), a2, core(a2) if h == 0 else None])
        pb.append([b0, core(b0), b2, core(b2) if h == 0 else None])

    shared = None
    d_resp, d_prompt = [], []
    for h in range(n_own):
        final = h == n_own - 1
        here = lambda par, h=h: par * n_own + h
        at = lambda par: 0
        att, dq, dra, drb, keep, *sends = attend(
            scalars,
            queries,
            d_out,
            (resp_a[h], at),
            (resp_b[h], at),
            [(a, at) for a in pa[h]],
            [(b, at) for b in pb[h]],
            (0, 2) if final else (0,),
            ((1, 3),) if final else ((1,), (2,), (3,)),
            h,
            GROUP,
            shared,
            (resp_kv, here),
        )
        shared = (att, dq, dra)
        d_resp.append(z(drb))
        if not final:
            pa[h + 1][3], pb[h + 1][3] = [core(v) for v in order([pa[h + 1][2], pb[h + 1][2]], [drb])]
        if final:
            (send,) = order([sends[0]], arrived)
            sums = keep + core(send).astype(jnp.float32)
            (across,) = order([x(sums[1].astype(jnp.bfloat16))], [d_resp[-1]])
            total = sums[0] + across.astype(jnp.float32)
        else:
            parts = [move(part[0]) for move, part in zip((core, x, both), sends)]
            arrived = [*parts, d_resp[-1]]
            total = keep[0] + sum(p.astype(jnp.float32) for p in parts)
        other = z(total[:, :, HD:].astype(jnp.bfloat16))
        d_prompt.append((total[:, :, :HD], other))

    even = parity == 0
    mine = jnp.concatenate([a for a, _ in d_prompt], axis=-1)
    other = jnp.concatenate([b.astype(jnp.float32) for _, b in d_prompt], axis=-1)
    d_prompt = jnp.concatenate([jnp.where(even, mine, other), jnp.where(even, other, mine)], axis=-1)
    att, dq, d_resp_kv = shared
    received = jnp.concatenate(d_resp, axis=-1)
    d_resp_kv = lax.dynamic_update_slice_in_dim(d_resp_kv, received, theirs * HD, axis=2)
    return att, dq, d_resp_kv, d_prompt


def shared_head(queries, resp_kv, prompt_kv, scalars, parity, d_out):
    first = lambda par: 0
    prompt_a = lax.all_gather(prompt_kv, "dp", axis=1, tiled=True)
    prompt_b = swap(prompt_a, "prefix", 1)
    resp_b = swap(resp_kv, "prefix", 1)
    att, dq, dra, drb, keep = attend(
        scalars,
        queries,
        d_out,
        (resp_kv, first),
        (resp_b, first),
        [(prompt_a, first)],
        [(prompt_b, first)],
        (0,),
        (),
        0,
        queries.shape[2] // HD,
        None,
        (resp_kv, first),
    )
    d_resp = (dra.astype(jnp.float32) + swap(drb, "prefix", 1).astype(jnp.float32)).astype(jnp.bfloat16)
    other = swap(keep[0, :, :, HD:].astype(jnp.bfloat16), "prefix", 1)
    paired = keep[0, :, :, :HD] + other.astype(jnp.float32)
    d_prompt = lax.psum_scatter(paired, "dp", scatter_dimension=1, tiled=True)
    return att, dq, d_resp, d_prompt


def solution(mesh):
    in_specs = (
        P(("groups", "dp"), None, "prefix"),
        P(("groups", "dp"), None, "prefix"),
        P("groups", "dp", "prefix"),
        P(("groups", "dp")),
        P(("groups", "dp"), None, "prefix"),
    )
    out_specs = (
        P(("groups", "dp"), None, "prefix"),
        P(("groups", "dp"), None, "prefix"),
        P(("groups", "dp"), None, "prefix"),
        P("groups", "dp", "prefix"),
    )
    return jax.shard_map(
        per_device, mesh=mesh, in_specs=in_specs, out_specs=out_specs, check_vma=False
    )
```

```python
import functools

import jax
import jax.numpy as jnp
from jax import lax
from jax.experimental import pallas as pl
from jax.experimental.pallas import tpu as pltpu
from jax.sharding import PartitionSpec as P

H = 32
KVH = 8
HD = 128
P_SIZE = 2
GROUP = H // KVH
BLOCK = 256
STRIP = 16
PAIR = 2
MASKED = -1e30
SCALE = HD ** (-0.5)

NT = (((1,), (1,)), ((), ()))
NN = (((1,), (0,)), ((), ()))


def dot(a, b, dims):
    return lax.dot_general(a, b, dims, preferred_element_type=jnp.float32)


def swap(block, axis, step):
    return lax.ppermute(block, axis, [(i, i ^ step) for i in range(lax.axis_size(axis))])


def attend_kernel(sizes, scalars, *refs):
    pieces, rows, keep, sends, n_pass = sizes
    refs = list(refs)
    q_ref, do_ref, ra_ref, rb_ref = refs[:4]
    pa_refs = refs[4 : 4 + pieces]
    pb_refs = refs[4 + pieces : 4 + 2 * pieces]
    rest = refs[4 + 2 * pieces + n_pass :]
    out_ref, dq_ref, dra_ref, drb_ref, keep_ref = rest[:5]
    send_refs = rest[5 : 5 + len(sends)]
    k_all, v_all, q_all, do_all, q_t, do_t, scores, grad_probs, probs, dscores, acc_k, acc_v, sum_k, sum_v = rest[5 + len(sends) :]

    r = pl.program_id(0)
    head = pl.program_id(1)
    n_resp = pl.num_programs(0)
    last = head == pl.num_programs(1) - 1
    prompt = scalars[r]
    even = scalars[n_resp] == 0
    n_prompt = pieces * rows
    n_query = q_ref.shape[1]
    n_blocks = n_query // BLOCK

    def gather(dst, piece_refs, resp_ref):
        for i, ref in enumerate(piece_refs):
            dst[i * rows : (i + 1) * rows, :] = ref[0]
        dst[n_prompt:, :] = resp_ref[0]

    @pl.when((head == 0) & even)
    def _():
        gather(k_all, pa_refs, ra_ref)
        gather(v_all, pb_refs, rb_ref)

    @pl.when((head == 0) & jnp.logical_not(even))
    def _():
        gather(k_all, pb_refs, rb_ref)
        gather(v_all, pa_refs, ra_ref)

    @pl.when(head == 0)
    def _():
        acc_k[...] = jnp.zeros_like(acc_k)
        acc_v[...] = jnp.zeros_like(acc_v)

    size = PAIR * BLOCK

    for i in range(n_blocks):
        for j in range(PAIR):
            at = slice(i * size + j * BLOCK, i * size + (j + 1) * BLOCK)
            from_t, lanes = slice(i * BLOCK, (i + 1) * BLOCK), slice(j * HD, (j + 1) * HD)
            q_all[at, :] = q_ref[0, from_t, lanes]
            do_all[at, :] = do_ref[0, from_t, lanes]

    def seeing(u):
        return slice(max(u - n_prompt, 0) // BLOCK * size, n_blocks * size)

    def score(u):
        t = seeing(u)
        scores[t, u : u + BLOCK] = dot(q_all[t, :], k_all[u : u + BLOCK, :], NT)

    def grad_prob(u):
        t = seeing(u)
        grad_probs[t, u : u + BLOCK] = dot(do_all[t, :], v_all[u : u + BLOCK, :], NT)

    def grad_value(u):
        t = seeing(u)
        acc_v[:, u : u + BLOCK] += dot(do_t[:, t], probs[t, u : u + BLOCK], NN)

    def grad_key(u):
        t = seeing(u)
        acc_k[:, u : u + BLOCK] += dot(q_t[:, t], dscores[t, u : u + BLOCK], NN)

    def turn():
        q_t[...] = q_all[...].T
        do_t[...] = do_all[...].T

    def stages(i):
        st = {}
        t0 = i * size
        t = slice(t0, t0 + size)
        edge = n_prompt + i * BLOCK
        seen = edge + BLOCK

        def put(ref, rows_out):
            for j in range(PAIR):
                part = rows_out[j * BLOCK : (j + 1) * BLOCK].astype(jnp.bfloat16)
                ref[0, i * BLOCK : (i + 1) * BLOCK, j * HD : (j + 1) * HD] = part

        def softmax(row):
            at = slice(t0 + row, t0 + row + STRIP)
            left = scores[at, :edge]
            rows_at = lax.broadcasted_iota(jnp.int32, (STRIP, BLOCK), 0) + row % BLOCK
            columns = lax.broadcasted_iota(jnp.int32, (STRIP, BLOCK), 1)
            right = jnp.where(columns <= rows_at, scores[at, edge:seen], MASKED)
            top = jnp.maximum(jnp.max(left, axis=1, keepdims=True), jnp.max(right, axis=1, keepdims=True)) * SCALE
            left = jnp.exp(left * SCALE - top)
            right = jnp.exp(right * SCALE - top)
            inv = 1.0 / (jnp.sum(left, axis=1, keepdims=True) + jnp.sum(right, axis=1, keepdims=True))
            for part, u in ((left * inv, slice(0, edge)), (right * inv, slice(edge, seen))):
                scores[at, u] = part
                probs[at, u] = part.astype(jnp.bfloat16)

        def output():
            o = dot(probs[t, :seen], v_all[:seen, :], NN)
            put(out_ref, o)
            st["delta"] = jnp.sum(o * do_all[t, :].astype(jnp.float32), axis=1, keepdims=True)

        def grad_score(row):
            at = slice(t0 + row, t0 + row + STRIP)
            delta = st["delta"][row : row + STRIP]
            ds = (scores[at, :seen] * SCALE) * (grad_probs[at, :seen] - delta)
            dscores[at, :seen] = ds.astype(jnp.bfloat16)

        def query():
            put(dq_ref, dot(dscores[t, :seen], k_all[:seen, :], NN))

        strips = range(0, size, STRIP)
        each = lambda f: [functools.partial(f, x) for x in strips]
        return {"softmax": each(softmax), "output": [output], "grad": each(grad_score), "query": [query]}

    def mix(*lists):
        order = [((at + 0.5) / len(x), k, f) for k, x in enumerate(lists) for at, f in enumerate(x)]
        for _, _, f in sorted(order, key=lambda e: e[:2]):
            f()

    plan = [stages(i) for i in range(n_blocks)]
    over = lambda f: [functools.partial(f, u) for u in range(0, n_prompt + n_query, BLOCK)]
    mix(over(score), [turn])
    mix(plan[0]["softmax"], over(grad_prob))
    for i in range(1, n_blocks):
        mix(plan[i]["softmax"], plan[i - 1]["output"])
        mix(plan[i - 1]["grad"], plan[i]["output"] if i == n_blocks - 1 else [])
    if n_blocks == 1:
        mix(plan[0]["output"])
    mix(plan[-1]["grad"], *[p["query"] for p in plan[:-1]], over(grad_value))
    mix(plan[-1]["query"], over(grad_key))

    def respond(ref, acc):
        ref[0] = acc[:, n_prompt:].T.astype(jnp.bfloat16)

    @pl.when(last & even)
    def _():
        respond(dra_ref, acc_k)
        respond(drb_ref, acc_v)

    @pl.when(last & jnp.logical_not(even))
    def _():
        respond(dra_ref, acc_v)
        respond(drb_ref, acc_k)

    @pl.when(last & (r == 0))
    def _():
        for whole, acc in ((sum_k, acc_k), (sum_v, acc_v)):
            whole[prompt] = acc[:, :n_prompt].T
            whole[1 - prompt] = jnp.zeros((n_prompt, HD), jnp.float32)

    @pl.when(last & (r > 0))
    def _():
        for whole, acc in ((sum_k, acc_k), (sum_v, acc_v)):
            whole[prompt] += acc[:, :n_prompt].T

    done = last & (r == n_resp - 1)

    def scatter(slot, whole):
        lanes = slice(slot * HD, (slot + 1) * HD)
        for ref, group in ((keep_ref, keep), *zip(send_refs, sends)):
            for at, i in enumerate(group):
                ref[at, :, :, lanes] = whole[:, i * rows : (i + 1) * rows, :].astype(ref.dtype)

    @pl.when(done & even)
    def _():
        scatter(0, sum_k)
        scatter(1, sum_v)

    @pl.when(done & jnp.logical_not(even))
    def _():
        scatter(0, sum_v)
        scatter(1, sum_k)


def attend(scalars, queries, d_out, resp_a, resp_b, prompt_a, prompt_b, keep, sends, chunk, heads, shared, own):
    n_resp, n_query, _ = queries.shape
    pieces = len(prompt_a)
    rows = prompt_a[0][0].shape[1]
    n_prompt = pieces * rows
    n_keys = n_prompt + n_query
    shape = jax.ShapeDtypeStruct

    def resp_map(column):
        return lambda r, j, sc: (r, 0, column(sc[n_resp]))

    def prompt_map(column):
        return lambda r, j, sc: (sc[r], 0, column(sc[n_resp]))

    steps = heads // PAIR
    n_rows = PAIR * n_query
    q_spec = pl.BlockSpec((1, n_query, PAIR * HD), lambda r, j, sc: (r, 0, chunk * steps + j))
    in_specs = [q_spec, q_spec]
    in_specs += [pl.BlockSpec((1, n_query, HD), resp_map(c)) for _, c in (resp_a, resp_b)]
    in_specs += [pl.BlockSpec((1, rows, HD), prompt_map(c)) for _, c in (*prompt_a, *prompt_b)]
    args = [queries, d_out, resp_a[0], resp_b[0], *[a for a, _ in (*prompt_a, *prompt_b)]]
    aliases = {}
    if shared is not None:
        aliases = {1 + len(args) + i: i for i in range(3)}
        args += list(shared)
    n_pass = len(args) - len(in_specs)
    in_specs += [pl.BlockSpec(memory_space=pl.ANY)] * n_pass
    grads = [shape((len(keep), P_SIZE, rows, 2 * HD), jnp.float32)]
    grads += [shape((len(g), P_SIZE, rows, 2 * HD), jnp.bfloat16) for g in sends]
    out_specs = [
        q_spec,
        q_spec,
        pl.BlockSpec((1, n_query, HD), resp_map(own[1])),
        pl.BlockSpec((1, n_query, HD), lambda r, j, sc: (r, 0, 0)),
    ]
    out_specs += [pl.BlockSpec(g.shape, lambda r, j, sc: (0, 0, 0, 0)) for g in grads]
    out_shape = [
        shape(queries.shape, jnp.bfloat16),
        shape(queries.shape, jnp.bfloat16),
        shape(own[0].shape, jnp.bfloat16),
        shape((n_resp, n_query, HD), jnp.bfloat16),
    ] + grads
    scratch = [
        pltpu.VMEM((n_keys, HD), jnp.bfloat16),
        pltpu.VMEM((n_keys, HD), jnp.bfloat16),
        pltpu.VMEM((n_rows, HD), jnp.bfloat16),
        pltpu.VMEM((n_rows, HD), jnp.bfloat16),
        pltpu.VMEM((HD, n_rows), jnp.bfloat16),
        pltpu.VMEM((HD, n_rows), jnp.bfloat16),
        pltpu.VMEM((n_rows, n_keys), jnp.float32),
        pltpu.VMEM((n_rows, n_keys), jnp.float32),
        pltpu.VMEM((n_rows, n_keys), jnp.bfloat16),
        pltpu.VMEM((n_rows, n_keys), jnp.bfloat16),
        pltpu.VMEM((HD, n_keys), jnp.float32),
        pltpu.VMEM((HD, n_keys), jnp.float32),
        pltpu.VMEM((P_SIZE, n_prompt, HD), jnp.float32),
        pltpu.VMEM((P_SIZE, n_prompt, HD), jnp.float32),
    ]
    flops = 12 * n_resp * heads * n_query * n_keys * HD
    return pl.pallas_call(
        functools.partial(attend_kernel, (pieces, rows, keep, sends, n_pass)),
        grid_spec=pltpu.PrefetchScalarGridSpec(
            num_scalar_prefetch=1,
            grid=(n_resp, steps),
            in_specs=in_specs,
            out_specs=out_specs,
            scratch_shapes=scratch,
        ),
        out_shape=out_shape,
        input_output_aliases=aliases,
        compiler_params=pltpu.CompilerParams(vmem_limit_bytes=48 * 2**20),
        cost_estimate=pl.CostEstimate(flops=2 * flops, bytes_accessed=4 * 2**20, transcendentals=0),
    )(scalars, *args)


def pack_kernel(n_own, prompt_ref, resp_ref, *outs):
    width = n_own * HD

    def split(own):
        for h in range(n_own):
            mine = slice(own + h * HD, own + (h + 1) * HD)
            theirs = slice(width - own + h * HD, width - own + (h + 1) * HD)
            for k, (ref, lanes) in enumerate(
                ((prompt_ref, mine), (prompt_ref, theirs), (resp_ref, mine), (resp_ref, theirs))
            ):
                outs[4 * h + k][...] = ref[:, :, lanes]

    parity = lax.axis_index("prefix") % 2

    @pl.when(parity == 0)
    def _():
        split(0)

    @pl.when(parity != 0)
    def _():
        split(width)


def pack(prompt_kv, resp_kv, n_own):
    block = lambda shape: pl.BlockSpec(shape, lambda i: (0, 0, 0))
    shapes = [x.shape[:2] + (HD,) for x in (prompt_kv, prompt_kv, resp_kv, resp_kv)] * n_own
    return pl.pallas_call(
        functools.partial(pack_kernel, n_own),
        grid=(1,),
        in_specs=[block(prompt_kv.shape), block(resp_kv.shape)],
        out_specs=[block(s) for s in shapes],
        out_shape=[jax.ShapeDtypeStruct(s, prompt_kv.dtype) for s in shapes],
        compiler_params=pltpu.CompilerParams(vmem_limit_bytes=48 * 2**20),
    )(prompt_kv, resp_kv)


def per_device(queries, resp_kv, prompt_kv, prompt_of, d_out):
    pair_heads = prompt_kv.shape[2] // HD
    parity = lax.axis_index("prefix") % 2
    scalars = jnp.concatenate([prompt_of, parity[None].astype(jnp.int32)])
    if lax.axis_size("dp") == 4 and pair_heads % 2 == 0:
        return whole_heads(queries, resp_kv, prompt_kv, scalars, parity, d_out)
    return shared_head(queries, resp_kv, prompt_kv, scalars, parity, d_out)


def whole_heads(queries, resp_kv, prompt_kv, scalars, parity, d_out):
    n_own = prompt_kv.shape[2] // HD // 2
    z = functools.partial(swap, axis="prefix", step=1)
    core, x, both = [functools.partial(swap, axis="dp", step=k) for k in (1, 2, 3)]
    theirs = (1 - parity) * n_own

    def order(values, done):
        return lax.optimization_barrier((tuple(values), tuple(done)))[0]

    packed = pack(prompt_kv, resp_kv, n_own)
    others = [z(packed[4 * h + 1]) for h in range(n_own)]
    pa, pb, resp_a, resp_b = [], [], [], []
    for h in range(n_own):
        a0, _, ra, rb = packed[4 * h : 4 * h + 4]
        if h > 0:
            (rb,) = order([rb], [resp_b[h - 1]])
        b0 = others[h]
        a2 = x(a0)
        if h == 0:
            (rb,) = order([rb], [others[-1]])
        resp_a.append(ra)
        resp_b.append(z(rb))
        if h == 0:
            (ready,) = order([b0], [a2])
        else:
            (ready,) = order([b0], [pb[0][2]])
        b2 = x(ready)
        pa.append([a0, core(a0), a2, core(a2) if h == 0 else None])
        pb.append([b0, core(b0), b2, core(b2) if h == 0 else None])

    shared = None
    d_resp, d_prompt = [], []
    for h in range(n_own):
        final = h == n_own - 1
        here = lambda par, h=h: par * n_own + h
        at = lambda par: 0
        att, dq, dra, drb, keep, *sends = attend(
            scalars,
            queries,
            d_out,
            (resp_a[h], at),
            (resp_b[h], at),
            [(a, at) for a in pa[h]],
            [(b, at) for b in pb[h]],
            (0, 2) if final else (0,),
            ((1, 3),) if final else ((1,), (2,), (3,)),
            h,
            GROUP,
            shared,
            (resp_kv, here),
        )
        shared = (att, dq, dra)
        d_resp.append(z(drb))
        if not final:
            pa[h + 1][3], pb[h + 1][3] = [core(v) for v in order([pa[h + 1][2], pb[h + 1][2]], [drb])]
        if final:
            (send,) = order([sends[0]], arrived)
            sums = keep + core(send).astype(jnp.float32)
            (across,) = order([x(sums[1].astype(jnp.bfloat16))], [d_resp[-1]])
            total = sums[0] + across.astype(jnp.float32)
        else:
            parts = [move(part[0]) for move, part in zip((core, x, both), sends)]
            arrived = [*parts, d_resp[-1]]
            total = keep[0] + sum(p.astype(jnp.float32) for p in parts)
        other = z(total[:, :, HD:].astype(jnp.bfloat16))
        d_prompt.append((total[:, :, :HD], other))

    even = parity == 0
    mine = jnp.concatenate([a for a, _ in d_prompt], axis=-1)
    other = jnp.concatenate([b.astype(jnp.float32) for _, b in d_prompt], axis=-1)
    d_prompt = jnp.concatenate([jnp.where(even, mine, other), jnp.where(even, other, mine)], axis=-1)
    att, dq, d_resp_kv = shared
    received = jnp.concatenate(d_resp, axis=-1)
    d_resp_kv = lax.dynamic_update_slice_in_dim(d_resp_kv, received, theirs * HD, axis=2)
    return att, dq, d_resp_kv, d_prompt


def shared_head(queries, resp_kv, prompt_kv, scalars, parity, d_out):
    first = lambda par: 0
    prompt_a = lax.all_gather(prompt_kv, "dp", axis=1, tiled=True)
    prompt_b = swap(prompt_a, "prefix", 1)
    resp_b = swap(resp_kv, "prefix", 1)
    att, dq, dra, drb, keep = attend(
        scalars,
        queries,
        d_out,
        (resp_kv, first),
        (resp_b, first),
        [(prompt_a, first)],
        [(prompt_b, first)],
        (0,),
        (),
        0,
        queries.shape[2] // HD,
        None,
        (resp_kv, first),
    )
    d_resp = (dra.astype(jnp.float32) + swap(drb, "prefix", 1).astype(jnp.float32)).astype(jnp.bfloat16)
    other = swap(keep[0, :, :, HD:].astype(jnp.bfloat16), "prefix", 1)
    paired = keep[0, :, :, :HD] + other.astype(jnp.float32)
    d_prompt = lax.psum_scatter(paired, "dp", scatter_dimension=1, tiled=True)
    return att, dq, d_resp, d_prompt


def solution(mesh):
    in_specs = (
        P(("groups", "dp"), None, "prefix"),
        P(("groups", "dp"), None, "prefix"),
        P("groups", "dp", "prefix"),
        P(("groups", "dp")),
        P(("groups", "dp"), None, "prefix"),
    )
    out_specs = (
        P(("groups", "dp"), None, "prefix"),
        P(("groups", "dp"), None, "prefix"),
        P(("groups", "dp"), None, "prefix"),
        P("groups", "dp", "prefix"),
    )
    return jax.shard_map(
        per_device, mesh=mesh, in_specs=in_specs, out_specs=out_specs, check_vma=False
    )
```
